32 devices in a mesh: dp: 8 (over z, x), seq: 4 (over y, core).
Axes of the slice: x: 2, y: 2, z: 4, core: 2. Of those that a mesh axis runs over, the one named last changes fastest.
Arguments:
- block_input: bfloat16 [8, 592, 1024], P('dp', 'seq')
- key_mask: int32 [8, 592], P('dp', 'seq'), may hold values from 0 to 1, as said below
- valid: int32 [8], P('dp'), may hold values 0 or 1
- gains: bfloat16 [2, 2, 1024], P(None, None, 'dp'), may hold values from 0.5 to 1.5
- biases: bfloat16 [2, 6, 1024], P(None, None, 'dp'), may hold values from -1.1953125 to 1.1953125
- w_qkv: bfloat16 [2, 1024, 3072], P(None, 'dp'), may hold values from -0.1875 to 0.1875
- w_out: bfloat16 [2, 1024, 1024], P(None, 'dp'), may hold values from -1.5 to 1.5
- w_fc1: bfloat16 [2, 1024, 4096], P(None, 'dp'), may hold values from -0.1875 to 0.1875
- b_fc1: bfloat16 [2, 4096], P(None, 'dp'), may hold values from -1.1953125 to 1.1953125
- w_fc2: bfloat16 [2, 4096, 1024], P(None, 'dp'), may hold values from -0.09375 to 0.09375
- cotangent: bfloat16 [8, 592, 1024], P('dp', 'seq'), may hold values from -6 to 6
Outputs:
- block_output: bfloat16 [8, 592, 1024], P('dp', 'seq')
- grad_x: float32 [8, 592, 1024], P('dp', 'seq')
- rms: float32 [2, 3], replicated
- grad_gains: float32 [2, 2, 1024], P(None, None, 'dp')
- grad_biases: float32 [2, 5, 1024], P(None, None, 'dp')
- grad_query_bias: float32 [2, 1024], P(None, 'dp')
- grad_qkv: float32 [2, 1024, 3072], P(None, 'dp')
- grad_out: float32 [2, 1024, 1024], P(None, 'dp')
- grad_fc1: float32 [2, 1024, 4096], P(None, 'dp')
- grad_bfc1: float32 [2, 4096], P(None, 'dp')
- grad_fc2: float32 [2, 4096, 1024], P(None, 'dp')
The draws below stay inside these ranges and needn't reach their ends.
Inputs may be any that keep to these rules, and one draw needn't show every extreme that they name: `key_mask`: position 0 of every image is 1 and positions 577 to 591 are 0.
All inputs are finite; a program needn't handle non-finite values. No bound on the sum of `valid` on one device may be relied on, other than what follows from the above.
Results may differ from the reference program's by a relative error of at most 0.015.
Values may be sent and summed in bfloat16 or wider, within the bound.
A program may use at most 320 MiB of HBM per device.

```python
import math
import jax
import jax.numpy as jnp
from jax import lax

D = 1024
HEADS = 16
HEAD_DIM = 64
FF = 4096
LAYERS = 2
LEN = 592
REAL_LEN = 577
IMAGES = 8


def draw_block_input(key, part):
    image_pos = jnp.arange(IMAGES, dtype=jnp.float32)[:, None, None]
    factor = 0.5 + 1.5 * image_pos / max(IMAGES - 1, 1)
    base = jnp.clip(jax.random.normal(key, (IMAGES, LEN, D), jnp.float32), -6.0, 6.0)
    return (base * factor).astype(jnp.bfloat16)


def draw_key_mask(key, part):
    position = jnp.arange(LEN, dtype=jnp.int32)[None, :]
    drawn = jax.random.randint(key, (IMAGES, LEN), 0, 8)
    inside = jnp.where(drawn < 7, 1, 0)
    return jnp.where(position == 0, 1, jnp.where(position < REAL_LEN, inside, 0)).astype(jnp.int32)


def set_ends(array, own_key, least, top_value):
    longest = array.shape.index(max(array.shape))
    spots = []
    for shift in (0, 1):
        where = [jax.random.randint(jax.random.fold_in(own_key, axis), (), 0, length) for axis, length in enumerate(array.shape)]
        where[longest] = (where[longest] + shift) % array.shape[longest]
        spots.append(tuple(where))
    return array.at[spots[0]].set(least).at[spots[1]].set(top_value)


def levels(rng, dims, split, least, top_value):
    loudness = 1.0
    for dim, parts in split:
        draws = jax.random.uniform(jax.random.fold_in(jax.random.fold_in(rng, 6), dim), (parts,), jnp.float32, least / len(split), top_value / len(split))
        loudness = loudness * jnp.repeat(jnp.exp(draws), dims[dim] // parts).reshape((-1,) + (1,) * (len(dims) - 1 - dim))
    return loudness


def scatter_about(rng, shape, scale, most, cuts=(), kind=jnp.bfloat16):
    values = jax.random.normal(rng, shape, jnp.float32) * scale
    if len(cuts) > 0:
        values = levels(rng, shape, cuts, -0.22, 0.18) * values
    return jnp.clip(values, min=-most, max=most).astype(kind)


def setup_inputs(seed: int = 0) -> dict:
    key_list = jax.random.split(jax.random.key(seed), 12)
    return {
        "block_input": draw_block_input(jax.random.fold_in(key_list[11], 71), 0),
        "key_mask": draw_key_mask(jax.random.fold_in(key_list[11], 71), 0),
        "valid": set_ends((jax.random.randint(key_list[2], (IMAGES,), 0, 8) < 7).astype(jnp.int32), jax.random.fold_in(key_list[2], 1), 0, 1),
        "gains": jnp.clip(1.0 + 0.1 * jax.random.normal(key_list[3], (LAYERS, 2, D), jnp.float32), 0.5, 1.5).astype(jnp.bfloat16),
        "biases": scatter_about(key_list[4], (LAYERS, 6, D), 0.2, 1.1953125, ((2, 8),)),
        "w_qkv": scatter_about(key_list[5], (LAYERS, D, 3 * D), D ** -0.5, 0.1875, ((1, 8),)),
        "w_out": scatter_about(key_list[6], (LAYERS, D, D), (D // 64) ** -0.5, 1.5, ((1, 8),)),
        "w_fc1": scatter_about(key_list[7], (LAYERS, D, FF), D ** -0.5, 0.1875, ((1, 8),)),
        "b_fc1": scatter_about(key_list[8], (LAYERS, FF), 0.2, 1.1953125, ((1, 8),)),
        "w_fc2": scatter_about(key_list[9], (LAYERS, FF, D), FF ** -0.5, 0.09375, ((1, 8),)),
        "cotangent": scatter_about(key_list[10], (IMAGES, LEN, D), 1.0, 6.0, ((0, 8), (1, 4))),
    }


@jax.custom_vjp
def low(v):
    return lax.optimization_barrier(v.astype(jnp.bfloat16)).astype(jnp.float32)

@jax.custom_vjp
def low_back(v):
    return v

def low_keep(v):
    return (low(v), None)

def low_pass(kept, grad):
    return (grad,)

def back_keep(v):
    return (v, None)

def back_low(kept, grad):
    return (low(grad),)
low.defvjp(low_keep, low_pass)
low_back.defvjp(back_keep, back_low)
highest = lax.Precision.HIGHEST

def project(rows, matrix):
    lead = rows.shape[:-1]
    flat = jnp.dot(rows.reshape(-1, rows.shape[-1]), matrix, precision=highest)
    return flat.reshape(lead + (matrix.shape[1],))

def layer_norm(values_in, gain, shift):
    center = values_in - lax.optimization_barrier(jnp.mean(values_in, -1, keepdims=True))
    spread = lax.optimization_barrier(jnp.mean(center * center, -1, keepdims=True))
    return center * lax.rsqrt(spread + 1e-05) * gain + shift

def one_layer(hidden, key_rows, tok_valid, weights):
    gains, biases, w_qkv, w_out, w_fc1, b_fc1, w_fc2 = weights
    blocks = hidden.shape[0]
    length = hidden.shape[1]
    width = hidden.shape[2]
    normed = low(layer_norm(hidden, gains[0], biases[0]))
    packed = project(normed, w_qkv)
    query = low_back(low(packed[..., :width] + biases[1]))
    keys = low_back(low(packed[..., width:2 * width]))
    values = low_back(low(packed[..., 2 * width:] + biases[2]))
    shape_four = (blocks, length, HEADS, HEAD_DIM)
    scores = jnp.einsum('bqhd,bkhd->bhqk', query.reshape(shape_four), keys.reshape(shape_four), precision=highest) * (1.0 / math.sqrt(HEAD_DIM))
    scores = low_back(jnp.where(key_rows[:, None, None, :] > 0, scores, -1000000000.0))
    probs = low(jax.nn.softmax(scores, axis=-1))
    mixed = jnp.einsum('bhqk,bkhd->bqhd', probs, values.reshape(shape_four), precision=highest).reshape(blocks, length, width)
    mixed = low_back(low(mixed))
    branch = low_back(project(mixed, w_out) + biases[3])
    middle = hidden + branch
    normed_two = low(layer_norm(middle, gains[1], biases[4]))
    inner = low_back(project(normed_two, w_fc1) + b_fc1)
    gated = low(inner * jax.nn.sigmoid(1.702 * inner))
    output = low_back(project(gated, w_fc2) + biases[5])
    result = middle + output
    stats = jnp.stack([jnp.sum(tok_valid * lax.optimization_barrier(jnp.sum(hidden * hidden, -1))), jnp.sum(tok_valid * lax.optimization_barrier(jnp.sum(branch * branch, -1))), jnp.sum(tok_valid * lax.optimization_barrier(jnp.sum(output * output, -1)))])
    return (result, stats)

def stack_forward(hidden, params, key_rows, tok_valid):
    stat_rows = []
    for layer in range(LAYERS):
        hidden, stats = one_layer(hidden, key_rows, tok_valid, tuple((p[layer] for p in params)))
        stat_rows.append(stats)
    return (hidden, jnp.stack(stat_rows))

def reference(block_input, key_mask, valid, gains, biases, w_qkv, w_out, w_fc1, b_fc1, w_fc2, cotangent):
    params = tuple((a.astype(jnp.float32) for a in (gains, biases, w_qkv, w_out, w_fc1, b_fc1, w_fc2)))
    tok_valid = (key_mask * valid[:, None]).astype(jnp.float32)
    block = 4 if IMAGES % 4 == 0 else 1
    nblocks = IMAGES // block
    inputs = (block_input.astype(jnp.float32).reshape(nblocks, block, LEN, D), key_mask.reshape(nblocks, block, LEN), tok_valid.reshape(nblocks, block, LEN), cotangent.astype(jnp.float32).reshape(nblocks, block, LEN, D))

    def step(carry, item):
        grads, sums = carry
        x_block, mask_block, valid_block, cot_block = item
        result, pull, stats = jax.vjp(lambda hh, pp: stack_forward(hh, pp, mask_block, valid_block), x_block, params, has_aux=True)
        grad_block, grad_params = pull(cot_block * valid_block[..., None])
        grads = jax.tree.map(jnp.add, grads, grad_params)
        return ((grads, sums + stats), (result.astype(jnp.bfloat16), grad_block))
    init = (tuple((jnp.zeros_like(p) for p in params)), jnp.zeros((LAYERS, 3), jnp.float32))
    (grads, sums), (outputs, grad_inputs) = lax.scan(step, init, inputs)
    token_count = jnp.sum(tok_valid)
    rms = jnp.sqrt(sums / (jnp.maximum(token_count, 1.0) * D))
    bias_all = grads[1]
    bias_rest = jnp.concatenate([bias_all[:, :1], bias_all[:, 2:]], 1)
    bias_query = bias_all[:, 1]
    return (outputs.reshape(IMAGES, LEN, D), grad_inputs.reshape(IMAGES, LEN, D), rms, grads[0], bias_rest, bias_query, grads[2], grads[3], grads[4], grads[5], grads[6])
```

```python
from functools import partial
import math

import jax
import jax.numpy as jnp
from jax import lax
from jax.sharding import PartitionSpec as P

HEADS = 16
HEAD_DIM = 64
F32 = jnp.float32
BF16 = jnp.bfloat16

epsilon = 1e-05


def norm_parts(values_in, gain, shift):
    center = values_in - jnp.mean(values_in, -1, keepdims=True)
    inverse = lax.rsqrt(jnp.mean(center * center, -1, keepdims=True) + epsilon)
    normal = center * inverse
    return (normal * gain + shift, normal, inverse)


def norm_back(grad_output, normal, inverse, gain):
    grad_gain = jnp.sum(grad_output * normal, 0)
    grad_shift = jnp.sum(grad_output, 0)
    grad_norm = grad_output * gain
    plain_mean = jnp.mean(grad_norm, -1, keepdims=True)
    cross_mean = jnp.mean(grad_norm * normal, -1, keepdims=True)
    return (grad_gain, grad_shift, inverse * (grad_norm - plain_mean - normal * cross_mean))


def dot(a, b, ca=1, cb=0):
    return lax.dot_general(a, b, (((ca,), (cb,)), ((), ())), preferred_element_type=F32)


def split_heads(x, width):
    return x.reshape(x.shape[0], width // HEAD_DIM, HEAD_DIM)


def scores_of(query, keys, mask_row, scale):
    scores = jnp.einsum("qhd,khd->hqk", query, keys, preferred_element_type=F32) * scale
    return jnp.where(mask_row[None, None, :] > 0, scores, -1000000000.0)


def gather_rows(x):
    return lax.all_gather(x, "seq", axis=0, tiled=True)


def scatter_rows(x):
    return lax.psum_scatter(x.astype(BF16), "seq", scatter_dimension=0, tiled=True).astype(F32)


def forward_layer(hidden, weights, params, mask_row, tok_valid):
    w_qkv, w_out, w_fc1, w_fc2 = weights
    gains, biases, bias_q, bias_v, b_fc1 = params
    scale = 1.0 / math.sqrt(HEAD_DIM)
    width = w_out.shape[0]
    normed, normal_one, inverse_one = norm_parts(hidden, gains[0], biases[0])
    normed_all = gather_rows(normed.astype(BF16))
    packed = dot(normed_all, w_qkv)
    packed = (packed + jnp.concatenate([bias_q, jnp.zeros_like(bias_q), bias_v])).astype(BF16)
    query, keys, values = (split_heads(packed[:, i * width : (i + 1) * width], width) for i in range(3))
    scores = scores_of(query, keys, mask_row, scale)
    row_max = jnp.max(scores, -1, keepdims=True)
    log_total = row_max + jnp.log(jnp.sum(jnp.exp(scores - row_max), -1, keepdims=True))
    probs = jnp.exp(scores - log_total).astype(BF16)
    mixed = jnp.einsum("hqk,khd->qhd", probs, values, preferred_element_type=F32).astype(BF16)
    mixed = mixed.reshape(mixed.shape[0], width)
    branch = scatter_rows(dot(mixed, w_out)) + biases[3]
    middle = hidden + branch
    normed_two, normal_two, inverse_two = norm_parts(middle, gains[1], biases[4])
    normed_two_all = gather_rows(normed_two.astype(BF16))
    inner = dot(normed_two_all, w_fc1) + b_fc1
    gate_sig = jax.nn.sigmoid(1.702 * inner)
    gated = (inner * gate_sig).astype(BF16)
    output = scatter_rows(dot(gated, w_fc2)) + biases[5]
    stat = jnp.stack([jnp.sum(tok_valid * jnp.sum(v * v, -1)) for v in (hidden, branch, output)])
    stored = (normal_one, inverse_one, normed_all, query, keys, values, log_total, mixed,
              normal_two, inverse_two, normed_two_all, inner, gate_sig, gated)
    return (middle + output, stored, stat)


def backward_layer(grad_result, weights, params, stored, mask_row):
    w_qkv, w_out, w_fc1, w_fc2 = weights
    gains = params[0]
    scale = 1.0 / math.sqrt(HEAD_DIM)
    (normal_one, inverse_one, normed_all, query, keys, values, log_total, mixed,
     normal_two, inverse_two, normed_two_all, inner, gate_sig, gated) = stored
    out_low = grad_result.astype(BF16)
    grad_bias_five = jnp.sum(out_low.astype(F32), 0)
    out_all = gather_rows(out_low)
    grad_fc2 = dot(gated, out_all, 0, 0)
    grad_gated = dot(out_all, w_fc2, 1, 1)
    grad_inner = (grad_gated * (gate_sig + 1.702 * inner * gate_sig * (1.0 - gate_sig))).astype(BF16)
    grad_bias_fc1 = jnp.sum(grad_inner.astype(F32), 0)
    grad_fc1 = dot(normed_two_all, grad_inner, 0, 0)
    grad_normed_two = scatter_rows(dot(grad_inner, w_fc1, 1, 1))
    grad_gain_two, grad_shift_two, grad_middle = norm_back(grad_normed_two, normal_two, inverse_two, gains[1])
    grad_middle = grad_middle + grad_result
    branch_low = grad_middle.astype(BF16)
    grad_bias_three = jnp.sum(branch_low.astype(F32), 0)
    branch_all = gather_rows(branch_low)
    grad_out = dot(mixed, branch_all, 0, 0)
    width = w_out.shape[0]
    grad_mixed = split_heads(dot(branch_all, w_out, 1, 1).astype(BF16), width)
    scores = scores_of(query, keys, mask_row, scale)
    probs = jnp.exp(scores - log_total)
    grad_probs = jnp.einsum("qhd,khd->hqk", grad_mixed, values, preferred_element_type=F32)
    inner_sum = jnp.sum(probs * grad_probs, -1, keepdims=True)
    grad_scores = (probs * (grad_probs - inner_sum)).astype(BF16)
    grad_q = (jnp.einsum("hqk,khd->qhd", grad_scores, keys, preferred_element_type=F32) * scale).astype(BF16)
    grad_k = (jnp.einsum("hqk,qhd->khd", grad_scores, query, preferred_element_type=F32) * scale).astype(BF16)
    grad_v = jnp.einsum("hqk,qhd->khd", probs.astype(BF16), grad_mixed, preferred_element_type=F32).astype(BF16)
    rows = grad_q.shape[0]
    grad_proj = jnp.concatenate([g.reshape(rows, width) for g in (grad_q, grad_k, grad_v)], 1)
    grad_bias_proj = jnp.sum(grad_proj.astype(F32), 0)
    grad_qkv = dot(normed_all, grad_proj, 0, 0)
    grad_normed = scatter_rows(dot(grad_proj, w_qkv, 1, 1))
    grad_gain_one, grad_shift_one, grad_hidden = norm_back(grad_normed, normal_one, inverse_one, gains[0])
    grad_hidden = grad_hidden + grad_middle
    rows_sum = jnp.stack([grad_gain_one, grad_gain_two, grad_shift_one, grad_bias_three, grad_shift_two, grad_bias_five])
    return (grad_hidden, (grad_qkv, grad_out, grad_fc1, grad_fc2), rows_sum, grad_bias_proj, grad_bias_fc1)


def local(block_input, key_mask, valid, gains, biases, w_qkv, w_out, w_fc1, b_fc1, w_fc2, cotangent):
    layers = w_qkv.shape[0]
    groups = lax.axis_size("seq")
    shards = lax.axis_size("dp")
    me = lax.axis_index("seq")
    width = block_input.shape[2]
    hidden_width = w_fc2.shape[1] * shards
    part = width // groups
    images = block_input.shape[0]
    assert images == 1
    mask_row = lax.all_gather(key_mask, "seq", axis=1, tiled=True)[0]
    tok_valid = (key_mask * valid[:, None]).astype(F32)[0]
    hidden = block_input[0].astype(F32)
    small = jnp.concatenate([gains.reshape(layers, -1), biases.reshape(layers, -1), b_fc1], 1)
    small = lax.all_gather(small, "dp", axis=0).astype(F32)
    n_g, n_b = gains.shape[1] * gains.shape[2], biases.shape[1] * biases.shape[2]
    gains_all = small[:, :, :n_g].reshape(shards, layers, 2, -1).transpose(1, 2, 0, 3).reshape(layers, 2, width)
    biases_all = small[:, :, n_g : n_g + n_b].reshape(shards, layers, 6, -1).transpose(1, 2, 0, 3).reshape(layers, 6, width)
    fc_all = small[:, :, n_g + n_b :].transpose(1, 0, 2).reshape(layers, shards, groups, -1)
    fc_mine = lax.dynamic_index_in_dim(fc_all, me, 2, False).reshape(layers, -1)
    proj_mine = lax.dynamic_index_in_dim(biases_all.reshape(layers, 6, groups, part), me, 2, False)

    def columns(w, outer):
        view = w.reshape(w.shape[0], outer, groups, -1)
        return lax.dynamic_index_in_dim(view, me, 2, False).reshape(w.shape[0], -1)

    def rows_of(w):
        view = w.reshape(groups, -1, w.shape[1])
        return lax.dynamic_index_in_dim(view, me, 0, False)

    def gather(w):
        return lax.all_gather(w, "dp", axis=0, tiled=True)

    weights, params, stored_all, stats = [], [], [], []
    for layer in range(layers):
        weights.append((
            gather(columns(w_qkv[layer], 3)),
            rows_of(gather(w_out[layer])),
            gather(columns(w_fc1[layer], shards)),
            gather(rows_of(w_fc2[layer])),
        ))
        params.append((gains_all[layer], biases_all[layer], proj_mine[layer, 1], proj_mine[layer, 2], fc_mine[layer]))
    for layer in range(layers):
        hidden, stored, stat = forward_layer(hidden, weights[layer], params[layer], mask_row, tok_valid)
        stored_all.append(stored)
        stats.append(stat)
    totals = lax.psum(jnp.concatenate([jnp.stack(stats).reshape(-1), jnp.sum(tok_valid)[None]]), ("dp", "seq"))
    rms = jnp.sqrt(totals[:-1].reshape(layers, 3) / (jnp.maximum(totals[-1], 1.0) * width))

    grad_hidden = cotangent[0].astype(F32) * tok_valid[:, None]
    big = [None] * layers
    sums = [None] * layers
    for layer in reversed(range(layers)):
        grad_hidden, grads, rows_sum, grad_proj, grad_fc = backward_layer(
            grad_hidden, weights[layer], params[layer], stored_all[layer], mask_row
        )
        g_qkv, g_out, g_fc1, g_fc2 = (g.astype(BF16) for g in grads)
        g_out = lax.all_to_all(g_out, "seq", split_axis=1, concat_axis=0, tiled=True)

        def reduce_(g):
            g = lax.psum_scatter(g, "dp", scatter_dimension=0, tiled=True)
            return lax.all_gather(g, "seq", axis=0)

        def join(g, outer):
            view = g.reshape(groups, g.shape[1], outer, -1)
            return view.transpose(1, 2, 0, 3).reshape(g.shape[1], -1)

        big[layer] = (
            join(reduce_(g_qkv), 3).astype(F32),
            join(reduce_(g_out), 1).astype(F32),
            join(reduce_(g_fc1), shards).astype(F32),
            reduce_(g_fc2).reshape(w_fc2.shape[1], -1).astype(F32),
        )
        proj = lax.dynamic_update_slice(jnp.zeros((3, groups, part), F32), grad_proj.reshape(3, 1, part), (0, me, 0))
        fc = lax.dynamic_update_slice(jnp.zeros((shards, groups, hidden_width // (shards * groups)), F32),
                                      grad_fc.reshape(shards, 1, -1), (0, me, 0))
        sums[layer] = jnp.concatenate([
            rows_sum.reshape(6, shards, -1).transpose(1, 0, 2).reshape(shards, -1),
            proj.reshape(3, shards, -1).transpose(1, 0, 2).reshape(shards, -1),
            fc.reshape(shards, -1),
        ], 1)
    flat = jnp.stack(sums, 1).astype(F32)
    flat = lax.psum(lax.psum_scatter(flat, "dp", scatter_dimension=0, tiled=True)[0], "seq")
    per = width // shards
    rows9 = flat[:, : 9 * per].reshape(layers, 9, per)
    grad_bfc1 = flat[:, 9 * per :]
    stack = lambda i: jnp.stack([b[i] for b in big])
    bias_rest = jnp.concatenate([rows9[:, 2:3], rows9[:, 8:9], rows9[:, 3:6]], 1)
    return (
        hidden.astype(BF16)[None],
        grad_hidden[None],
        rms,
        rows9[:, :2],
        bias_rest,
        rows9[:, 6],
        stack(0),
        stack(1),
        stack(2),
        grad_bfc1,
        stack(3),
    )


def solution(mesh):
    return jax.shard_map(
        local,
        mesh=mesh,
        in_specs=(
            P("dp", "seq", None),
            P("dp", "seq"),
            P("dp"),
            P(None, None, "dp"),
            P(None, None, "dp"),
            P(None, "dp", None),
            P(None, "dp", None),
            P(None, "dp", None),
            P(None, "dp"),
            P(None, "dp", None),
            P("dp", "seq", None),
        ),
        out_specs=(
            P("dp", "seq", None),
            P("dp", "seq", None),
            P(),
            P(None, None, "dp"),
            P(None, None, "dp"),
            P(None, "dp"),
            P(None, "dp", None),
            P(None, "dp", None),
            P(None, "dp", None),
            P(None, "dp"),
            P(None, "dp", None),
        ),
        check_vma=False,
    )
```

```python
from functools import partial
import math

import jax
import jax.numpy as jnp
from jax import lax
from jax.experimental import pallas as pl
from jax.experimental.pallas import tpu as pltpu
from jax.sharding import PartitionSpec as P

HEADS = 16
HEAD_DIM = 64
F32 = jnp.float32
BF16 = jnp.bfloat16

epsilon = 1e-05


def norm_parts(values_in, gain, shift):
    center = values_in - jnp.mean(values_in, -1, keepdims=True)
    inverse = lax.rsqrt(jnp.mean(center * center, -1, keepdims=True) + epsilon)
    normal = center * inverse
    return (normal * gain + shift, normal, inverse)


def norm_back(grad_output, normal, inverse, gain):
    grad_gain = jnp.sum(grad_output * normal, 0)
    grad_shift = jnp.sum(grad_output, 0)
    grad_norm = grad_output * gain
    plain_mean = jnp.mean(grad_norm, -1, keepdims=True)
    cross_mean = jnp.mean(grad_norm * normal, -1, keepdims=True)
    return (grad_gain, grad_shift, inverse * (grad_norm - plain_mean - normal * cross_mean))


def dot(a, b, ca=1, cb=0):
    return lax.dot_general(a, b, (((ca,), (cb,)), ((), ())), preferred_element_type=F32)


def split_heads(x, width):
    return x.reshape(x.shape[0], width // HEAD_DIM, HEAD_DIM)


def scores_of(query, keys, mask_row, scale):
    scores = jnp.einsum("qhd,khd->hqk", query, keys, preferred_element_type=F32) * scale
    return jnp.where(mask_row[None, None, :] > 0, scores, -1000000000.0)


def gather_rows(x):
    return lax.all_gather(x, "seq", axis=0, tiled=True)


def scatter_rows(x):
    return lax.psum_scatter(x.astype(BF16), "seq", scatter_dimension=0, tiled=True).astype(F32)


def forward_layer(hidden, weights, params, mask_row, tok_valid):
    w_qkv, w_out, w_fc1, w_fc2 = weights
    gains, biases, bias_q, bias_v, b_fc1 = params
    scale = 1.0 / math.sqrt(HEAD_DIM)
    width = w_out.shape[0]
    normed, normal_one, inverse_one = norm_parts(hidden, gains[0], biases[0])
    normed_all = gather_rows(normed.astype(BF16))
    packed = dot(normed_all, w_qkv)
    packed = (packed + jnp.concatenate([bias_q, jnp.zeros_like(bias_q), bias_v])).astype(BF16)
    query, keys, values = (split_heads(packed[:, i * width : (i + 1) * width], width) for i in range(3))
    scores = scores_of(query, keys, mask_row, scale)
    row_max = jnp.max(scores, -1, keepdims=True)
    log_total = row_max + jnp.log(jnp.sum(jnp.exp(scores - row_max), -1, keepdims=True))
    probs = jnp.exp(scores - log_total).astype(BF16)
    mixed = jnp.einsum("hqk,khd->qhd", probs, values, preferred_element_type=F32).astype(BF16)
    mixed = mixed.reshape(mixed.shape[0], width)
    branch = scatter_rows(dot(mixed, w_out)) + biases[3]
    middle = hidden + branch
    normed_two, normal_two, inverse_two = norm_parts(middle, gains[1], biases[4])
    normed_two_all = gather_rows(normed_two.astype(BF16))
    inner = dot(normed_two_all, w_fc1) + b_fc1
    gate_sig = jax.nn.sigmoid(1.702 * inner)
    gated = (inner * gate_sig).astype(BF16)
    output = scatter_rows(dot(gated, w_fc2)) + biases[5]
    stat = jnp.stack([jnp.sum(tok_valid * jnp.sum(v * v, -1)) for v in (hidden, branch, output)])
    stored = (normal_one, inverse_one, normed_all, query, keys, values, log_total, mixed,
              normal_two, inverse_two, normed_two_all, inner, gate_sig, gated)
    return (middle + output, stored, stat)


def backward_layer(grad_result, weights, params, stored, mask_row):
    w_qkv, w_out, w_fc1, w_fc2 = weights
    gains = params[0]
    scale = 1.0 / math.sqrt(HEAD_DIM)
    (normal_one, inverse_one, normed_all, query, keys, values, log_total, mixed,
     normal_two, inverse_two, normed_two_all, inner, gate_sig, gated) = stored
    out_low = grad_result.astype(BF16)
    grad_bias_five = jnp.sum(out_low.astype(F32), 0)
    out_all = gather_rows(out_low)
    grad_fc2 = dot(gated, out_all, 0, 0)
    grad_gated = dot(out_all, w_fc2, 1, 1)
    grad_inner = (grad_gated * (gate_sig + 1.702 * inner * gate_sig * (1.0 - gate_sig))).astype(BF16)
    grad_bias_fc1 = jnp.sum(grad_inner.astype(F32), 0)
    grad_fc1 = dot(normed_two_all, grad_inner, 0, 0)
    grad_normed_two = scatter_rows(dot(grad_inner, w_fc1, 1, 1))
    grad_gain_two, grad_shift_two, grad_middle = norm_back(grad_normed_two, normal_two, inverse_two, gains[1])
    grad_middle = grad_middle + grad_result
    branch_low = grad_middle.astype(BF16)
    grad_bias_three = jnp.sum(branch_low.astype(F32), 0)
    branch_all = gather_rows(branch_low)
    grad_out = dot(mixed, branch_all, 0, 0)
    width = w_out.shape[0]
    grad_mixed = split_heads(dot(branch_all, w_out, 1, 1).astype(BF16), width)
    scores = scores_of(query, keys, mask_row, scale)
    probs = jnp.exp(scores - log_total)
    grad_probs = jnp.einsum("qhd,khd->hqk", grad_mixed, values, preferred_element_type=F32)
    inner_sum = jnp.sum(probs * grad_probs, -1, keepdims=True)
    grad_scores = (probs * (grad_probs - inner_sum)).astype(BF16)
    grad_q = (jnp.einsum("hqk,khd->qhd", grad_scores, keys, preferred_element_type=F32) * scale).astype(BF16)
    grad_k = (jnp.einsum("hqk,qhd->khd", grad_scores, query, preferred_element_type=F32) * scale).astype(BF16)
    grad_v = jnp.einsum("hqk,qhd->khd", probs.astype(BF16), grad_mixed, preferred_element_type=F32).astype(BF16)
    rows = grad_q.shape[0]
    grad_proj = jnp.concatenate([g.reshape(rows, width) for g in (grad_q, grad_k, grad_v)], 1)
    grad_bias_proj = jnp.sum(grad_proj.astype(F32), 0)
    grad_qkv = dot(normed_all, grad_proj, 0, 0)
    grad_normed = scatter_rows(dot(grad_proj, w_qkv, 1, 1))
    grad_gain_one, grad_shift_one, grad_hidden = norm_back(grad_normed, normal_one, inverse_one, gains[0])
    grad_hidden = grad_hidden + grad_middle
    rows_sum = jnp.stack([grad_gain_one, grad_gain_two, grad_shift_one, grad_bias_three, grad_shift_two, grad_bias_five])
    return (grad_hidden, (grad_qkv, grad_out, grad_fc1, grad_fc2), rows_sum, grad_bias_proj, grad_bias_fc1)


def plain_local(block_input, key_mask, valid, gains, biases, w_qkv, w_out, w_fc1, b_fc1, w_fc2, cotangent):
    layers = w_qkv.shape[0]
    groups = lax.axis_size("seq")
    shards = lax.axis_size("dp")
    me = lax.axis_index("seq")
    width = block_input.shape[2]
    hidden_width = w_fc2.shape[1] * shards
    part = width // groups
    images = block_input.shape[0]
    assert images == 1
    mask_row = lax.all_gather(key_mask, "seq", axis=1, tiled=True)[0]
    tok_valid = (key_mask * valid[:, None]).astype(F32)[0]
    hidden = block_input[0].astype(F32)
    small = jnp.concatenate([gains.reshape(layers, -1), biases.reshape(layers, -1), b_fc1], 1)
    small = lax.all_gather(small, "dp", axis=0).astype(F32)
    n_g, n_b = gains.shape[1] * gains.shape[2], biases.shape[1] * biases.shape[2]
    gains_all = small[:, :, :n_g].reshape(shards, layers, 2, -1).transpose(1, 2, 0, 3).reshape(layers, 2, width)
    biases_all = small[:, :, n_g : n_g + n_b].reshape(shards, layers, 6, -1).transpose(1, 2, 0, 3).reshape(layers, 6, width)
    fc_all = small[:, :, n_g + n_b :].transpose(1, 0, 2).reshape(layers, shards, groups, -1)
    fc_mine = lax.dynamic_index_in_dim(fc_all, me, 2, False).reshape(layers, -1)
    proj_mine = lax.dynamic_index_in_dim(biases_all.reshape(layers, 6, groups, part), me, 2, False)

    def columns(w, outer):
        view = w.reshape(w.shape[0], outer, groups, -1)
        return lax.dynamic_index_in_dim(view, me, 2, False).reshape(w.shape[0], -1)

    def rows_of(w):
        view = w.reshape(groups, -1, w.shape[1])
        return lax.dynamic_index_in_dim(view, me, 0, False)

    def gather(w):
        return lax.all_gather(w, "dp", axis=0, tiled=True)

    weights, params, stored_all, stats = [], [], [], []
    for layer in range(layers):
        weights.append((
            gather(columns(w_qkv[layer], 3)),
            rows_of(gather(w_out[layer])),
            gather(columns(w_fc1[layer], shards)),
            gather(rows_of(w_fc2[layer])),
        ))
        params.append((gains_all[layer], biases_all[layer], proj_mine[layer, 1], proj_mine[layer, 2], fc_mine[layer]))
    for layer in range(layers):
        hidden, stored, stat = forward_layer(hidden, weights[layer], params[layer], mask_row, tok_valid)
        stored_all.append(stored)
        stats.append(stat)
    totals = lax.psum(jnp.concatenate([jnp.stack(stats).reshape(-1), jnp.sum(tok_valid)[None]]), ("dp", "seq"))
    rms = jnp.sqrt(totals[:-1].reshape(layers, 3) / (jnp.maximum(totals[-1], 1.0) * width))

    grad_hidden = cotangent[0].astype(F32) * tok_valid[:, None]
    big = [None] * layers
    sums = [None] * layers
    for layer in reversed(range(layers)):
        grad_hidden, grads, rows_sum, grad_proj, grad_fc = backward_layer(
            grad_hidden, weights[layer], params[layer], stored_all[layer], mask_row
        )
        g_qkv, g_out, g_fc1, g_fc2 = (g.astype(BF16) for g in grads)
        g_out = lax.all_to_all(g_out, "seq", split_axis=1, concat_axis=0, tiled=True)

        def reduce_(g):
            g = lax.psum_scatter(g, "dp", scatter_dimension=0, tiled=True)
            return lax.all_gather(g, "seq", axis=0)

        def join(g, outer):
            view = g.reshape(groups, g.shape[1], outer, -1)
            return view.transpose(1, 2, 0, 3).reshape(g.shape[1], -1)

        big[layer] = (
            join(reduce_(g_qkv), 3).astype(F32),
            join(reduce_(g_out), 1).astype(F32),
            join(reduce_(g_fc1), shards).astype(F32),
            reduce_(g_fc2).reshape(w_fc2.shape[1], -1).astype(F32),
        )
        proj = lax.dynamic_update_slice(jnp.zeros((3, groups, part), F32), grad_proj.reshape(3, 1, part), (0, me, 0))
        fc = lax.dynamic_update_slice(jnp.zeros((shards, groups, hidden_width // (shards * groups)), F32),
                                      grad_fc.reshape(shards, 1, -1), (0, me, 0))
        sums[layer] = jnp.concatenate([
            rows_sum.reshape(6, shards, -1).transpose(1, 0, 2).reshape(shards, -1),
            proj.reshape(3, shards, -1).transpose(1, 0, 2).reshape(shards, -1),
            fc.reshape(shards, -1),
        ], 1)
    flat = jnp.stack(sums, 1).astype(F32)
    flat = lax.psum(lax.psum_scatter(flat, "dp", scatter_dimension=0, tiled=True)[0], "seq")
    per = width // shards
    rows9 = flat[:, : 9 * per].reshape(layers, 9, per)
    grad_bfc1 = flat[:, 9 * per :]
    stack = lambda i: jnp.stack([b[i] for b in big])
    bias_rest = jnp.concatenate([rows9[:, 2:3], rows9[:, 8:9], rows9[:, 3:6]], 1)
    return (
        hidden.astype(BF16)[None],
        grad_hidden[None],
        rms,
        rows9[:, :2],
        bias_rest,
        rows9[:, 6],
        stack(0),
        stack(1),
        stack(2),
        grad_bfc1,
        stack(3),
    )


MESH = pl.DeviceIdType.MESH
NEG = -1000000000.0


def ddot(a, b, ca, cb):
    return lax.dot_general(a, b, (((ca,), (cb,)), ((), ())), preferred_element_type=F32)


def fused_kernel(cfg, x_ref, maskrow_ref, tv_ref, small_ref, w_in, cot_ref,
                 y_ref, gx_ref, tot_ref, o_hbm,
                 W, WO, XR, ZR, AF, QKV, OB, MF, U, H, H2, LSE,
                 BF, PB, R0, R1, R2, DU, GW, DQKV, DO, DKV, DH, MK, MR, PS, PR, SGF, SG, SX, SZ, ST, FIN, STAT,
                 loc_sem, agz_s, agz_r, agx_s, agx_r, ge_s, ge_r, re_s, re_r, wo_s, wo_r, gw_s, gw_r,
                 rx_s, rx_r, rz_s, rz_r, fo_s, fo_r, mk_s, mk_r, st_s, st_r):
    L, M, RB, T, TP, D, NC = cfg["L"], cfg["M"], cfg["RB"], cfg["T"], cfg["TP"], cfg["D"], cfg["NC"]
    S = 4
    R = S * TP
    C = D // S
    FS = cfg["FS"]
    SCALE = 1.0 / math.sqrt(HEAD_DIM)
    COLS = (0, 3 * C, 3 * C + C, 3 * C + C + FS, NC)
    QK, OUT, FC1, FC2 = range(4)
    d = lax.axis_index("dp")
    s = lax.axis_index("seq")
    z = d // 2
    xx = d % 2
    ypos = s // 2
    cpos = s % 2
    core = (d, s + 1 - 2 * cpos)
    ydev = (d, s + 2 - 4 * ypos)
    diag = (d, (s + 1 - 2 * cpos) + 2 - 4 * ypos)
    xdev = (d + 1 - 2 * xx, s)
    zof = [lax.rem(z + k, M) for k in range(M)]
    zdev = [(2 * zof[k] + xx, s) for k in range(M)]
    zfrom = [lax.rem(z + M - k, M) for k in range(M)]

    def rcopy(src, dst, ss, rs, dev):
        return pltpu.make_async_remote_copy(src_ref=src, dst_ref=dst, send_sem=ss, recv_sem=rs,
                                            device_id=dev, device_id_type=MESH)

    bar = pltpu.get_barrier_semaphore()
    for dev in [core, ydev, diag, xdev] + zdev[1:]:
        pl.semaphore_signal(bar, inc=1, device_id=dev, device_id_type=MESH)
    pl.semaphore_wait(bar, 3 + M)

    def wslot(l, zz, xp, j):
        return W.at[l, zz, xp, :, COLS[j]:COLS[j + 1]]

    def wsrc(l, j):
        return w_in.at[l, :, COLS[j]:COLS[j + 1]]

    def ag_pair(p, zz, xp):
        if p == 0:
            return PS.at[zz, xp]
        l, j = divmod(p - 1, 4)
        return wslot(l, zz, xp, j)

    def ag_own(p):
        if p == 0:
            return small_ref
        l, j = divmod(p - 1, 4)
        return wsrc(l, j)

    def ag_z(p, k):
        return rcopy(ag_own(p), ag_pair(p, z, xx), agz_s.at[p, k], agz_r.at[p, z], zdev[k])

    def ag_z_recv(p, k):
        zz = zfrom[k]
        return rcopy(ag_own(p), ag_pair(p, zz, xx), agz_s.at[p, k], agz_r.at[p, zz], zdev[k])

    def ag_x(p, zz, own):
        src = ag_own(p) if own else ag_pair(p, zz, xx)
        return rcopy(src, ag_pair(p, zz, xx), agx_s.at[p, zz], agx_r.at[p, zz], xdev)

    def ag_x_recv(p, zz):
        return rcopy(ag_own(p), ag_pair(p, zz, 1 - xx), agx_s.at[p, zz], agx_r.at[p, zz], xdev)

    def ag_issue(p):
        for k in range(1, M):
            ag_z(p, k).start()
        ag_x(p, z, True).start()

    NP = 1 + 4 * L
    queue = [(p, k) for p in range(NP) for k in range(1, M)]
    state = {"next": 0, "issued": 0}

    def ag_issue_to(n):
        while state["issued"] < min(n, NP):
            ag_issue(state["issued"])
            state["issued"] += 1

    def ag_service(n):
        for _ in range(n):
            if state["next"] == len(queue):
                return
            p, k = queue[state["next"]]
            ag_issue_to(p + 1)
            ag_z_recv(p, k).wait_recv()
            ag_x(p, zfrom[k], False).start()
            state["next"] += 1
            if k == M - 1:
                ag_issue_to(p + 1 + cfg["ahead"])

    def ag_finish(p):
        while state["next"] < (p + 1) * (M - 1):
            ag_service(1)
        for k in range(M):
            ag_x_recv(p, zfrom[k]).wait_recv()

    def ag_drain():
        for p in range(NP):
            for k in range(1, M):
                ag_z(p, k).wait_send()
            for k in range(M):
                ag_x(p, zof[k], k == 0).wait_send()

    locs = []
    for l in range(L):
        locs.append(pltpu.make_async_copy(w_in.at[l], W.at[l, z, xx], loc_sem.at[l]))
    ag_issue_to(1 + cfg["ahead"])
    for c in locs:
        c.start()
    PS[z, xx] = small_ref[...]
    MK[s] = maskrow_ref[...]
    mks = [rcopy(maskrow_ref, MK.at[s], mk_s.at[i], mk_r.at[i], dev) for i, dev in enumerate((core, ydev, diag))]
    for c in mks:
        c.start()
    H[0] = jnp.zeros((TP, D), F32)
    H[0, 0:T, :] = x_ref[...].astype(F32)
    SGF[...] = jnp.zeros_like(SGF)
    SG[...] = jnp.zeros_like(SG)
    STAT[...] = jnp.zeros_like(STAT)
    for c in mks:
        c.wait()
    MR[...] = (MK[0] + MK[1]) + (MK[2] + MK[3])
    ag_finish(0)
    for i in range(M):
        for j in range(2):
            PR[:, 128 * (2 * i + j):128 * (2 * i + j) + 128] = PS[i, j]
    for c in locs:
        c.wait()

    def prow(l, i):
        return PR[12 * l + i:12 * l + i + 1, :]

    def prow_cols(l, i):
        return PR[12 * l + i:12 * l + i + 1, pl.ds(pl.multiple_of(C * s, C), C)]

    HB = TP // 2

    def ge_part(e, buf, i, h):
        rows = pl.ds(h * HB, HB)
        if i == 0:
            return rcopy(buf.at[s, rows], buf.at[s, rows], ge_s.at[e, 0, h], ge_r.at[e, 0, h], core)
        if i == 1:
            return rcopy(buf.at[s, rows], buf.at[s, rows], ge_s.at[e, 1, h], ge_r.at[e, 1, h], ydev)
        return rcopy(buf.at[ydev[1], rows], buf.at[ydev[1], rows], ge_s.at[e, 2, h], ge_r.at[e, 2, h], core)

    def ge_start(e, buf):
        for h in range(2):
            ge_part(e, buf, 1, h).start()
        for h in range(2):
            ge_part(e, buf, 0, h).start()

    def ge_end(e, buf):
        for h in range(2):
            rcopy(buf.at[s, pl.ds(h * HB, HB)], buf.at[ydev[1], pl.ds(h * HB, HB)],
                  ge_s.at[e, 1, h], ge_r.at[e, 1, h], ydev).wait_recv()
            ge_part(e, buf, 2, h).start()
        for h in range(2):
            rcopy(buf.at[s, pl.ds(h * HB, HB)], buf.at[core[1], pl.ds(h * HB, HB)],
                  ge_s.at[e, 0, h], ge_r.at[e, 0, h], core).wait_recv()
        for h in range(2):
            rcopy(buf.at[ydev[1], pl.ds(h * HB, HB)], buf.at[diag[1], pl.ds(h * HB, HB)],
                  ge_s.at[e, 2, h], ge_r.at[e, 2, h], core).wait_recv()
        for i in range(3):
            for h in range(2):
                ge_part(e, buf, i, h).wait_send()

    def re_copy(e, i):
        b = e % 2
        if i == 0:
            return rcopy(PB.at[b, 1 - ypos, 1 - cpos], R0.at[b], re_s.at[e, 0], re_r.at[e, 0], core)
        if i == 1:
            return rcopy(PB.at[b, 1 - ypos, cpos], R1.at[b], re_s.at[e, 1], re_r.at[e, 1], ydev)
        return rcopy(PB.at[b, ypos, 1 - cpos], R2.at[b], re_s.at[e, 2], re_r.at[e, 2], core)

    def re_run(e, partial):
        b = e % 2
        partial(1 - ypos, b)
        re_copy(e, 0).start()
        re_copy(e, 0).wait_recv()

        def add(i, _):
            rows = pl.ds(pl.multiple_of(i * 16, 16), 16)
            PB[b, 1 - ypos, cpos, rows, :] = (PB[b, 1 - ypos, cpos, rows, :].astype(F32) + R0[b, rows, :].astype(F32)).astype(BF16)
            return 0
        lax.fori_loop(0, TP // 16, add, 0)
        re_copy(e, 1).start()
        partial(ypos, b)
        re_copy(e, 2).start()

    def re_end(e):
        for i in (2, 1):
            re_copy(e, i).wait_recv()
        for i in range(3):
            re_copy(e, i).wait_send()

    def re_rows(e, rows):
        b = e % 2
        return (PB[b, ypos, cpos, rows, :].astype(F32) + R2[b, rows, :].astype(F32)) + R1[b, rows, :].astype(F32)

    def partial_of(lhs, rhs, cb):
        def run(chip, b):
            def tile(j, _):
                cols = pl.ds(pl.multiple_of(j * C, C), C)
                r = ddot(lhs(chip), rhs(j), 1, cb).astype(BF16)
                PB[b, chip, :, :, cols] = r.reshape(2, TP, C)
                return 0
            lax.fori_loop(0, S, tile, 0)
        return run

    def row_loop(body, init):
        def one(i, carry):
            return body(pl.ds(pl.multiple_of(i * 16, 16), 16), carry)
        return lax.fori_loop(0, TP // 16, one, init)

    def norm(v):
        center = v - jnp.mean(v, -1, keepdims=True)
        inverse = lax.rsqrt(jnp.mean(center * center, -1, keepdims=True) + epsilon)
        return center * inverse, inverse

    def fold(v):
        return v[0:8] + v[8:16]

    def col_sum(v):
        return jnp.sum(v, axis=0, keepdims=True)

    lane_low = lax.broadcasted_iota(jnp.int32, (1, 2 * HEAD_DIM), 1) < HEAD_DIM
    lane_idx = lax.broadcasted_iota(jnp.int32, (1, 128), 1)

    def attend(l, pair):
        def block(i, _):
            rows = pl.ds(pl.multiple_of(i * TP, 16), TP)
            q = QKV[l, rows, 128 * pair:128 * pair + 128]
            k = QKV[l, :, C + 128 * pair:C + 128 * pair + 128]
            v = QKV[l, :, 2 * C + 128 * pair:2 * C + 128 * pair + 128]
            outs, lses = [], []
            for h in range(2):
                keep = lane_low if h == 0 else jnp.logical_not(lane_low)
                qh = jnp.where(keep, q, jnp.zeros_like(q))
                sc = ddot(qh, k, 1, 1) * SCALE
                sc = jnp.where(MR[0:1, :] > 0, sc, NEG)
                mx = jnp.max(sc, -1, keepdims=True)
                ex = jnp.exp(sc - mx)
                tot = jnp.sum(ex, -1, keepdims=True)
                outs.append(ddot(ex.astype(BF16), v, 1, 0) / tot)
                lses.append(mx + jnp.log(tot))
            OB[l, rows, 128 * pair:128 * pair + 128] = jnp.where(lane_low, outs[0], outs[1]).astype(BF16)
            LSE[l, pair, rows, :] = jnp.where(lane_idx == 0, lses[0], lses[1])
            return 0
        lax.fori_loop(0, S, block, 0)

    def attend_back(l, pair):
        DKV[...] = jnp.zeros_like(DKV)

        def block(i, _):
            rows = pl.ds(pl.multiple_of(i * TP, 16), TP)
            q = QKV[l, rows, 128 * pair:128 * pair + 128]
            k = QKV[l, :, C + 128 * pair:C + 128 * pair + 128]
            v = QKV[l, :, 2 * C + 128 * pair:2 * C + 128 * pair + 128]
            do = DO[rows, 128 * pair:128 * pair + 128]
            lse = LSE[l, pair, rows, :]
            dqs = []
            dk = dv = None
            for h in range(2):
                keep = lane_low if h == 0 else jnp.logical_not(lane_low)
                qh = jnp.where(keep, q, jnp.zeros_like(q))
                doh = jnp.where(keep, do, jnp.zeros_like(do))
                sc = ddot(qh, k, 1, 1) * SCALE
                sc = jnp.where(MR[0:1, :] > 0, sc, NEG)
                p = jnp.exp(sc - lse[:, h:h + 1])
                dp = ddot(doh, v, 1, 1)
                inner = jnp.sum(p * dp, -1, keepdims=True)
                ds = (p * (dp - inner)).astype(BF16)
                dqs.append(ddot(ds, k, 1, 0))
                dkh = ddot(ds, qh, 0, 0)
                dvh = ddot(p.astype(BF16), doh, 0, 0)
                dk = dkh if dk is None else dk + dkh
                dv = dvh if dv is None else dv + dvh
            DQKV[rows, 128 * pair:128 * pair + 128] = (jnp.where(lane_low, dqs[0], dqs[1]) * SCALE).astype(BF16)
            DKV[0] += dk
            DKV[1] += dv
            return 0
        lax.fori_loop(0, S, block, 0)
        DQKV[:, C + 128 * pair:C + 128 * pair + 128] = (DKV[0] * SCALE).astype(BF16)
        DQKV[:, 2 * C + 128 * pair:2 * C + 128 * pair + 128] = DKV[1].astype(BF16)

    peers = (core, ydev, diag)

    def wo_copy(l, i):
        to = peers[i][1]
        return rcopy(W.at[l, to, :, :, COLS[OUT]:COLS[FC1]], WO.at[l, :, :, pl.ds(pl.multiple_of(C * s, C), C)],
                     wo_s.at[l, i], wo_r.at[l, i], peers[i])

    def wo_start(l):
        for i in range(3):
            wo_copy(l, i).start()
        WO[l, :, :, pl.ds(pl.multiple_of(C * s, C), C)] = W[l, s, :, :, COLS[OUT]:COLS[FC1]]

    def wo_end(l):
        for i in range(3):
            wo_copy(l, i).wait()

    def gw_copy(l, i):
        to = peers[i][1]
        return rcopy(WO.at[l, :, :, pl.ds(pl.multiple_of(C * to, C), C)], W.at[l, s, :, :, COLS[OUT]:COLS[FC1]],
                     gw_s.at[l, i], gw_r.at[l, i], peers[i])

    def gw_start(l):
        for i in range(3):
            gw_copy(l, i).start()
        W[l, s, :, :, COLS[OUT]:COLS[FC1]] = WO[l, :, :, pl.ds(pl.multiple_of(C * s, C), C)]

    def gw_end(l):
        for i in range(3):
            gw_copy(l, i).wait()

    def wtile(l, j, a, b):
        n = M // S
        if n == 1:
            return W[l, j, :, :, a:b].reshape(2 * RB, b - a)
        return W[l, pl.ds(j * n, n), :, :, a:b].reshape(2 * RB * n, b - a)

    def forward(l):
        e = 2 * l

        def ln1(rows, _):
            n, _r = norm(H[l, rows, :])
            AF[l, s, rows, :] = (n * prow(l, 0) + prow(l, 2)).astype(BF16)
            return 0
        row_loop(ln1, 0)
        ge_start(e, AF.at[l])
        ag_service(3)
        ge_end(e, AF.at[l])
        ag_finish(1 + 4 * l + QK)
        for n in range(3):
            r = ddot(AF[l].reshape(R, D), W[l, :, :, :, C * n:C * n + C].reshape(D, C), 1, 0)
            if n == 0:
                r = r + prow_cols(l, 3)
            if n == 2:
                r = r + prow_cols(l, 4)
            QKV[l, :, C * n:C * n + C] = r.astype(BF16)
        ag_finish(1 + 4 * l + OUT)
        wo_start(l)
        attend(l, 0)
        ag_service(1)
        attend(l, 1)
        ag_service(1)
        wo_end(l)
        re_run(e + 0, partial_of(
            lambda chip: OB[l, pl.ds(pl.multiple_of(chip * 2 * TP, 16), 2 * TP), :],
            lambda j: WO[l, :, :, pl.ds(pl.multiple_of(j * C, C), C)].reshape(C, C), 0))
        ag_service(1)
        re_end(e + 0)

        def post(rows, acc):
            hv = H[l, rows, :]
            br = re_rows(e + 0, rows) + prow(l, 5)
            mid = hv + br
            H2[l, rows, :] = mid
            n, _r = norm(mid)
            MF[l, s, rows, :] = (n * prow(l, 1) + prow(l, 6)).astype(BF16)
            t = tv_ref[rows, 0:1]
            return acc[0] + fold(t * hv * hv), acc[1] + fold(t * br * br)
        zero = jnp.zeros((8, D), F32)
        s0, s1 = row_loop(post, (zero, zero))
        ge_start(e + 1, MF.at[l])
        ag_service(2)
        ge_end(e + 1, MF.at[l])
        ag_finish(1 + 4 * l + FC1)
        bias = PR[pl.ds(12 * l + 8 + s, 1), :]
        for j in range(FS // C):
            u = ddot(MF[l].reshape(R, D), W[l, :, :, :, COLS[FC1] + C * j:COLS[FC1] + C * j + C].reshape(D, C), 1, 0)
            u = u + bias[:, C * j:C * j + C]
            U[l, :, C * j:C * j + C] = u
            GW[:, C * j:C * j + C] = (u / (1.0 + jnp.exp(-1.702 * u))).astype(BF16)
        ag_finish(1 + 4 * l + FC2)
        re_run(e + 1, partial_of(
            lambda chip: GW[pl.ds(pl.multiple_of(chip * 2 * TP, 16), 2 * TP), :],
            lambda j: W[l, :, :, :, pl.ds(pl.multiple_of(COLS[FC2] + j * C, C), C)].reshape(FS, C), 0))
        ag_service(2)
        re_end(e + 1)

        def last(rows, acc):
            out = re_rows(e + 1, rows) + prow(l, 7)
            res = H2[l, rows, :] + out
            H[l + 1, rows, :] = res
            t = tv_ref[rows, 0:1]
            return acc + fold(t * out * out)
        s2 = row_loop(last, zero)
        for i, v in enumerate((s0, s1, s2)):
            STAT[...] = jnp.where(lane_idx == 3 * l + i, jnp.sum(col_sum(v), axis=1, keepdims=True), STAT[...])

    for l in range(L):
        forward(l)
    STAT[...] = jnp.where(lane_idx == 3 * L, col_sum(tv_ref[:, 0:1]), STAT[...])
    y_ref[...] = H[L, 0:T, :].astype(BF16)
    ag_drain()

    def rx_copy(l, j):
        a, b = COLS[j], COLS[j + 1]
        return rcopy(W.at[l, :, 1 - xx, :, a:b], XR.at[l, :, :, a:b], rx_s.at[l, j], rx_r.at[l, j], xdev)

    def rz_copy(l, j, k):
        a, b = COLS[j], COLS[j + 1]
        return rcopy(XR.at[l, zof[k], :, a:b], ZR.at[l, z, :, a:b], rz_s.at[l, j, k], rz_r.at[l, j, k], zdev[k])

    def rz_recv(l, j, k):
        a, b = COLS[j], COLS[j + 1]
        return rcopy(XR.at[l, zof[k], :, a:b], ZR.at[l, zfrom[k], :, a:b], rz_s.at[l, j, k], rz_r.at[l, j, k], zdev[k])

    def fo_copy(l, j, i):
        a, b = COLS[j], COLS[j + 1]
        return rcopy(FIN.at[l, :, a:b], o_hbm.at[l, s, :, a:b], fo_s.at[l, j, i], fo_r.at[l, j, i], peers[i])

    def fo_recv(l, j, i):
        a, b = COLS[j], COLS[j + 1]
        return rcopy(FIN.at[l, :, a:b], o_hbm.at[l, peers[i][1], :, a:b], fo_s.at[l, j, i], fo_r.at[l, j, i], peers[i])

    def fo_local(l, j):
        a, b = COLS[j], COLS[j + 1]
        return pltpu.make_async_copy(FIN.at[l, :, a:b], o_hbm.at[l, s, :, a:b], loc_sem.at[L + 4 * l + j])

    def red_first(l, j):
        a, b = COLS[j], COLS[j + 1]
        rx_copy(l, j).wait_recv()
        for k in list(range(1, M)) + [0]:
            zz = zof[k]
            for r0 in range(0, RB, 32):
                XR[l, zz, r0:r0 + 32, a:b] = (XR[l, zz, r0:r0 + 32, a:b].astype(F32) + W[l, zz, xx, r0:r0 + 32, a:b].astype(F32)).astype(BF16)
            if k > 0:
                rz_copy(l, j, k).start()

    def red_second(l, j):
        a, b = COLS[j], COLS[j + 1]
        for k in range(1, M):
            rz_recv(l, j, k).wait_recv()
        for r0 in range(0, RB, 32):
            t = XR[l, z, r0:r0 + 32, a:b].astype(F32)
            for k in range(1, M):
                t = t + ZR[l, zfrom[k], r0:r0 + 32, a:b].astype(F32)
            FIN[l, r0:r0 + 32, a:b] = t.astype(BF16)
        for i in range(3):
            fo_copy(l, j, i).start()
        fo_local(l, j).start()

    def red_end(l, j):
        rx_copy(l, j).wait_send()
        for k in range(1, M):
            rz_copy(l, j, k).wait_send()
        for i in range(3):
            fo_copy(l, j, i).wait_send()
            fo_recv(l, j, i).wait_recv()
        fo_local(l, j).wait()

    events = []
    done = {"n": 0}

    def red_push(l, j):
        rx_copy(l, j).start()
        events.append((red_first, l, j))

    def red_service(n):
        for _ in range(n):
            if done["n"] >= len(events):
                return
            f, l, j = events[done["n"]]
            done["n"] += 1
            f(l, j)
            if f is red_first:
                events.insert(min(done["n"] + 1, len(events)), (red_second, l, j))

    def norm_back(l, src, e, gain):
        def one(rows, acc):
            n, r = norm(src[l, rows, :])
            dm = re_rows(e, rows)
            dn = dm * gain
            pm = jnp.mean(dn, -1, keepdims=True)
            cm = jnp.mean(dn * n, -1, keepdims=True)
            DH[rows, :] = DH[rows, :] + r * (dn - pm - n * cm)
            return acc[0] + fold(dm * n), acc[1] + fold(dm)
        zero = jnp.zeros((8, D), F32)
        g, b = row_loop(one, (zero, zero))
        return col_sum(g), col_sum(b)

    def low_of(buf):
        def one(rows, acc):
            v = DH[rows, :].astype(BF16)
            buf[s, rows, :] = v
            return acc + fold(v.astype(F32))
        return col_sum(row_loop(one, jnp.zeros((8, D), F32)))

    def backward(l):
        ge_a = re_a = 2 * L + 2 * (L - 1 - l)
        ge_b = re_b = ge_a + 1
        B0, B1 = BF.at[0], BF.at[1]
        SGF[12 * l + 7:12 * l + 8, :] = low_of(B0)
        ge_start(ge_a, B0)
        red_service(1)
        ge_end(ge_a, B0)
        for j in range(FS // C):
            dg = ddot(BF[0].reshape(R, D), wtile(l, j, COLS[FC2], COLS[FC2] + D), 1, 1)
            u = U[l, :, C * j:C * j + C]
            sg = 1.0 / (1.0 + jnp.exp(-1.702 * u))
            GW[:, C * j:C * j + C] = (u * sg).astype(BF16)
            du = (dg * (sg + 1.702 * u * sg * (1.0 - sg))).astype(BF16)
            DU[:, C * j:C * j + C] = du
            SGF[pl.ds(12 * l + 8 + s, 1), C * j:C * j + C] = jnp.sum(du.astype(F32), axis=0, keepdims=True)
        red_service(1)
        for j in range(FS // C):
            W[l, j, :, :, COLS[FC2]:COLS[FC2] + D] = ddot(GW[:, C * j:C * j + C], BF[0].reshape(R, D), 0, 0).astype(BF16).reshape(2, RB, D)
        red_push(l, FC2)
        re_run(re_a, partial_of(
            lambda chip: DU[pl.ds(pl.multiple_of(chip * 2 * TP, 16), 2 * TP), :],
            lambda j: wtile(l, j, COLS[FC1], COLS[FC1] + FS), 1))
        for j in range(S):
            W[l, j, :, :, COLS[FC1]:COLS[FC1] + FS] = ddot(MF[l, :, :, C * j:C * j + C].reshape(R, C), DU[...], 0, 0).astype(BF16).reshape(2, RB, FS)
        red_push(l, FC1)
        re_end(re_a)
        gg, bb = norm_back(l, H2, re_a, prow(l, 1))
        SGF[12 * l + 1:12 * l + 2, :] = gg
        SGF[12 * l + 6:12 * l + 7, :] = bb
        SGF[12 * l + 5:12 * l + 6, :] = low_of(B1)
        ge_start(ge_b, B1)
        red_service(1)
        ge_end(ge_b, B1)
        DO[...] = ddot(BF[1].reshape(R, D), WO[l].reshape(C, D), 1, 1).astype(BF16)
        for j in range(S):
            WO[l, :, :, C * j:C * j + C] = ddot(OB[l], BF[1, :, :, C * j:C * j + C].reshape(R, C), 0, 0).astype(BF16).reshape(2, RB, C)
        gw_start(l)
        attend_back(l, 0)
        red_service(1)
        attend_back(l, 1)
        gw_end(l)
        red_push(l, OUT)
        red_service(1)
        for i, (row, c0) in enumerate(((3, 0), (4, 2 * C))):
            SGF[12 * l + row:12 * l + row + 1, pl.ds(pl.multiple_of(C * s, C), C)] = jnp.sum(
                DQKV[:, c0:c0 + C].astype(F32), axis=0, keepdims=True)
        re_run(re_b, partial_of(
            lambda chip: DQKV[pl.ds(pl.multiple_of(chip * 2 * TP, 16), 2 * TP), :],
            lambda j: wtile(l, j, 0, 3 * C), 1))
        for j in range(S):
            W[l, j, :, :, 0:3 * C] = ddot(AF[l, :, :, C * j:C * j + C].reshape(R, C), DQKV[...], 0, 0).astype(BF16).reshape(2, RB, 3 * C)
        red_push(l, QK)
        re_end(re_b)
        gg, bb = norm_back(l, H, re_b, prow(l, 0))
        SGF[12 * l + 0:12 * l + 1, :] = gg
        SGF[12 * l + 2:12 * l + 3, :] = bb

    DH[...] = jnp.zeros_like(DH)
    DH[0:T, :] = cot_ref[...].astype(F32) * tv_ref[0:T, 0:1]
    for l in reversed(range(L)):
        backward(l)
    gx_ref[...] = DH[0:T, :]

    for i in range(M):
        for j in range(2):
            SG[i, j, 0:24, :] = SGF[0:24, 128 * (2 * i + j):128 * (2 * i + j) + 128]
            SG[i, j, 24:25, :] = STAT[...]
    sgx = rcopy(SG.at[:, 1 - xx], SX, st_s.at[0], st_r.at[0], xdev)
    sgx.start()
    sgx.wait()
    SX[...] = SX[...] + SG[:, xx]
    SZ[z] = SX[z]

    def sz(k, frm):
        return rcopy(SX.at[zof[k]], SZ.at[zfrom[k] if frm else z], st_s.at[k], st_r.at[k], zdev[k])
    for k in range(1, M):
        sz(k, False).start()
    red_service(2)
    for k in range(1, M):
        sz(k, True).wait_recv()
    tot = SZ[0]
    for k in range(1, M):
        tot = tot + SZ[k]
    ST[s] = tot

    def stc(i, frm):
        slot = peers[i][1] if frm else s
        return rcopy(ST.at[s], ST.at[slot], st_s.at[M + i], st_r.at[M + i], peers[i])
    for i in range(3):
        stc(i, False).start()
    while done["n"] < len(events):
        red_service(1)
    for i in range(3):
        stc(i, True).wait_recv()
    tot_ref[...] = (ST[0] + ST[1]) + (ST[2] + ST[3])
    for k in range(1, M):
        sz(k, False).wait_send()
    for i in range(3):
        stc(i, False).wait_send()
    for l in reversed(range(L)):
        for j in (FC2, FC1, OUT, QK):
            red_end(l, j)


def fused_local(cfg, block_input, key_mask, valid, gains, biases, w_qkv, w_out, w_fc1, b_fc1, w_fc2, cotangent):
    L, M, RB, T, TP, D, NC, FS = (cfg[n] for n in ("L", "M", "RB", "T", "TP", "D", "NC", "FS"))
    S, dp = 4, 2 * M
    me = lax.axis_index("seq")
    C = D // S
    R = S * TP

    def columns(w, outer):
        view = w.reshape(L, RB, outer, S, -1)
        return lax.dynamic_index_in_dim(view, me, 3, False).reshape(L, RB, -1)

    w_in = jnp.concatenate([
        columns(w_qkv, 3), columns(w_out, 1), columns(w_fc1, dp),
        lax.dynamic_index_in_dim(w_fc2.reshape(L, S, RB, D), me, 1, False)], 2)
    small = jnp.concatenate([gains, biases, b_fc1.reshape(L, S, -1)], 1).astype(F32).reshape(L * 12, RB)
    mask = jnp.pad(key_mask[0].astype(F32), (0, TP - T))
    mask_row = jnp.where(jnp.arange(S)[:, None] == me, mask[None, :], 0.0).reshape(1, R)
    mask_row = jnp.broadcast_to(mask_row, (8, R))
    tv = jnp.broadcast_to((mask * valid[0].astype(F32))[:, None], (TP, 128))
    vm = pl.BlockSpec(memory_space=pltpu.VMEM)
    hbm = pl.BlockSpec(memory_space=pl.ANY)
    dma = pltpu.SemaphoreType.DMA
    v = pltpu.VMEM
    NP, NE = 1 + 4 * L, 4 * L
    y, gx, tot, og = pl.pallas_call(
        partial(fused_kernel, cfg),
        out_shape=(
            jax.ShapeDtypeStruct((T, D), BF16),
            jax.ShapeDtypeStruct((T, D), F32),
            jax.ShapeDtypeStruct((32, RB), F32),
            jax.ShapeDtypeStruct((L, S, RB, NC), BF16),
        ),
        in_specs=[vm, vm, vm, vm, hbm, vm],
        out_specs=(vm, vm, vm, hbm),
        scratch_shapes=[
            v((L, M, 2, RB, NC), BF16),
            v((L, 2, RB, D), BF16),
            v((L, M, RB, NC), BF16),
            v((L, M, RB, NC), BF16),
            v((L, S, TP, D), BF16),
            v((L, R, 3 * C), BF16),
            v((L, R, C), BF16),
            v((L, S, TP, D), BF16),
            v((L, R, FS), F32),
            v((L + 1, TP, D), F32),
            v((L, TP, D), F32),
            v((L, 2, R, 128), F32),
            v((2, S, TP, D), BF16),
            v((2, 2, 2, TP, D), BF16),
            v((2, TP, D), BF16),
            v((2, TP, D), BF16),
            v((2, TP, D), BF16),
            v((R, FS), BF16),
            v((R, FS), BF16),
            v((R, 3 * C), BF16),
            v((R, C), BF16),
            v((2, R, 128), F32),
            v((TP, D), F32),
            v((S, 8, R), F32),
            v((8, R), F32),
            v((M, 2, 12 * L, RB), F32),
            v((12 * L, D), F32),
            v((12 * L, D), F32),
            v((M, 2, 32, RB), F32),
            v((M, 32, RB), F32),
            v((M, 32, RB), F32),
            v((S, 32, RB), F32),
            v((L, RB, NC), BF16),
            v((1, RB), F32),
            dma((5 * L,)),
            dma((NP, M)), dma((NP, M)), dma((NP, M)), dma((NP, M)),
            dma((NE, 3, 2)), dma((NE, 3, 2)), dma((NE, 3)), dma((NE, 3)),
            dma((L, 3)), dma((L, 3)), dma((L, 3)), dma((L, 3)),
            dma((L, 4)), dma((L, 4)), dma((L, 4, M)), dma((L, 4, M)),
            dma((L, 4, 3)), dma((L, 4, 3)), dma((3,)), dma((3,)), dma((M + 3,)), dma((M + 3,)),
        ],
        compiler_params=pltpu.CompilerParams(
            collective_id=0, has_side_effects=True, vmem_limit_bytes=cfg["vmem"]),
        cost_estimate=pl.CostEstimate(flops=24_000_000_000, bytes_accessed=20_000_000, transcendentals=0),
    )(block_input[0], mask_row, tv, small, w_in, cotangent[0])
    g = og.astype(F32)
    parts = (g[..., :3 * C], g[..., 3 * C:4 * C], g[..., 4 * C:4 * C + FS], g[..., 4 * C + FS:])
    join = lambda a, outer: a.reshape(L, S, RB, outer, -1).transpose(0, 2, 3, 1, 4).reshape(L, RB, -1)
    rows = tot[:12 * L].reshape(L, 12, RB)
    rms = jnp.sqrt(tot[24, :3 * L].reshape(L, 3) / (jnp.maximum(tot[24, 3 * L], 1.0) * D))
    return (
        y[None],
        gx[None],
        rms,
        rows[:, :2],
        jnp.concatenate([rows[:, 2:3], rows[:, 4:8]], 1),
        rows[:, 3],
        join(parts[0], 3),
        join(parts[1], 1),
        join(parts[2], dp),
        rows[:, 8:12].reshape(L, S * RB),
        parts[3].reshape(L, S * RB, D),
    )


def local(*args):
    block_input, w_qkv, w_fc2 = args[0], args[5], args[9]
    L, RB = w_qkv.shape[:2]
    T, D = block_input.shape[1:]
    S, dp = lax.axis_size("seq"), lax.axis_size("dp")
    FS = w_fc2.shape[1] * dp // S
    fits = (S == 4 and dp == 2 * S and RB % 128 == 0 and D // S == 2 * RB and L * 12 + 1 <= 32
            and FS // dp == RB and HEAD_DIM * 2 == 128 and D // S == 4 * HEAD_DIM and block_input.shape[0] == 1)
    if not fits:
        return plain_local(*args)
    cfg = dict(L=L, M=dp // 2, RB=RB, T=T, TP=-(-T // 16) * 16, D=D, NC=D + 2 * FS, FS=FS, ahead=2, vmem=60 * 2**20)
    return fused_local(cfg, *args)


def solution(mesh):
    return jax.shard_map(
        local,
        mesh=mesh,
        in_specs=(
            P("dp", "seq", None),
            P("dp", "seq"),
            P("dp"),
            P(None, None, "dp"),
            P(None, None, "dp"),
            P(None, "dp", None),
            P(None, "dp", None),
            P(None, "dp", None),
            P(None, "dp"),
            P(None, "dp", None),
            P("dp", "seq", None),
        ),
        out_specs=(
            P("dp", "seq", None),
            P("dp", "seq", None),
            P(),
            P(None, None, "dp"),
            P(None, None, "dp"),
            P(None, "dp"),
            P(None, "dp", None),
            P(None, "dp", None),
            P(None, "dp", None),
            P(None, "dp"),
            P(None, "dp", None),
        ),
        check_vma=False,
    )
```

```python
from functools import partial
import math

import jax
import jax.numpy as jnp
from jax import lax
from jax.experimental import pallas as pl
from jax.experimental.pallas import tpu as pltpu
from jax.sharding import PartitionSpec as P

HEADS = 16
HEAD_DIM = 64
F32 = jnp.float32
BF16 = jnp.bfloat16

epsilon = 1e-05


def norm_parts(values_in, gain, shift):
    center = values_in - jnp.mean(values_in, -1, keepdims=True)
    inverse = lax.rsqrt(jnp.mean(center * center, -1, keepdims=True) + epsilon)
    normal = center * inverse
    return (normal * gain + shift, normal, inverse)


def norm_back(grad_output, normal, inverse, gain):
    grad_gain = jnp.sum(grad_output * normal, 0)
    grad_shift = jnp.sum(grad_output, 0)
    grad_norm = grad_output * gain
    plain_mean = jnp.mean(grad_norm, -1, keepdims=True)
    cross_mean = jnp.mean(grad_norm * normal, -1, keepdims=True)
    return (grad_gain, grad_shift, inverse * (grad_norm - plain_mean - normal * cross_mean))


def dot(a, b, ca=1, cb=0):
    return lax.dot_general(a, b, (((ca,), (cb,)), ((), ())), preferred_element_type=F32)


def split_heads(x, width):
    return x.reshape(x.shape[0], width // HEAD_DIM, HEAD_DIM)


def scores_of(query, keys, mask_row, scale):
    scores = jnp.einsum("qhd,khd->hqk", query, keys, preferred_element_type=F32) * scale
    return jnp.where(mask_row[None, None, :] > 0, scores, -1000000000.0)


def gather_rows(x):
    return lax.all_gather(x, "seq", axis=0, tiled=True)


def scatter_rows(x):
    return lax.psum_scatter(x.astype(BF16), "seq", scatter_dimension=0, tiled=True).astype(F32)


def forward_layer(hidden, weights, params, mask_row, tok_valid):
    w_qkv, w_out, w_fc1, w_fc2 = weights
    gains, biases, bias_q, bias_v, b_fc1 = params
    scale = 1.0 / math.sqrt(HEAD_DIM)
    width = w_out.shape[0]
    normed, normal_one, inverse_one = norm_parts(hidden, gains[0], biases[0])
    normed_all = gather_rows(normed.astype(BF16))
    packed = dot(normed_all, w_qkv)
    packed = (packed + jnp.concatenate([bias_q, jnp.zeros_like(bias_q), bias_v])).astype(BF16)
    query, keys, values = (split_heads(packed[:, i * width : (i + 1) * width], width) for i in range(3))
    scores = scores_of(query, keys, mask_row, scale)
    row_max = jnp.max(scores, -1, keepdims=True)
    log_total = row_max + jnp.log(jnp.sum(jnp.exp(scores - row_max), -1, keepdims=True))
    probs = jnp.exp(scores - log_total).astype(BF16)
    mixed = jnp.einsum("hqk,khd->qhd", probs, values, preferred_element_type=F32).astype(BF16)
    mixed = mixed.reshape(mixed.shape[0], width)
    branch = scatter_rows(dot(mixed, w_out)) + biases[3]
    middle = hidden + branch
    normed_two, normal_two, inverse_two = norm_parts(middle, gains[1], biases[4])
    normed_two_all = gather_rows(normed_two.astype(BF16))
    inner = dot(normed_two_all, w_fc1) + b_fc1
    gate_sig = jax.nn.sigmoid(1.702 * inner)
    gated = (inner * gate_sig).astype(BF16)
    output = scatter_rows(dot(gated, w_fc2)) + biases[5]
    stat = jnp.stack([jnp.sum(tok_valid * jnp.sum(v * v, -1)) for v in (hidden, branch, output)])
    stored = (normal_one, inverse_one, normed_all, query, keys, values, log_total, mixed,
              normal_two, inverse_two, normed_two_all, inner, gate_sig, gated)
    return (middle + output, stored, stat)


def backward_layer(grad_result, weights, params, stored, mask_row):
    w_qkv, w_out, w_fc1, w_fc2 = weights
    gains = params[0]
    scale = 1.0 / math.sqrt(HEAD_DIM)
    (normal_one, inverse_one, normed_all, query, keys, values, log_total, mixed,
     normal_two, inverse_two, normed_two_all, inner, gate_sig, gated) = stored
    out_low = grad_result.astype(BF16)
    grad_bias_five = jnp.sum(out_low.astype(F32), 0)
    out_all = gather_rows(out_low)
    grad_fc2 = dot(gated, out_all, 0, 0)
    grad_gated = dot(out_all, w_fc2, 1, 1)
    grad_inner = (grad_gated * (gate_sig + 1.702 * inner * gate_sig * (1.0 - gate_sig))).astype(BF16)
    grad_bias_fc1 = jnp.sum(grad_inner.astype(F32), 0)
    grad_fc1 = dot(normed_two_all, grad_inner, 0, 0)
    grad_normed_two = scatter_rows(dot(grad_inner, w_fc1, 1, 1))
    grad_gain_two, grad_shift_two, grad_middle = norm_back(grad_normed_two, normal_two, inverse_two, gains[1])
    grad_middle = grad_middle + grad_result
    branch_low = grad_middle.astype(BF16)
    grad_bias_three = jnp.sum(branch_low.astype(F32), 0)
    branch_all = gather_rows(branch_low)
    grad_out = dot(mixed, branch_all, 0, 0)
    width = w_out.shape[0]
    grad_mixed = split_heads(dot(branch_all, w_out, 1, 1).astype(BF16), width)
    scores = scores_of(query, keys, mask_row, scale)
    probs = jnp.exp(scores - log_total)
    grad_probs = jnp.einsum("qhd,khd->hqk", grad_mixed, values, preferred_element_type=F32)
    inner_sum = jnp.sum(probs * grad_probs, -1, keepdims=True)
    grad_scores = (probs * (grad_probs - inner_sum)).astype(BF16)
    grad_q = (jnp.einsum("hqk,khd->qhd", grad_scores, keys, preferred_element_type=F32) * scale).astype(BF16)
    grad_k = (jnp.einsum("hqk,qhd->khd", grad_scores, query, preferred_element_type=F32) * scale).astype(BF16)
    grad_v = jnp.einsum("hqk,qhd->khd", probs.astype(BF16), grad_mixed, preferred_element_type=F32).astype(BF16)
    rows = grad_q.shape[0]
    grad_proj = jnp.concatenate([g.reshape(rows, width) for g in (grad_q, grad_k, grad_v)], 1)
    grad_bias_proj = jnp.sum(grad_proj.astype(F32), 0)
    grad_qkv = dot(normed_all, grad_proj, 0, 0)
    grad_normed = scatter_rows(dot(grad_proj, w_qkv, 1, 1))
    grad_gain_one, grad_shift_one, grad_hidden = norm_back(grad_normed, normal_one, inverse_one, gains[0])
    grad_hidden = grad_hidden + grad_middle
    rows_sum = jnp.stack([grad_gain_one, grad_gain_two, grad_shift_one, grad_bias_three, grad_shift_two, grad_bias_five])
    return (grad_hidden, (grad_qkv, grad_out, grad_fc1, grad_fc2), rows_sum, grad_bias_proj, grad_bias_fc1)


def plain_local(block_input, key_mask, valid, gains, biases, w_qkv, w_out, w_fc1, b_fc1, w_fc2, cotangent):
    layers = w_qkv.shape[0]
    groups = lax.axis_size("seq")
    shards = lax.axis_size("dp")
    me = lax.axis_index("seq")
    width = block_input.shape[2]
    hidden_width = w_fc2.shape[1] * shards
    part = width // groups
    images = block_input.shape[0]
    assert images == 1
    mask_row = lax.all_gather(key_mask, "seq", axis=1, tiled=True)[0]
    tok_valid = (key_mask * valid[:, None]).astype(F32)[0]
    hidden = block_input[0].astype(F32)
    small = jnp.concatenate([gains.reshape(layers, -1), biases.reshape(layers, -1), b_fc1], 1)
    small = lax.all_gather(small, "dp", axis=0).astype(F32)
    n_g, n_b = gains.shape[1] * gains.shape[2], biases.shape[1] * biases.shape[2]
    gains_all = small[:, :, :n_g].reshape(shards, layers, 2, -1).transpose(1, 2, 0, 3).reshape(layers, 2, width)
    biases_all = small[:, :, n_g : n_g + n_b].reshape(shards, layers, 6, -1).transpose(1, 2, 0, 3).reshape(layers, 6, width)
    fc_all = small[:, :, n_g + n_b :].transpose(1, 0, 2).reshape(layers, shards, groups, -1)
    fc_mine = lax.dynamic_index_in_dim(fc_all, me, 2, False).reshape(layers, -1)
    proj_mine = lax.dynamic_index_in_dim(biases_all.reshape(layers, 6, groups, part), me, 2, False)

    def columns(w, outer):
        view = w.reshape(w.shape[0], outer, groups, -1)
        return lax.dynamic_index_in_dim(view, me, 2, False).reshape(w.shape[0], -1)

    def rows_of(w):
        view = w.reshape(groups, -1, w.shape[1])
        return lax.dynamic_index_in_dim(view, me, 0, False)

    def gather(w):
        return lax.all_gather(w, "dp", axis=0, tiled=True)

    weights, params, stored_all, stats = [], [], [], []
    for layer in range(layers):
        weights.append((
            gather(columns(w_qkv[layer], 3)),
            rows_of(gather(w_out[layer])),
            gather(columns(w_fc1[layer], shards)),
            gather(rows_of(w_fc2[layer])),
        ))
        params.append((gains_all[layer], biases_all[layer], proj_mine[layer, 1], proj_mine[layer, 2], fc_mine[layer]))
    for layer in range(layers):
        hidden, stored, stat = forward_layer(hidden, weights[layer], params[layer], mask_row, tok_valid)
        stored_all.append(stored)
        stats.append(stat)
    totals = lax.psum(jnp.concatenate([jnp.stack(stats).reshape(-1), jnp.sum(tok_valid)[None]]), ("dp", "seq"))
    rms = jnp.sqrt(totals[:-1].reshape(layers, 3) / (jnp.maximum(totals[-1], 1.0) * width))

    grad_hidden = cotangent[0].astype(F32) * tok_valid[:, None]
    big = [None] * layers
    sums = [None] * layers
    for layer in reversed(range(layers)):
        grad_hidden, grads, rows_sum, grad_proj, grad_fc = backward_layer(
            grad_hidden, weights[layer], params[layer], stored_all[layer], mask_row
        )
        g_qkv, g_out, g_fc1, g_fc2 = (g.astype(BF16) for g in grads)
        g_out = lax.all_to_all(g_out, "seq", split_axis=1, concat_axis=0, tiled=True)

        def reduce_(g):
            g = lax.psum_scatter(g, "dp", scatter_dimension=0, tiled=True)
            return lax.all_gather(g, "seq", axis=0)

        def join(g, outer):
            view = g.reshape(groups, g.shape[1], outer, -1)
            return view.transpose(1, 2, 0, 3).reshape(g.shape[1], -1)

        big[layer] = (
            join(reduce_(g_qkv), 3).astype(F32),
            join(reduce_(g_out), 1).astype(F32),
            join(reduce_(g_fc1), shards).astype(F32),
            reduce_(g_fc2).reshape(w_fc2.shape[1], -1).astype(F32),
        )
        proj = lax.dynamic_update_slice(jnp.zeros((3, groups, part), F32), grad_proj.reshape(3, 1, part), (0, me, 0))
        fc = lax.dynamic_update_slice(jnp.zeros((shards, groups, hidden_width // (shards * groups)), F32),
                                      grad_fc.reshape(shards, 1, -1), (0, me, 0))
        sums[layer] = jnp.concatenate([
            rows_sum.reshape(6, shards, -1).transpose(1, 0, 2).reshape(shards, -1),
            proj.reshape(3, shards, -1).transpose(1, 0, 2).reshape(shards, -1),
            fc.reshape(shards, -1),
        ], 1)
    flat = jnp.stack(sums, 1).astype(F32)
    flat = lax.psum(lax.psum_scatter(flat, "dp", scatter_dimension=0, tiled=True)[0], "seq")
    per = width // shards
    rows9 = flat[:, : 9 * per].reshape(layers, 9, per)
    grad_bfc1 = flat[:, 9 * per :]
    stack = lambda i: jnp.stack([b[i] for b in big])
    bias_rest = jnp.concatenate([rows9[:, 2:3], rows9[:, 8:9], rows9[:, 3:6]], 1)
    return (
        hidden.astype(BF16)[None],
        grad_hidden[None],
        rms,
        rows9[:, :2],
        bias_rest,
        rows9[:, 6],
        stack(0),
        stack(1),
        stack(2),
        grad_bfc1,
        stack(3),
    )


MESH = pl.DeviceIdType.MESH
NEG = -1000000000.0


def ddot(a, b, ca, cb):
    return lax.dot_general(a, b, (((ca,), (cb,)), ((), ())), preferred_element_type=F32)


def fused_kernel(cfg, x_ref, mask_ref, valid_ref, gains_ref, biases_ref, bfc_ref, cot_ref, w_qkv, w_out, w_fc1, w_fc2,
                 y_ref, gx_ref, rms_ref, ogain_ref, obias_ref, oquery_ref, obfc_ref, o_qkv, o_out, o_fc1, o_fc2,
                 W, WO, XR, ZR, AF, QKV, OB, MF, U, H, H2, LSE,
                 GF, BF, PB, R0, R1, R2, DU, GW, DQKV, DO, DKV, DH, MK, MR, TV, PS, PR, SGF, SG, SX, SZ, ST, FIN, STAT,
                 loc_sem, agz_s, agz_r, agx_s, agx_r, ge_s, ge_r, re_s, re_r, wo_s, wo_r, gw_s, gw_r,
                 rx_s, rx_r, rz_s, rz_r, fo_s, fo_r, mk_s, mk_r, st_s, st_r):
    L, M, RB, T, TP, D, NC = cfg["L"], cfg["M"], cfg["RB"], cfg["T"], cfg["TP"], cfg["D"], cfg["NC"]
    S = 4
    R = S * TP
    C = D // S
    FS = cfg["FS"]
    SCALE = 1.0 / math.sqrt(HEAD_DIM)
    COLS = (0, 3 * C, 3 * C + C, 3 * C + C + FS, NC)
    QK, OUT, FC1, FC2 = range(4)
    d = lax.axis_index("dp")
    s = lax.axis_index("seq")
    z = d // 2
    xx = d % 2
    ypos = s // 2
    cpos = s % 2
    core = (d, s + 1 - 2 * cpos)
    ydev = (d, s + 2 - 4 * ypos)
    diag = (d, (s + 1 - 2 * cpos) + 2 - 4 * ypos)
    xdev = (d + 1 - 2 * xx, s)
    zof = [lax.rem(z + k, M) for k in range(M)]
    zdev = [(2 * zof[k] + xx, s) for k in range(M)]
    zfrom = [lax.rem(z + M - k, M) for k in range(M)]

    def rcopy(src, dst, ss, rs, dev):
        return pltpu.make_async_remote_copy(src_ref=src, dst_ref=dst, send_sem=ss, recv_sem=rs,
                                            device_id=dev, device_id_type=MESH)

    bar = pltpu.get_barrier_semaphore()
    for dev in [core, ydev, diag, xdev] + zdev[1:]:
        pl.semaphore_signal(bar, inc=1, device_id=dev, device_id_type=MESH)
    pl.semaphore_wait(bar, 3 + M)

    def wslot(l, zz, xp, j):
        return W.at[l, zz, xp, :, COLS[j]:COLS[j + 1]]

    def own_parts(l, j, s):
        a = COLS[j]

        def at_s(start, width):
            return pl.ds(pl.multiple_of(start + width * s, width), width)
        if j == QK:
            return [(w_qkv.at[l, :, at_s(D * i, C)], o_qkv.at[l, :, at_s(D * i, C)], a + C * i, C) for i in range(3)]
        if j == OUT:
            return [(w_out.at[l, :, at_s(0, C)], o_out.at[l, :, at_s(0, C)], a, C)]
        if j == FC1:
            return [(w_fc1.at[l, :, at_s(S * RB * i, RB)], o_fc1.at[l, :, at_s(S * RB * i, RB)], a + RB * i, RB) for i in range(2 * M)]
        return [(w_fc2.at[l, at_s(0, RB), :], o_fc2.at[l, at_s(0, RB), :], a, D)]

    def own_load(l, j):
        for src, _, c0, n in own_parts(l, j, s):
            pltpu.make_async_copy(src, W.at[l, z, xx, :, c0:c0 + n], loc_sem.at[l, j]).start()

    def own_wait(l, j):
        pltpu.make_async_copy(wslot(l, z, xx, j), wslot(l, z, xx, j), loc_sem.at[l, j]).wait()

    def ag_pair(p, zz, xp):
        if p == 0:
            return PS.at[zz, xp]
        l, j = divmod(p - 1, 4)
        return wslot(l, zz, xp, j)

    def ag_own(p):
        return ag_pair(p, z, xx)

    def ag_z(p, k):
        return rcopy(ag_own(p), ag_pair(p, z, xx), agz_s.at[p, k], agz_r.at[p, z], zdev[k])

    def ag_z_recv(p, k):
        zz = zfrom[k]
        return rcopy(ag_own(p), ag_pair(p, zz, xx), agz_s.at[p, k], agz_r.at[p, zz], zdev[k])

    def ag_x(p, zz, own):
        src = ag_own(p) if own else ag_pair(p, zz, xx)
        return rcopy(src, ag_pair(p, zz, xx), agx_s.at[p, zz], agx_r.at[p, zz], xdev)

    def ag_x_recv(p, zz):
        return rcopy(ag_own(p), ag_pair(p, zz, 1 - xx), agx_s.at[p, zz], agx_r.at[p, zz], xdev)

    def ag_issue(p):
        if p > 0:
            own_wait(*divmod(p - 1, 4))
        for k in range(1, M):
            ag_z(p, k).start()
        ag_x(p, z, True).start()

    NP = 1 + 4 * L
    queue = [(p, k) for p in range(NP) for k in range(1, M)]
    state = {"next": 0, "issued": 0}

    def ag_issue_to(n):
        while state["issued"] < min(n, NP):
            ag_issue(state["issued"])
            state["issued"] += 1

    def ag_service(n):
        for _ in range(n):
            if state["next"] == len(queue):
                return
            p, k = queue[state["next"]]
            ag_issue_to(p + 1)
            ag_z_recv(p, k).wait_recv()
            ag_x(p, zfrom[k], False).start()
            state["next"] += 1
            if k == M - 1:
                ag_issue_to(p + 1 + cfg["ahead"])

    def ag_finish(p):
        while state["next"] < (p + 1) * (M - 1):
            ag_service(1)
        for k in range(M):
            ag_x_recv(p, zfrom[k]).wait_recv()

    def ag_drain(first, last):
        for p in range(first, last):
            for k in range(1, M):
                ag_z(p, k).wait_send()
            for k in range(M):
                ag_x(p, zof[k], k == 0).wait_send()

    for l in range(L):
        for j in range(4):
            own_load(l, j)
    for l in range(L):
        PS[z, xx, 12 * l:12 * l + 2, :] = gains_ref[l].astype(F32)
        PS[z, xx, 12 * l + 2:12 * l + 8, :] = biases_ref[l].astype(F32)
        for i in range(S):
            PS[z, xx, 12 * l + 8 + i:12 * l + 9 + i, :] = bfc_ref[l:l + 1, RB * i:RB * i + RB].astype(F32)
    row = mask_ref[...].astype(F32)
    MK[s] = jnp.zeros_like(MK[s])
    MK[s, 0:1, 0:T] = row
    ag_issue_to(1)
    mks = [rcopy(MK.at[s], MK.at[s], mk_s.at[i], mk_r.at[i], dev) for i, dev in enumerate((core, ydev, diag))]
    for c in mks:
        c.start()
    ag_issue_to(1 + cfg["ahead"])
    diagonal = lax.broadcasted_iota(jnp.int32, (T, T), 0) == lax.broadcasted_iota(jnp.int32, (T, T), 1)
    TV[...] = jnp.zeros_like(TV)
    TV[0:T, :] = jnp.broadcast_to(
        jnp.sum(jnp.where(diagonal, row, 0.0), axis=1, keepdims=True) * valid_ref[0].astype(F32), (T, 128))
    H[0] = jnp.zeros((TP, D), F32)
    H[0, 0:T, :] = x_ref[...].astype(F32)
    SGF[...] = jnp.zeros_like(SGF)
    SG[...] = jnp.zeros_like(SG)
    STAT[...] = jnp.zeros_like(STAT)
    for i, c in enumerate(mks):
        c.wait_send()
        rcopy(MK.at[s], MK.at[(core, ydev, diag)[i][1]], mk_s.at[i], mk_r.at[i], (core, ydev, diag)[i]).wait_recv()
    MR[...] = jnp.concatenate([MK[i, :, 0:TP] for i in range(S)], axis=1)
    ag_finish(0)
    for i in range(M):
        for j in range(2):
            PR[:, 128 * (2 * i + j):128 * (2 * i + j) + 128] = PS[i, j]

    DH[...] = jnp.zeros_like(DH)
    DH[0:T, :] = cot_ref[...].astype(F32) * TV[0:T, 0:1]

    def prow(l, i):
        return PR[12 * l + i:12 * l + i + 1, :]

    def prow_cols(l, i):
        return PR[12 * l + i:12 * l + i + 1, pl.ds(pl.multiple_of(C * s, C), C)]

    HB = TP // 2

    def ge_part(e, buf, i, h):
        rows = pl.ds(h * HB, HB)
        if i == 0:
            return rcopy(buf.at[s, rows], buf.at[s, rows], ge_s.at[e, 0, h], ge_r.at[e, 0, h], core)
        if i == 1:
            return rcopy(buf.at[s, rows], buf.at[s, rows], ge_s.at[e, 1, h], ge_r.at[e, 1, h], ydev)
        return rcopy(buf.at[ydev[1], rows], buf.at[ydev[1], rows], ge_s.at[e, 2, h], ge_r.at[e, 2, h], core)

    def ge_start(e, buf):
        for h in range(2):
            ge_part(e, buf, 1, h).start()
        for h in range(2):
            ge_part(e, buf, 0, h).start()

    def ge_end(e, buf):
        for h in range(2):
            rcopy(buf.at[s, pl.ds(h * HB, HB)], buf.at[ydev[1], pl.ds(h * HB, HB)],
                  ge_s.at[e, 1, h], ge_r.at[e, 1, h], ydev).wait_recv()
            ge_part(e, buf, 2, h).start()
        for h in range(2):
            rcopy(buf.at[s, pl.ds(h * HB, HB)], buf.at[core[1], pl.ds(h * HB, HB)],
                  ge_s.at[e, 0, h], ge_r.at[e, 0, h], core).wait_recv()
        for h in range(2):
            rcopy(buf.at[ydev[1], pl.ds(h * HB, HB)], buf.at[diag[1], pl.ds(h * HB, HB)],
                  ge_s.at[e, 2, h], ge_r.at[e, 2, h], core).wait_recv()
        for i in range(3):
            for h in range(2):
                ge_part(e, buf, i, h).wait_send()

    def re_copy(e, i):
        b = e % 2
        if i == 0:
            return rcopy(PB.at[b, 1 - ypos, 1 - cpos], R0.at[b], re_s.at[e, 0], re_r.at[e, 0], core)
        if i == 1:
            return rcopy(PB.at[b, 1 - ypos, cpos], R1.at[b], re_s.at[e, 1], re_r.at[e, 1], ydev)
        return rcopy(PB.at[b, ypos, 1 - cpos], R2.at[b], re_s.at[e, 2], re_r.at[e, 2], core)

    def re_run(e, partial):
        b = e % 2
        partial(1 - ypos, b)
        re_copy(e, 0).start()
        re_copy(e, 0).wait_recv()

        def add(i, _):
            rows = pl.ds(pl.multiple_of(i * 16, 16), 16)
            PB[b, 1 - ypos, cpos, rows, :] = (PB[b, 1 - ypos, cpos, rows, :].astype(F32) + R0[b, rows, :].astype(F32)).astype(BF16)
            return 0
        lax.fori_loop(0, TP // 16, add, 0)
        re_copy(e, 1).start()
        partial(ypos, b)
        re_copy(e, 2).start()

    def re_end(e):
        for i in (2, 1):
            re_copy(e, i).wait_recv()
        for i in range(3):
            re_copy(e, i).wait_send()

    def re_rows(e, rows):
        b = e % 2
        return (PB[b, ypos, cpos, rows, :].astype(F32) + R2[b, rows, :].astype(F32)) + R1[b, rows, :].astype(F32)

    def partial_of(lhs, rhs, cb):
        def run(chip, b):
            def tile(j, _):
                cols = pl.ds(pl.multiple_of(j * C, C), C)
                r = ddot(lhs(chip), rhs(j), 1, cb).astype(BF16)
                PB[b, chip, :, :, cols] = r.reshape(2, TP, C)
                return 0
            lax.fori_loop(0, S, tile, 0)
        return run

    def row_loop(body, init):
        def one(i, carry):
            return body(pl.ds(pl.multiple_of(i * 16, 16), 16), carry)
        return lax.fori_loop(0, TP // 16, one, init)

    def norm(v):
        center = v - jnp.mean(v, -1, keepdims=True)
        inverse = lax.rsqrt(jnp.mean(center * center, -1, keepdims=True) + epsilon)
        return center * inverse, inverse

    def fold(v):
        return v[0:8] + v[8:16]

    def col_sum(v):
        return jnp.sum(v, axis=0, keepdims=True)

    lane_low = lax.broadcasted_iota(jnp.int32, (1, 2 * HEAD_DIM), 1) < HEAD_DIM
    lane_idx = lax.broadcasted_iota(jnp.int32, (1, 128), 1)

    def attend(l, pair):
        def block(i, _):
            rows = pl.ds(pl.multiple_of(i * TP, 16), TP)
            q = QKV[l, rows, 128 * pair:128 * pair + 128]
            k = QKV[l, :, C + 128 * pair:C + 128 * pair + 128]
            v = QKV[l, :, 2 * C + 128 * pair:2 * C + 128 * pair + 128]
            outs, lses = [], []
            for h in range(2):
                keep = lane_low if h == 0 else jnp.logical_not(lane_low)
                qh = jnp.where(keep, q, jnp.zeros_like(q))
                sc = ddot(qh, k, 1, 1) * SCALE
                sc = jnp.where(MR[0:1, :] > 0, sc, NEG)
                mx = jnp.max(sc, -1, keepdims=True)
                ex = jnp.exp(sc - mx)
                tot = jnp.sum(ex, -1, keepdims=True)
                outs.append(ddot(ex.astype(BF16), v, 1, 0) / tot)
                lses.append(mx + jnp.log(tot))
            OB[l, rows, 128 * pair:128 * pair + 128] = jnp.where(lane_low, outs[0], outs[1]).astype(BF16)
            held = jnp.where(lane_idx == 2 * pair, lses[0], lses[1])
            LSE[l, rows, :] = held if pair == 0 else jnp.where(lane_idx < 2 * pair, LSE[l, rows, :], held)
            return 0
        lax.fori_loop(0, S, block, 0)

    def attend_back(l, pair):
        DKV[...] = jnp.zeros_like(DKV)

        def block(i, _):
            rows = pl.ds(pl.multiple_of(i * TP, 16), TP)
            q = QKV[l, rows, 128 * pair:128 * pair + 128]
            k = QKV[l, :, C + 128 * pair:C + 128 * pair + 128]
            v = QKV[l, :, 2 * C + 128 * pair:2 * C + 128 * pair + 128]
            do = DO[rows, 128 * pair:128 * pair + 128]
            lse = LSE[l, rows, :]
            dqs = []
            dk = dv = None
            for h in range(2):
                keep = lane_low if h == 0 else jnp.logical_not(lane_low)
                qh = jnp.where(keep, q, jnp.zeros_like(q))
                doh = jnp.where(keep, do, jnp.zeros_like(do))
                sc = ddot(qh, k, 1, 1) * SCALE
                sc = jnp.where(MR[0:1, :] > 0, sc, NEG)
                p = jnp.exp(sc - lse[:, 2 * pair + h:2 * pair + h + 1])
                dp = ddot(doh, v, 1, 1)
                inner = jnp.sum(p * dp, -1, keepdims=True)
                ds = (p * (dp - inner)).astype(BF16)
                dqs.append(ddot(ds, k, 1, 0))
                dkh = ddot(ds, qh, 0, 0)
                dvh = ddot(p.astype(BF16), doh, 0, 0)
                dk = dkh if dk is None else dk + dkh
                dv = dvh if dv is None else dv + dvh
            DQKV[rows, 128 * pair:128 * pair + 128] = (jnp.where(lane_low, dqs[0], dqs[1]) * SCALE).astype(BF16)
            DKV[0] += dk
            DKV[1] += dv
            return 0
        lax.fori_loop(0, S, block, 0)
        DQKV[:, C + 128 * pair:C + 128 * pair + 128] = (DKV[0] * SCALE).astype(BF16)
        DQKV[:, 2 * C + 128 * pair:2 * C + 128 * pair + 128] = DKV[1].astype(BF16)

    peers = (core, ydev, diag)

    def wo_copy(l, i):
        to = peers[i][1]
        return rcopy(W.at[l, to, :, :, COLS[OUT]:COLS[FC1]], WO.at[l, :, :, pl.ds(pl.multiple_of(C * s, C), C)],
                     wo_s.at[l, i], wo_r.at[l, i], peers[i])

    def wo_start(l):
        for i in range(3):
            wo_copy(l, i).start()
        WO[l, :, :, pl.ds(pl.multiple_of(C * s, C), C)] = W[l, s, :, :, COLS[OUT]:COLS[FC1]]

    def wo_end(l):
        for i in range(3):
            wo_copy(l, i).wait()

    def gw_copy(l, i):
        to = peers[i][1]
        return rcopy(WO.at[l, :, :, pl.ds(pl.multiple_of(C * to, C), C)], W.at[l, s, :, :, COLS[OUT]:COLS[FC1]],
                     gw_s.at[l, i], gw_r.at[l, i], peers[i])

    def gw_start(l):
        for i in range(3):
            gw_copy(l, i).start()
        W[l, s, :, :, COLS[OUT]:COLS[FC1]] = WO[l, :, :, pl.ds(pl.multiple_of(C * s, C), C)]

    def gw_end(l):
        for i in range(3):
            gw_copy(l, i).wait()

    def wtile(l, j, a, b):
        n = M // S
        if n == 1:
            return W[l, j, :, :, a:b].reshape(2 * RB, b - a)
        return W[l, pl.ds(j * n, n), :, :, a:b].reshape(2 * RB * n, b - a)

    def grad_of(l, j):
        return GF if (l, j) == (L - 1, FC2) else W.at[l]

    def GC(l, j):
        return slice(0, D) if (l, j) == (L - 1, FC2) else slice(COLS[j], COLS[j + 1])

    def rx_copy(l, j, k):
        a, b = COLS[j], COLS[j + 1]
        return rcopy(grad_of(l, j).at[zof[k], 1 - xx, :, GC(l, j)], XR.at[l, zof[k], :, a:b], rx_s.at[l, j, k], rx_r.at[l, j, k], xdev)

    def rz_copy(l, j, k):
        a, b = COLS[j], COLS[j + 1]
        return rcopy(XR.at[l, zof[k], :, a:b], ZR.at[l, k - 1, :, a:b], rz_s.at[l, j, k], rz_r.at[l, j, k], zdev[k])

    def rz_recv(l, j, k):
        a, b = COLS[j], COLS[j + 1]
        return rcopy(XR.at[l, zof[k], :, a:b], ZR.at[l, k - 1, :, a:b], rz_s.at[l, j, k], rz_r.at[l, j, k], zdev[k])

    def whole_of(l, j):
        return FIN.at[l, :, COLS[j]:COLS[j + 1]]

    def fo_start(l, j):
        for _, dst, c0, n in own_parts(l, j, s):
            src = FIN.at[l, :, c0:c0 + n]
            for i in range(2):
                rcopy(src, dst, fo_s.at[l, j, i], fo_r.at[l, j, i], peers[i]).start()
            pltpu.make_async_copy(src, dst, loc_sem.at[l, j]).start()

    def fo_pass(l, j):
        rcopy(whole_of(l, j), whole_of(l, j), fo_s.at[l, j, 1], fo_r.at[l, j, 1], peers[1]).wait_recv()
        for _, dst, c0, n in own_parts(l, j, ydev[1]):
            rcopy(dst, dst, fo_s.at[l, j, 2], fo_r.at[l, j, 2], core).start()

    def fo_wait(l, j):
        for i in range(3):
            c = rcopy(whole_of(l, j), whole_of(l, j), fo_s.at[l, j, i], fo_r.at[l, j, i], peers[i])
            c.wait_send()
            if i != 1:
                c.wait_recv()
        pltpu.make_async_copy(whole_of(l, j), whole_of(l, j), loc_sem.at[l, j]).wait()

    def red_first(l, j, k):
        a, b = COLS[j], COLS[j + 1]
        rx_copy(l, j, k).wait_recv()
        zz = zof[k]
        if k == 0:
            return
        for r0 in range(0, RB, 32):
            XR[l, zz, r0:r0 + 32, a:b] = (XR[l, zz, r0:r0 + 32, a:b].astype(F32) + grad_of(l, j)[zz, xx, r0:r0 + 32, GC(l, j)].astype(F32)).astype(BF16)
        rz_copy(l, j, k).start()

    def red_second(l, j):
        a, b = COLS[j], COLS[j + 1]
        red_first(l, j, 0)
        for k in range(1, M):
            rz_recv(l, j, k).wait_recv()
        for r0 in range(0, RB, 32):
            t = XR[l, z, r0:r0 + 32, a:b].astype(F32) + grad_of(l, j)[z, xx, r0:r0 + 32, GC(l, j)].astype(F32)
            for k in range(1, M):
                t = t + ZR[l, k - 1, r0:r0 + 32, a:b].astype(F32)
            FIN[l, r0:r0 + 32, a:b] = t.astype(BF16)
        fo_start(l, j)

    def red_end(l, j):
        for k in range(M):
            rx_copy(l, j, k).wait_send()
        for k in range(1, M):
            rz_copy(l, j, k).wait_send()
        fo_wait(l, j)

    events = []
    later = []
    done = {"n": 0}

    def red_later():
        if len(later) > 1:
            events.append((fo_pass,) + later.pop(0))
        if later:
            events.append((red_second,) + later[-1])

    def red_push(l, j):
        for k in list(range(1, M)) + [0]:
            rx_copy(l, j, k).start()
        events.extend((red_first, l, j, k) for k in range(1, M))
        red_later()
        later.append((l, j))

    def red_service(n):
        for _ in range(n):
            if done["n"] >= len(events):
                return
            f, *a = events[done["n"]]
            done["n"] += 1
            f(*a)

    def norm_back(l, src, e, gain):
        def one(rows, acc):
            n, r = norm(src[l, rows, :])
            dm = re_rows(e, rows)
            dn = dm * gain
            pm = jnp.mean(dn, -1, keepdims=True)
            cm = jnp.mean(dn * n, -1, keepdims=True)
            DH[rows, :] = DH[rows, :] + r * (dn - pm - n * cm)
            return acc[0] + fold(dm * n), acc[1] + fold(dm)
        zero = jnp.zeros((8, D), F32)
        g, b = row_loop(one, (zero, zero))
        return col_sum(g), col_sum(b)

    def low_of(buf):
        def one(rows, acc):
            v = DH[rows, :].astype(BF16)
            buf[s, rows, :] = v
            return acc + fold(v.astype(F32))
        return col_sum(row_loop(one, jnp.zeros((8, D), F32)))

    def forward(l):
        e = 2 * l

        def ln1(rows, _):
            n, _r = norm(H[l, rows, :])
            AF[l, s, rows, :] = (n * prow(l, 0) + prow(l, 2)).astype(BF16)
            return 0
        row_loop(ln1, 0)
        ge_start(e, AF.at[l])
        ag_service(3)
        ge_end(e, AF.at[l])
        ag_finish(1 + 4 * l + QK)
        for n in range(3):
            r = ddot(AF[l].reshape(R, D), W[l, :, :, :, C * n:C * n + C].reshape(D, C), 1, 0)
            if n == 0:
                r = r + prow_cols(l, 3)
            if n == 2:
                r = r + prow_cols(l, 4)
            QKV[l, :, C * n:C * n + C] = r.astype(BF16)
        ag_finish(1 + 4 * l + OUT)
        wo_start(l)
        if l == 0:
            SGF[12 * (L - 1) + 7:12 * (L - 1) + 8, :] = low_of(BF.at[0])
            ge_start(2 * L, BF.at[0])
        attend(l, 0)
        ag_service(1)
        attend(l, 1)
        ag_service(1)
        if l == 0:
            ge_end(2 * L, BF.at[0])
        wo_end(l)
        re_run(e + 0, partial_of(
            lambda chip: OB[l, pl.ds(pl.multiple_of(chip * 2 * TP, 16), 2 * TP), :],
            lambda j: WO[l, :, :, pl.ds(pl.multiple_of(j * C, C), C)].reshape(C, C), 0))
        ag_service(1)
        re_end(e + 0)

        def post(rows, acc):
            hv = H[l, rows, :]
            br = re_rows(e + 0, rows) + prow(l, 5)
            mid = hv + br
            H2[l, rows, :] = mid
            n, _r = norm(mid)
            MF[l, s, rows, :] = (n * prow(l, 1) + prow(l, 6)).astype(BF16)
            t = TV[rows, 0:1]
            return acc[0] + fold(t * hv * hv), acc[1] + fold(t * br * br)
        zero = jnp.zeros((8, D), F32)
        s0, s1 = row_loop(post, (zero, zero))
        ge_start(e + 1, MF.at[l])
        ag_service(2)
        ge_end(e + 1, MF.at[l])
        ag_finish(1 + 4 * l + FC1)
        bias = PR[pl.ds(12 * l + 8 + s, 1), :]
        for j in range(FS // C):
            u = ddot(MF[l].reshape(R, D), W[l, :, :, :, COLS[FC1] + C * j:COLS[FC1] + C * j + C].reshape(D, C), 1, 0)
            u = u + bias[:, C * j:C * j + C]
            U[l, :, C * j:C * j + C] = u
            GW[:, C * j:C * j + C] = (u / (1.0 + jnp.exp(-1.702 * u))).astype(BF16)
        stat(3 * l, s0)
        stat(3 * l + 1, s1)
        if l == L - 1:
            for j in range(FS // C):
                GF[j, :, :, :] = ddot(GW[:, C * j:C * j + C], BF[0].reshape(R, D), 0, 0).astype(BF16).reshape(2, RB, D)
        ag_finish(1 + 4 * l + FC2)
        if l == L - 1:
            red_push(l, FC2)
        re_run(e + 1, partial_of(
            lambda chip: GW[pl.ds(pl.multiple_of(chip * 2 * TP, 16), 2 * TP), :],
            lambda j: W[l, :, :, :, pl.ds(pl.multiple_of(COLS[FC2] + j * C, C), C)].reshape(FS, C), 0))

    def forward_end(l):
        e = 2 * l

        def last(rows, acc):
            out = re_rows(e + 1, rows) + prow(l, 7)
            res = H2[l, rows, :] + out
            H[l + 1, rows, :] = res
            t = TV[rows, 0:1]
            return acc + fold(t * out * out)
        re_end(e + 1)
        stat(3 * l + 2, row_loop(last, jnp.zeros((8, D), F32)))

    def stat(i, v):
        STAT[...] = jnp.where(lane_idx == i, jnp.sum(col_sum(v), axis=1, keepdims=True), STAT[...])

    def backward(l):
        ge_a = re_a = 2 * L + 2 * (L - 1 - l)
        ge_b = re_b = ge_a + 1
        B0, B1 = BF.at[0], BF.at[1]
        svc = cfg["svc"][L - 1 - l]
        if l < L - 1:
            SGF[12 * l + 7:12 * l + 8, :] = low_of(B0)
            ge_start(ge_a, B0)
            red_service(svc[0])
            ge_end(ge_a, B0)
        for j in range(FS // C):
            dg = ddot(BF[0].reshape(R, D), wtile(l, j, COLS[FC2], COLS[FC2] + D), 1, 1)
            u = U[l, :, C * j:C * j + C]
            sg = 1.0 / (1.0 + jnp.exp(-1.702 * u))
            if l < L - 1:
                GW[:, C * j:C * j + C] = (u * sg).astype(BF16)
            du = (dg * (sg + 1.702 * u * sg * (1.0 - sg))).astype(BF16)
            DU[:, C * j:C * j + C] = du
            SGF[pl.ds(12 * l + 8 + s, 1), C * j:C * j + C] = jnp.sum(du.astype(F32), axis=0, keepdims=True)
        red_service(svc[1])
        if l < L - 1:
            for j in range(FS // C):
                W[l, j, :, :, COLS[FC2]:COLS[FC2] + D] = ddot(GW[:, C * j:C * j + C], BF[0].reshape(R, D), 0, 0).astype(BF16).reshape(2, RB, D)
            red_push(l, FC2)
        re_run(re_a, partial_of(
            lambda chip: DU[pl.ds(pl.multiple_of(chip * 2 * TP, 16), 2 * TP), :],
            lambda j: wtile(l, j, COLS[FC1], COLS[FC1] + FS), 1))
        for j in range(S):
            W[l, j, :, :, COLS[FC1]:COLS[FC1] + FS] = ddot(MF[l, :, :, C * j:C * j + C].reshape(R, C), DU[...], 0, 0).astype(BF16).reshape(2, RB, FS)
        red_push(l, FC1)
        if l == L - 1:
            forward_end(l)
        red_service(svc[2])
        re_end(re_a)
        gg, bb = norm_back(l, H2, re_a, prow(l, 1))
        SGF[12 * l + 1:12 * l + 2, :] = gg
        SGF[12 * l + 6:12 * l + 7, :] = bb
        SGF[12 * l + 5:12 * l + 6, :] = low_of(B1)
        ge_start(ge_b, B1)
        red_service(svc[3])
        ge_end(ge_b, B1)
        DO[...] = ddot(BF[1].reshape(R, D), WO[l].reshape(C, D), 1, 1).astype(BF16)
        for j in range(S):
            WO[l, :, :, C * j:C * j + C] = ddot(OB[l], BF[1, :, :, C * j:C * j + C].reshape(R, C), 0, 0).astype(BF16).reshape(2, RB, C)
        gw_start(l)
        attend_back(l, 0)
        red_service(svc[4])
        attend_back(l, 1)
        gw_end(l)
        red_push(l, OUT)
        red_service(svc[5])
        for i, (row, c0) in enumerate(((3, 0), (4, 2 * C))):
            SGF[12 * l + row:12 * l + row + 1, pl.ds(pl.multiple_of(C * s, C), C)] = jnp.sum(
                DQKV[:, c0:c0 + C].astype(F32), axis=0, keepdims=True)
        re_run(re_b, partial_of(
            lambda chip: DQKV[pl.ds(pl.multiple_of(chip * 2 * TP, 16), 2 * TP), :],
            lambda j: wtile(l, j, 0, 3 * C), 1))
        for j in range(S):
            W[l, j, :, :, 0:3 * C] = ddot(AF[l, :, :, C * j:C * j + C].reshape(R, C), DQKV[...], 0, 0).astype(BF16).reshape(2, RB, 3 * C)
        red_push(l, QK)
        red_service(svc[6])
        re_end(re_b)
        gg, bb = norm_back(l, H, re_b, prow(l, 0))
        SGF[12 * l + 0:12 * l + 1, :] = gg
        SGF[12 * l + 2:12 * l + 3, :] = bb
        red_service(svc[7])

    for l in range(L):
        forward(l)
        if l < L - 1:
            forward_end(l)
    ag_drain(0, NP - 1)
    for l in reversed(range(L)):
        backward(l)
    gx_ref[...] = DH[0:T, :]
    y_ref[...] = H[L, 0:T, :].astype(BF16)
    STAT[...] = jnp.where(lane_idx == 3 * L, col_sum(TV[:, 0:1]), STAT[...])

    for i in range(M):
        for j in range(2):
            SG[i, j, 0:24, :] = SGF[0:24, 128 * (2 * i + j):128 * (2 * i + j) + 128]
            SG[i, j, 24:25, :] = STAT[...]
    sgx = rcopy(SG.at[:, 1 - xx], SX, st_s.at[0], st_r.at[0], xdev)
    sgx.start()

    def sz(k, frm):
        return rcopy(SX.at[zof[k]], SZ.at[zfrom[k] if frm else z], st_s.at[k], st_r.at[k], zdev[k])

    def stc(i, frm):
        slot = peers[i][1] if frm else s
        return rcopy(ST.at[s], ST.at[slot], st_s.at[M + i], st_r.at[M + i], peers[i])

    red_service(len(events))
    sgx.wait()
    SX[...] = SX[...] + SG[:, xx]
    SZ[z] = SX[z]
    for k in range(1, M):
        sz(k, False).start()
    red_later()
    red_service(len(events))
    for k in range(1, M):
        sz(k, True).wait_recv()
    tot = SZ[0]
    for k in range(1, M):
        tot = tot + SZ[k]
    ST[s] = tot
    for i in range(3):
        stc(i, False).start()
    for p in later:
        fo_pass(*p)
    for i in range(3):
        stc(i, True).wait_recv()
    tot = (ST[0] + ST[1]) + (ST[2] + ST[3])
    for l in range(L):
        ogain_ref[l] = tot[12 * l:12 * l + 2]
        obias_ref[l, 0:1, :] = tot[12 * l + 2:12 * l + 3]
        obias_ref[l, 1:5, :] = tot[12 * l + 4:12 * l + 8]
        oquery_ref[l:l + 1, :] = tot[12 * l + 3:12 * l + 4]
        for i in range(S):
            obfc_ref[l:l + 1, RB * i:RB * i + RB] = tot[12 * l + 8 + i:12 * l + 9 + i]
    sums = tot[12 * L:12 * L + 1]
    root = jnp.sqrt(sums / (jnp.maximum(sums[:, 3 * L:3 * L + 1], 1.0) * D))
    for l in range(L):
        rms_ref[l:l + 1, :] = root[:, 3 * l:3 * l + 3]
    for k in range(1, M):
        sz(k, False).wait_send()
    for i in range(3):
        stc(i, False).wait_send()
    ag_drain(NP - 1, NP)
    for l in reversed(range(L)):
        for j in (FC2, FC1, OUT, QK):
            red_end(l, j)


def fused_local(cfg, block_input, key_mask, valid, gains, biases, w_qkv, w_out, w_fc1, b_fc1, w_fc2, cotangent):
    L, M, RB, T, TP, D, NC, FS = (cfg[n] for n in ("L", "M", "RB", "T", "TP", "D", "NC", "FS"))
    S, dp = 4, 2 * M
    C = D // S
    R = S * TP
    vm = pl.BlockSpec(memory_space=pltpu.VMEM)
    hbm = pl.BlockSpec(memory_space=pl.ANY)
    dma = pltpu.SemaphoreType.DMA
    v = pltpu.VMEM
    NP, NE = 1 + 4 * L, 4 * L
    out = pl.pallas_call(
        partial(fused_kernel, cfg),
        out_shape=(
            jax.ShapeDtypeStruct((T, D), BF16),
            jax.ShapeDtypeStruct((T, D), F32),
            jax.ShapeDtypeStruct((L, 3), F32),
            jax.ShapeDtypeStruct((L, 2, RB), F32),
            jax.ShapeDtypeStruct((L, 5, RB), F32),
            jax.ShapeDtypeStruct((L, RB), F32),
            jax.ShapeDtypeStruct((L, S * RB), F32),
            jax.ShapeDtypeStruct(w_qkv.shape, BF16),
            jax.ShapeDtypeStruct(w_out.shape, BF16),
            jax.ShapeDtypeStruct(w_fc1.shape, BF16),
            jax.ShapeDtypeStruct(w_fc2.shape, BF16),
        ),
        in_specs=[vm, vm, pl.BlockSpec(memory_space=pltpu.SMEM), vm, vm, vm, vm, hbm, hbm, hbm, hbm],
        out_specs=(vm,) * 7 + (hbm,) * 4,
        scratch_shapes=[
            v((L, M, 2, RB, NC), BF16),
            v((L, 2, RB, D), BF16),
            v((L, M, RB, NC), BF16),
            v((L, M - 1, RB, NC), BF16),
            v((L, S, TP, D), BF16),
            v((L, R, 3 * C), BF16),
            v((L, R, C), BF16),
            v((L, S, TP, D), BF16),
            v((L, R, FS), F32),
            v((L + 1, TP, D), F32),
            v((L, TP, D), F32),
            v((L, R, 128), F32),
            v((M, 2, RB, D), BF16),
            v((2, S, TP, D), BF16),
            v((2, 2, 2, TP, D), BF16),
            v((2, TP, D), BF16),
            v((2, TP, D), BF16),
            v((2, TP, D), BF16),
            v((R, FS), BF16),
            v((R, FS), BF16),
            v((R, 3 * C), BF16),
            v((R, C), BF16),
            v((2, R, 128), F32),
            v((TP, D), F32),
            v((S, 8, -(-TP // 128) * 128), F32),
            v((8, R), F32),
            v((TP, 128), F32),
            v((M, 2, 12 * L, RB), F32),
            v((12 * L, D), F32),
            v((12 * L, D), F32),
            v((M, 2, 32, RB), F32),
            v((M, 32, RB), F32),
            v((M, 32, RB), F32),
            v((S, 32, RB), F32),
            v((L, RB, NC), BF16),
            v((1, RB), F32),
            dma((L, 4)),
            dma((NP, M)), dma((NP, M)), dma((NP, M)), dma((NP, M)),
            dma((NE, 3, 2)), dma((NE, 3, 2)), dma((NE, 3)), dma((NE, 3)),
            dma((L, 3)), dma((L, 3)), dma((L, 3)), dma((L, 3)),
            dma((L, 4, M)), dma((L, 4, M)), dma((L, 4, M)), dma((L, 4, M)),
            dma((L, 4, 3)), dma((L, 4, 3)), dma((3,)), dma((3,)), dma((M + 3,)), dma((M + 3,)),
        ],
        compiler_params=pltpu.CompilerParams(
            collective_id=0, has_side_effects=True, vmem_limit_bytes=cfg["vmem"]),
        cost_estimate=pl.CostEstimate(flops=24_000_000_000, bytes_accessed=20_000_000, transcendentals=0),
    )(block_input[0], key_mask, valid, gains, biases, b_fc1, cotangent[0], w_qkv, w_out, w_fc1, w_fc2)
    y, gx, rms, o_gain, o_bias, o_query, o_bfc, o_qkv, o_out, o_fc1, o_fc2 = out
    return (y[None], gx[None], rms, o_gain, o_bias, o_query,
            o_qkv.astype(F32), o_out.astype(F32), o_fc1.astype(F32), o_bfc, o_fc2.astype(F32))


def local(*args):
    block_input, w_qkv, w_fc2 = args[0], args[5], args[9]
    L, RB = w_qkv.shape[:2]
    T, D = block_input.shape[1:]
    S, dp = lax.axis_size("seq"), lax.axis_size("dp")
    FS = w_fc2.shape[1] * dp // S
    fits = (S == 4 and dp == 2 * S and RB % 128 == 0 and D // S == 2 * RB and L * 12 + 1 <= 32
            and FS // dp == RB and HEAD_DIM * 2 == 128 and D // S == 4 * HEAD_DIM and block_input.shape[0] == 1)
    if not fits:
        return plain_local(*args)
    cfg = dict(L=L, M=dp // 2, RB=RB, T=T, TP=-(-T // 16) * 16, D=D, NC=D + 2 * FS, FS=FS, ahead=2, vmem=62 * 2**20,
               svc=((0, 0, 2, 1, 0, 1, 2, 0),) + ((8, 3, 2, 3, 1, 1, 3, 0),) * (L - 1))
    return fused_local(cfg, *args)


def solution(mesh):
    return jax.shard_map(
        local,
        mesh=mesh,
        in_specs=(
            P("dp", "seq", None),
            P("dp", "seq"),
            P("dp"),
            P(None, None, "dp"),
            P(None, None, "dp"),
            P(None, "dp", None),
            P(None, "dp", None),
            P(None, "dp", None),
            P(None, "dp"),
            P(None, "dp", None),
            P("dp", "seq", None),
        ),
        out_specs=(
            P("dp", "seq", None),
            P("dp", "seq", None),
            P(),
            P(None, None, "dp"),
            P(None, None, "dp"),
            P(None, "dp"),
            P(None, "dp", None),
            P(None, "dp", None),
            P(None, "dp", None),
            P(None, "dp"),
            P(None, "dp", None),
        ),
        check_vma=False,
    )
```

```python
from functools import partial
import math

import jax
import jax.numpy as jnp
from jax import lax
from jax.experimental import pallas as pl
from jax.experimental.pallas import tpu as pltpu
from jax.sharding import PartitionSpec as P

HEADS = 16
HEAD_DIM = 64
F32 = jnp.float32
BF16 = jnp.bfloat16

epsilon = 1e-05


def norm_parts(values_in, gain, shift):
    center = values_in - jnp.mean(values_in, -1, keepdims=True)
    inverse = lax.rsqrt(jnp.mean(center * center, -1, keepdims=True) + epsilon)
    normal = center * inverse
    return (normal * gain + shift, normal, inverse)


def norm_back(grad_output, normal, inverse, gain):
    grad_gain = jnp.sum(grad_output * normal, 0)
    grad_shift = jnp.sum(grad_output, 0)
    grad_norm = grad_output * gain
    plain_mean = jnp.mean(grad_norm, -1, keepdims=True)
    cross_mean = jnp.mean(grad_norm * normal, -1, keepdims=True)
    return (grad_gain, grad_shift, inverse * (grad_norm - plain_mean - normal * cross_mean))


def dot(a, b, ca=1, cb=0):
    return lax.dot_general(a, b, (((ca,), (cb,)), ((), ())), preferred_element_type=F32)


def split_heads(x, width):
    return x.reshape(x.shape[0], width // HEAD_DIM, HEAD_DIM)


def scores_of(query, keys, mask_row, scale):
    scores = jnp.einsum("qhd,khd->hqk", query, keys, preferred_element_type=F32) * scale
    return jnp.where(mask_row[None, None, :] > 0, scores, -1000000000.0)


def gather_rows(x):
    return lax.all_gather(x, "seq", axis=0, tiled=True)


def scatter_rows(x):
    return lax.psum_scatter(x.astype(BF16), "seq", scatter_dimension=0, tiled=True).astype(F32)


def forward_layer(hidden, weights, params, mask_row, tok_valid):
    w_qkv, w_out, w_fc1, w_fc2 = weights
    gains, biases, bias_q, bias_v, b_fc1 = params
    scale = 1.0 / math.sqrt(HEAD_DIM)
    width = w_out.shape[0]
    normed, normal_one, inverse_one = norm_parts(hidden, gains[0], biases[0])
    normed_all = gather_rows(normed.astype(BF16))
    packed = dot(normed_all, w_qkv)
    packed = (packed + jnp.concatenate([bias_q, jnp.zeros_like(bias_q), bias_v])).astype(BF16)
    query, keys, values = (split_heads(packed[:, i * width : (i + 1) * width], width) for i in range(3))
    scores = scores_of(query, keys, mask_row, scale)
    row_max = jnp.max(scores, -1, keepdims=True)
    log_total = row_max + jnp.log(jnp.sum(jnp.exp(scores - row_max), -1, keepdims=True))
    probs = jnp.exp(scores - log_total).astype(BF16)
    mixed = jnp.einsum("hqk,khd->qhd", probs, values, preferred_element_type=F32).astype(BF16)
    mixed = mixed.reshape(mixed.shape[0], width)
    branch = scatter_rows(dot(mixed, w_out)) + biases[3]
    middle = hidden + branch
    normed_two, normal_two, inverse_two = norm_parts(middle, gains[1], biases[4])
    normed_two_all = gather_rows(normed_two.astype(BF16))
    inner = dot(normed_two_all, w_fc1) + b_fc1
    gate_sig = jax.nn.sigmoid(1.702 * inner)
    gated = (inner * gate_sig).astype(BF16)
    output = scatter_rows(dot(gated, w_fc2)) + biases[5]
    stat = jnp.stack([jnp.sum(tok_valid * jnp.sum(v * v, -1)) for v in (hidden, branch, output)])
    stored = (normal_one, inverse_one, normed_all, query, keys, values, log_total, mixed,
              normal_two, inverse_two, normed_two_all, inner, gate_sig, gated)
    return (middle + output, stored, stat)


def backward_layer(grad_result, weights, params, stored, mask_row):
    w_qkv, w_out, w_fc1, w_fc2 = weights
    gains = params[0]
    scale = 1.0 / math.sqrt(HEAD_DIM)
    (normal_one, inverse_one, normed_all, query, keys, values, log_total, mixed,
     normal_two, inverse_two, normed_two_all, inner, gate_sig, gated) = stored
    out_low = grad_result.astype(BF16)
    grad_bias_five = jnp.sum(out_low.astype(F32), 0)
    out_all = gather_rows(out_low)
    grad_fc2 = dot(gated, out_all, 0, 0)
    grad_gated = dot(out_all, w_fc2, 1, 1)
    grad_inner = (grad_gated * (gate_sig + 1.702 * inner * gate_sig * (1.0 - gate_sig))).astype(BF16)
    grad_bias_fc1 = jnp.sum(grad_inner.astype(F32), 0)
    grad_fc1 = dot(normed_two_all, grad_inner, 0, 0)
    grad_normed_two = scatter_rows(dot(grad_inner, w_fc1, 1, 1))
    grad_gain_two, grad_shift_two, grad_middle = norm_back(grad_normed_two, normal_two, inverse_two, gains[1])
    grad_middle = grad_middle + grad_result
    branch_low = grad_middle.astype(BF16)
    grad_bias_three = jnp.sum(branch_low.astype(F32), 0)
    branch_all = gather_rows(branch_low)
    grad_out = dot(mixed, branch_all, 0, 0)
    width = w_out.shape[0]
    grad_mixed = split_heads(dot(branch_all, w_out, 1, 1).astype(BF16), width)
    scores = scores_of(query, keys, mask_row, scale)
    probs = jnp.exp(scores - log_total)
    grad_probs = jnp.einsum("qhd,khd->hqk", grad_mixed, values, preferred_element_type=F32)
    inner_sum = jnp.sum(probs * grad_probs, -1, keepdims=True)
    grad_scores = (probs * (grad_probs - inner_sum)).astype(BF16)
    grad_q = (jnp.einsum("hqk,khd->qhd", grad_scores, keys, preferred_element_type=F32) * scale).astype(BF16)
    grad_k = (jnp.einsum("hqk,qhd->khd", grad_scores, query, preferred_element_type=F32) * scale).astype(BF16)
    grad_v = jnp.einsum("hqk,qhd->khd", probs.astype(BF16), grad_mixed, preferred_element_type=F32).astype(BF16)
    rows = grad_q.shape[0]
    grad_proj = jnp.concatenate([g.reshape(rows, width) for g in (grad_q, grad_k, grad_v)], 1)
    grad_bias_proj = jnp.sum(grad_proj.astype(F32), 0)
    grad_qkv = dot(normed_all, grad_proj, 0, 0)
    grad_normed = scatter_rows(dot(grad_proj, w_qkv, 1, 1))
    grad_gain_one, grad_shift_one, grad_hidden = norm_back(grad_normed, normal_one, inverse_one, gains[0])
    grad_hidden = grad_hidden + grad_middle
    rows_sum = jnp.stack([grad_gain_one, grad_gain_two, grad_shift_one, grad_bias_three, grad_shift_two, grad_bias_five])
    return (grad_hidden, (grad_qkv, grad_out, grad_fc1, grad_fc2), rows_sum, grad_bias_proj, grad_bias_fc1)


def plain_local(block_input, key_mask, valid, gains, biases, w_qkv, w_out, w_fc1, b_fc1, w_fc2, cotangent):
    layers = w_qkv.shape[0]
    groups = lax.axis_size("seq")
    shards = lax.axis_size("dp")
    me = lax.axis_index("seq")
    width = block_input.shape[2]
    hidden_width = w_fc2.shape[1] * shards
    part = width // groups
    images = block_input.shape[0]
    assert images == 1
    mask_row = lax.all_gather(key_mask, "seq", axis=1, tiled=True)[0]
    tok_valid = (key_mask * valid[:, None]).astype(F32)[0]
    hidden = block_input[0].astype(F32)
    small = jnp.concatenate([gains.reshape(layers, -1), biases.reshape(layers, -1), b_fc1], 1)
    small = lax.all_gather(small, "dp", axis=0).astype(F32)
    n_g, n_b = gains.shape[1] * gains.shape[2], biases.shape[1] * biases.shape[2]
    gains_all = small[:, :, :n_g].reshape(shards, layers, 2, -1).transpose(1, 2, 0, 3).reshape(layers, 2, width)
    biases_all = small[:, :, n_g : n_g + n_b].reshape(shards, layers, 6, -1).transpose(1, 2, 0, 3).reshape(layers, 6, width)
    fc_all = small[:, :, n_g + n_b :].transpose(1, 0, 2).reshape(layers, shards, groups, -1)
    fc_mine = lax.dynamic_index_in_dim(fc_all, me, 2, False).reshape(layers, -1)
    proj_mine = lax.dynamic_index_in_dim(biases_all.reshape(layers, 6, groups, part), me, 2, False)

    def columns(w, outer):
        view = w.reshape(w.shape[0], outer, groups, -1)
        return lax.dynamic_index_in_dim(view, me, 2, False).reshape(w.shape[0], -1)

    def rows_of(w):
        view = w.reshape(groups, -1, w.shape[1])
        return lax.dynamic_index_in_dim(view, me, 0, False)

    def gather(w):
        return lax.all_gather(w, "dp", axis=0, tiled=True)

    weights, params, stored_all, stats = [], [], [], []
    for layer in range(layers):
        weights.append((
            gather(columns(w_qkv[layer], 3)),
            rows_of(gather(w_out[layer])),
            gather(columns(w_fc1[layer], shards)),
            gather(rows_of(w_fc2[layer])),
        ))
        params.append((gains_all[layer], biases_all[layer], proj_mine[layer, 1], proj_mine[layer, 2], fc_mine[layer]))
    for layer in range(layers):
        hidden, stored, stat = forward_layer(hidden, weights[layer], params[layer], mask_row, tok_valid)
        stored_all.append(stored)
        stats.append(stat)
    totals = lax.psum(jnp.concatenate([jnp.stack(stats).reshape(-1), jnp.sum(tok_valid)[None]]), ("dp", "seq"))
    rms = jnp.sqrt(totals[:-1].reshape(layers, 3) / (jnp.maximum(totals[-1], 1.0) * width))

    grad_hidden = cotangent[0].astype(F32) * tok_valid[:, None]
    big = [None] * layers
    sums = [None] * layers
    for layer in reversed(range(layers)):
        grad_hidden, grads, rows_sum, grad_proj, grad_fc = backward_layer(
            grad_hidden, weights[layer], params[layer], stored_all[layer], mask_row
        )
        g_qkv, g_out, g_fc1, g_fc2 = (g.astype(BF16) for g in grads)
        g_out = lax.all_to_all(g_out, "seq", split_axis=1, concat_axis=0, tiled=True)

        def reduce_(g):
            g = lax.psum_scatter(g, "dp", scatter_dimension=0, tiled=True)
            return lax.all_gather(g, "seq", axis=0)

        def join(g, outer):
            view = g.reshape(groups, g.shape[1], outer, -1)
            return view.transpose(1, 2, 0, 3).reshape(g.shape[1], -1)

        big[layer] = (
            join(reduce_(g_qkv), 3).astype(F32),
            join(reduce_(g_out), 1).astype(F32),
            join(reduce_(g_fc1), shards).astype(F32),
            reduce_(g_fc2).reshape(w_fc2.shape[1], -1).astype(F32),
        )
        proj = lax.dynamic_update_slice(jnp.zeros((3, groups, part), F32), grad_proj.reshape(3, 1, part), (0, me, 0))
        fc = lax.dynamic_update_slice(jnp.zeros((shards, groups, hidden_width // (shards * groups)), F32),
                                      grad_fc.reshape(shards, 1, -1), (0, me, 0))
        sums[layer] = jnp.concatenate([
            rows_sum.reshape(6, shards, -1).transpose(1, 0, 2).reshape(shards, -1),
            proj.reshape(3, shards, -1).transpose(1, 0, 2).reshape(shards, -1),
            fc.reshape(shards, -1),
        ], 1)
    flat = jnp.stack(sums, 1).astype(F32)
    flat = lax.psum(lax.psum_scatter(flat, "dp", scatter_dimension=0, tiled=True)[0], "seq")
    per = width // shards
    rows9 = flat[:, : 9 * per].reshape(layers, 9, per)
    grad_bfc1 = flat[:, 9 * per :]
    stack = lambda i: jnp.stack([b[i] for b in big])
    bias_rest = jnp.concatenate([rows9[:, 2:3], rows9[:, 8:9], rows9[:, 3:6]], 1)
    return (
        hidden.astype(BF16)[None],
        grad_hidden[None],
        rms,
        rows9[:, :2],
        bias_rest,
        rows9[:, 6],
        stack(0),
        stack(1),
        stack(2),
        grad_bfc1,
        stack(3),
    )


MESH = pl.DeviceIdType.MESH
NEG = -1000000000.0


def ddot(a, b, ca, cb):
    return lax.dot_general(a, b, (((ca,), (cb,)), ((), ())), preferred_element_type=F32)


def fused_kernel(cfg, x_ref, mask_ref, valid_ref, gains_ref, biases_ref, bfc_ref, cot_ref, w_qkv, w_out, w_fc1, w_fc2,
                 y_ref, gx_ref, rms_ref, ogain_ref, obias_ref, oquery_ref, obfc_ref, o_qkv, o_out, o_fc1, o_fc2,
                 W, WO, XR, ZR, AF, QKV, OB, MF, U, H, H2, LSE,
                 GF, BF, PB, R0, R1, R2, DU, GW, DQKV, DO, DKV, DH, MK, MR, TV, PS, PR, SGF, SG, SX, SZ, ST, FIN, STAT,
                 loc_sem, agz_s, agz_r, agx_s, agx_r, agw_s, agw_r, ge_s, ge_r, re_s, re_r, wo_s, wo_r, gw_s, gw_r,
                 rx_s, rx_r, rz_s, rz_r, fo_s, fo_r, mk_s, mk_r, st_s, st_r):
    L, M, RB, T, TP, D, NC = cfg["L"], cfg["M"], cfg["RB"], cfg["T"], cfg["TP"], cfg["D"], cfg["NC"]
    S = 4
    R = S * TP
    C = D // S
    FS = cfg["FS"]
    SCALE = 1.0 / math.sqrt(HEAD_DIM)
    COLS = (0, 3 * C, 3 * C + C, 3 * C + C + FS, NC)
    QK, OUT, FC1, FC2 = range(4)
    d = lax.axis_index("dp")
    s = lax.axis_index("seq")
    z = d // 2
    xx = d % 2
    ypos = s // 2
    cpos = s % 2
    core = (d, s + 1 - 2 * cpos)
    ydev = (d, s + 2 - 4 * ypos)
    diag = (d, (s + 1 - 2 * cpos) + 2 - 4 * ypos)
    xdev = (d + 1 - 2 * xx, s)
    zof = [lax.rem(z + k, M) for k in range(M)]
    zdev = [(2 * zof[k] + xx, s) for k in range(M)]
    zfrom = [lax.rem(z + M - k, M) for k in range(M)]

    def rcopy(src, dst, ss, rs, dev):
        return pltpu.make_async_remote_copy(src_ref=src, dst_ref=dst, send_sem=ss, recv_sem=rs,
                                            device_id=dev, device_id_type=MESH)

    bar = pltpu.get_barrier_semaphore()
    for dev in [core, ydev, diag, xdev] + zdev[1:]:
        pl.semaphore_signal(bar, inc=1, device_id=dev, device_id_type=MESH)
    pl.semaphore_wait(bar, 3 + M)

    def wslot(l, zz, xp, j):
        return W.at[l, zz, xp, :, COLS[j]:COLS[j + 1]]

    def own_parts(l, j, s):
        a = COLS[j]

        def at_s(start, width):
            return pl.ds(pl.multiple_of(start + width * s, width), width)
        if j == QK:
            return [(w_qkv.at[l, :, at_s(D * i, C)], o_qkv.at[l, :, at_s(D * i, C)], a + C * i, C) for i in range(3)]
        if j == OUT:
            return [(w_out.at[l, :, at_s(0, C)], o_out.at[l, :, at_s(0, C)], a, C)]
        if j == FC1:
            return [(w_fc1.at[l, :, at_s(S * RB * i, RB)], o_fc1.at[l, :, at_s(S * RB * i, RB)], a + RB * i, RB) for i in range(2 * M)]
        return [(w_fc2.at[l, at_s(0, RB), :], o_fc2.at[l, at_s(0, RB), :], a, D)]

    def own_load(l, j):
        for src, _, c0, n in own_parts(l, j, s):
            pltpu.make_async_copy(src, W.at[l, z, xx, :, c0:c0 + n], loc_sem.at[l, j]).start()

    def own_wait(l, j):
        pltpu.make_async_copy(wslot(l, z, xx, j), wslot(l, z, xx, j), loc_sem.at[l, j]).wait()

    pieces = [(0, 0, 0, 0, False)]
    for l in range(L):
        for j in range(4):
            n, turned = cfg["cuts"][j], cfg["turned"][j]
            w = (COLS[j + 1] - COLS[j]) // n
            pieces += [(l, j, COLS[j] + w * i, COLS[j] + w * i + w, i in turned) for i in range(n)]
    NP = len(pieces)
    last_of = {(l, j): max(p for p in range(1, NP) if pieces[p][:2] == (l, j)) for l in range(L) for j in range(4)}
    far = M - 1
    lower = z < M // 2
    edge = jnp.where(lower, z, far - z)
    near_of = []
    for i in range(M - 1):
        t = i + jnp.where(i >= edge, 1, 0)
        near_of.append(jnp.where(lower, t, far - t))
    relay_to = jnp.where(lower, 0, far)
    relays = jnp.logical_and(z > 0, z < far)
    direct = {k: (z < far if k == 1 else z > 0 if k == M - 1 else None) for k in range(1, M)}
    if not cfg["relay"]:
        direct, relays = {k: None for k in range(1, M)}, z < 0

    def when(cond, f):
        if cond is None:
            f()
        else:
            pl.when(cond)(f)

    def ag_slot(p, zz, xp):
        l, j, c0, c1, _ = pieces[p]
        return PS.at[zz, xp] if p == 0 else W.at[l, zz, xp, :, c0:c1]

    def ag_z(p, zz, xp, to, i, ss, rs):
        return rcopy(ag_slot(p, zz, xp), ag_slot(p, zz, xp), ss.at[p, i], rs.at[p, zz], (2 * to + xx, s))

    def ag_x(p, zz, xp):
        return rcopy(ag_slot(p, zz, xp), ag_slot(p, zz, xp), agx_s.at[p, zz], agx_r.at[p, zz], xdev)

    def ag_issue(p):
        l, j, _, _, x_first = pieces[p]
        ag_load(p)
        for k in range(1, M):
            when(direct[k], ag_z(p, z, xx, zof[k], k, agz_s, agz_r).start)
        if not x_first:
            ag_x(p, z, xx).start()
            return
        ag_x(p, z, 1 - xx).wait_recv()
        for k in range(1, M):
            when(direct[k], ag_z(p, z, 1 - xx, zof[k], k, agw_s, agw_r).start)

    def ag_load(p):
        l, j = pieces[p][:2]
        if p > 0 and (l, j) not in loaded:
            own_wait(l, j)
            loaded.add((l, j))

    def ag_turned():
        for p in range(NP):
            if pieces[p][4]:
                ag_load(p)
                ag_x(p, z, xx).start()

    loaded = set()
    queue = []
    for p in range(NP):
        queue += [(p, i) for i in range(M - 1)]
    state = {"next": 0, "issued": 0}

    def ag_issue_to(n):
        while state["issued"] < min(n, NP):
            ag_issue(state["issued"])
            state["issued"] += 1

    def ag_service(n):
        for _ in range(n):
            if state["next"] == len(queue):
                return
            p, i = queue[state["next"]]
            x_first = pieces[p][4]
            ag_issue_to(p + 1)
            zz = near_of[i]
            got = [(xx, agz_s, agz_r)] + ([(1 - xx, agw_s, agw_r)] if x_first else [])
            for xp, ss, rs in got:
                ag_z(p, zz, xp, zz, 0, ss, rs).wait_recv()
                if not x_first:
                    ag_x(p, zz, xp).start()
                if i == M - 2 and cfg["relay"]:
                    when(relays, ag_z(p, zz, xp, relay_to, 0, ss, rs).start)
            state["next"] += 1
            if i == M - 2:
                ag_issue_to(p + 1 + cfg["ahead"])

    def ag_finish(p):
        while state["next"] < len(queue) and queue[state["next"]][0] <= p:
            ag_service(1)
        for q in range(p + 1):
            if q not in finished:
                finished.add(q)
                if not pieces[q][4]:
                    for zz in range(M):
                        ag_x(q, zz, 1 - xx).wait_recv()

    finished = set()

    def ag_drain(first, last):
        for p in range(first, last):
            x_first = pieces[p][4]
            for ss, rs in [(agz_s, agz_r)] + ([(agw_s, agw_r)] if x_first else []):
                for k in range(1, M):
                    when(direct[k], ag_z(p, z, xx, zof[k], k, ss, rs).wait_send)
                if cfg["relay"]:
                    when(relays, ag_z(p, z, xx, relay_to, 0, ss, rs).wait_send)
            for zz in [z] if x_first else range(M):
                ag_x(p, zz, xx).wait_send()

    for l in range(L):
        for j in range(4):
            own_load(l, j)
    for l in range(L):
        PS[z, xx, 12 * l:12 * l + 2, :] = gains_ref[l].astype(F32)
        PS[z, xx, 12 * l + 2:12 * l + 8, :] = biases_ref[l].astype(F32)
        for i in range(S):
            PS[z, xx, 12 * l + 8 + i:12 * l + 9 + i, :] = bfc_ref[l:l + 1, RB * i:RB * i + RB].astype(F32)
    row = mask_ref[...].astype(F32)
    MK[s] = jnp.zeros_like(MK[s])
    MK[s, 0:1, 0:T] = row
    ag_issue_to(1)
    mks = [rcopy(MK.at[s], MK.at[s], mk_s.at[i], mk_r.at[i], dev) for i, dev in enumerate((core, ydev, diag))]
    for c in mks:
        c.start()
    ag_issue_to(2)
    ag_turned()
    ag_issue_to(1 + cfg["ahead"])
    diagonal = lax.broadcasted_iota(jnp.int32, (T, T), 0) == lax.broadcasted_iota(jnp.int32, (T, T), 1)
    TV[...] = jnp.zeros_like(TV)
    TV[0:T, :] = jnp.broadcast_to(
        jnp.sum(jnp.where(diagonal, row, 0.0), axis=1, keepdims=True) * valid_ref[0].astype(F32), (T, 128))
    H[0] = jnp.zeros((TP, D), F32)
    H[0, 0:T, :] = x_ref[...].astype(F32)
    SGF[...] = jnp.zeros_like(SGF)
    SG[...] = jnp.zeros_like(SG)
    STAT[...] = jnp.zeros_like(STAT)
    for i, c in enumerate(mks):
        c.wait_send()
        rcopy(MK.at[s], MK.at[(core, ydev, diag)[i][1]], mk_s.at[i], mk_r.at[i], (core, ydev, diag)[i]).wait_recv()
    MR[...] = jnp.concatenate([MK[i, :, 0:TP] for i in range(S)], axis=1)
    ag_finish(0)
    for i in range(M):
        for j in range(2):
            PR[:, 128 * (2 * i + j):128 * (2 * i + j) + 128] = PS[i, j]

    DH[...] = jnp.zeros_like(DH)
    DH[0:T, :] = cot_ref[...].astype(F32) * TV[0:T, 0:1]

    def prow(l, i):
        return PR[12 * l + i:12 * l + i + 1, :]

    def prow_cols(l, i):
        return PR[12 * l + i:12 * l + i + 1, pl.ds(pl.multiple_of(C * s, C), C)]

    HB = TP // 2

    def ge_part(e, buf, i, h):
        rows = pl.ds(h * HB, HB)
        if i == 0:
            return rcopy(buf.at[s, rows], buf.at[s, rows], ge_s.at[e, 0, h], ge_r.at[e, 0, h], core)
        if i == 1:
            return rcopy(buf.at[s, rows], buf.at[s, rows], ge_s.at[e, 1, h], ge_r.at[e, 1, h], ydev)
        return rcopy(buf.at[ydev[1], rows], buf.at[ydev[1], rows], ge_s.at[e, 2, h], ge_r.at[e, 2, h], core)

    def ge_send(e, buf, h):
        ge_part(e, buf, 1, h).start()
        ge_part(e, buf, 0, h).start()

    def ge_end(e, buf):
        for h in range(2):
            rcopy(buf.at[s, pl.ds(h * HB, HB)], buf.at[ydev[1], pl.ds(h * HB, HB)],
                  ge_s.at[e, 1, h], ge_r.at[e, 1, h], ydev).wait_recv()
            ge_part(e, buf, 2, h).start()
        for h in range(2):
            rcopy(buf.at[s, pl.ds(h * HB, HB)], buf.at[core[1], pl.ds(h * HB, HB)],
                  ge_s.at[e, 0, h], ge_r.at[e, 0, h], core).wait_recv()
        for h in range(2):
            rcopy(buf.at[ydev[1], pl.ds(h * HB, HB)], buf.at[diag[1], pl.ds(h * HB, HB)],
                  ge_s.at[e, 2, h], ge_r.at[e, 2, h], core).wait_recv()
        for i in range(3):
            for h in range(2):
                ge_part(e, buf, i, h).wait_send()

    def re_copy(e, i, h):
        b = e % 2
        rows = pl.ds(h * HB, HB)
        if i == 0:
            return rcopy(PB.at[b, 1 - ypos, 1 - cpos, rows], R0.at[b, rows], re_s.at[e, 0, h], re_r.at[e, 0, h], core)
        if i == 1:
            return rcopy(PB.at[b, 1 - ypos, cpos, rows], R1.at[b, rows], re_s.at[e, 1, h], re_r.at[e, 1, h], ydev)
        return rcopy(PB.at[b, ypos, 1 - cpos, rows], R2.at[b, rows], re_s.at[e, 2, h], re_r.at[e, 2, h], core)

    def re_run(e, partial):
        b = e % 2
        partial(1 - ypos, b)
        for h in range(2):
            re_copy(e, 0, h).start()
        for h in range(2):
            re_copy(e, 0, h).wait_recv()
            for r0 in range(h * HB, h * HB + HB, 16):
                PB[b, 1 - ypos, cpos, r0:r0 + 16, :] = (
                    PB[b, 1 - ypos, cpos, r0:r0 + 16, :].astype(F32) + R0[b, r0:r0 + 16, :].astype(F32)).astype(BF16)
            re_copy(e, 1, h).start()
        partial(ypos, b)
        for h in range(2):
            re_copy(e, 2, h).start()

    def re_half(e, h):
        for i in (2, 1):
            re_copy(e, i, h).wait_recv()

    def re_sent(e):
        for i in range(3):
            for h in range(2):
                re_copy(e, i, h).wait_send()

    def re_rows(e, rows):
        b = e % 2
        return (PB[b, ypos, cpos, rows, :].astype(F32) + R2[b, rows, :].astype(F32)) + R1[b, rows, :].astype(F32)

    def partial_of(lhs, rhs, cb):
        def run(chip, b):
            def tile(j, _):
                cols = pl.ds(pl.multiple_of(j * C, C), C)
                r = ddot(lhs(chip), rhs(j), 1, cb).astype(BF16)
                PB[b, chip, :, :, cols] = r.reshape(2, TP, C)
                return 0
            lax.fori_loop(0, S, tile, 0)
        return run

    def row_loop(body, init, before=None, after=None):
        for h in range(2):
            if before is not None:
                before(h)

            def one(i, carry):
                return body(pl.ds(pl.multiple_of(h * HB + i * 16, 16), 16), carry)
            init = lax.fori_loop(0, HB // 16, one, init, unroll=cfg["unroll"])
            if after is not None:
                after(h)
        return init

    def norm(v):
        center = v - jnp.mean(v, -1, keepdims=True)
        inverse = lax.rsqrt(jnp.mean(center * center, -1, keepdims=True) + epsilon)
        return center * inverse, inverse

    def fold(v):
        return v[0:8] + v[8:16]

    def col_sum(v):
        return jnp.sum(v, axis=0, keepdims=True)

    lane_low = lax.broadcasted_iota(jnp.int32, (1, 2 * HEAD_DIM), 1) < HEAD_DIM
    lane_idx = lax.broadcasted_iota(jnp.int32, (1, 128), 1)

    def attend(l, pair):
        def block(i, _):
            rows = pl.ds(pl.multiple_of(i * TP, 16), TP)
            q = QKV[l, rows, 128 * pair:128 * pair + 128]
            k = QKV[l, :, C + 128 * pair:C + 128 * pair + 128]
            v = QKV[l, :, 2 * C + 128 * pair:2 * C + 128 * pair + 128]
            outs, lses = [], []
            for h in range(2):
                keep = lane_low if h == 0 else jnp.logical_not(lane_low)
                qh = jnp.where(keep, q, jnp.zeros_like(q))
                sc = ddot(qh, k, 1, 1) * SCALE
                sc = jnp.where(MR[0:1, :] > 0, sc, NEG)
                mx = jnp.max(sc, -1, keepdims=True)
                ex = jnp.exp(sc - mx)
                tot = jnp.sum(ex, -1, keepdims=True)
                outs.append(ddot(ex.astype(BF16), v, 1, 0) / tot)
                lses.append(mx + jnp.log(tot))
            OB[l, rows, 128 * pair:128 * pair + 128] = jnp.where(lane_low, outs[0], outs[1]).astype(BF16)
            held = jnp.where(lane_idx == 2 * pair, lses[0], lses[1])
            LSE[l, rows, :] = held if pair == 0 else jnp.where(lane_idx < 2 * pair, LSE[l, rows, :], held)
            return 0
        lax.fori_loop(0, S, block, 0)

    def attend_back(l, pair):
        DKV[...] = jnp.zeros_like(DKV)

        def block(i, _):
            rows = pl.ds(pl.multiple_of(i * TP, 16), TP)
            q = QKV[l, rows, 128 * pair:128 * pair + 128]
            k = QKV[l, :, C + 128 * pair:C + 128 * pair + 128]
            v = QKV[l, :, 2 * C + 128 * pair:2 * C + 128 * pair + 128]
            do = DO[rows, 128 * pair:128 * pair + 128]
            lse = LSE[l, rows, :]
            dqs = []
            dk = dv = None
            for h in range(2):
                keep = lane_low if h == 0 else jnp.logical_not(lane_low)
                qh = jnp.where(keep, q, jnp.zeros_like(q))
                doh = jnp.where(keep, do, jnp.zeros_like(do))
                sc = ddot(qh, k, 1, 1) * SCALE
                sc = jnp.where(MR[0:1, :] > 0, sc, NEG)
                p = jnp.exp(sc - lse[:, 2 * pair + h:2 * pair + h + 1])
                dp = ddot(doh, v, 1, 1)
                inner = jnp.sum(p * dp, -1, keepdims=True)
                ds = (p * (dp - inner)).astype(BF16)
                dqs.append(ddot(ds, k, 1, 0))
                dkh = ddot(ds, qh, 0, 0)
                dvh = ddot(p.astype(BF16), doh, 0, 0)
                dk = dkh if dk is None else dk + dkh
                dv = dvh if dv is None else dv + dvh
            DQKV[rows, 128 * pair:128 * pair + 128] = (jnp.where(lane_low, dqs[0], dqs[1]) * SCALE).astype(BF16)
            DKV[0] += dk
            DKV[1] += dv
            return 0
        lax.fori_loop(0, S, block, 0)
        DQKV[:, C + 128 * pair:C + 128 * pair + 128] = (DKV[0] * SCALE).astype(BF16)
        DQKV[:, 2 * C + 128 * pair:2 * C + 128 * pair + 128] = DKV[1].astype(BF16)

    peers = (core, ydev, diag)

    def wo_copy(l, i):
        to = peers[i][1]
        return rcopy(W.at[l, to, :, :, COLS[OUT]:COLS[FC1]], WO.at[l, :, :, pl.ds(pl.multiple_of(C * s, C), C)],
                     wo_s.at[l, i], wo_r.at[l, i], peers[i])

    def wo_start(l):
        for i in range(3):
            wo_copy(l, i).start()
        WO[l, :, :, pl.ds(pl.multiple_of(C * s, C), C)] = W[l, s, :, :, COLS[OUT]:COLS[FC1]]

    def wo_end(l):
        for i in range(3):
            wo_copy(l, i).wait()

    def gw_copy(l, i):
        to = peers[i][1]
        return rcopy(WO.at[l, :, :, pl.ds(pl.multiple_of(C * to, C), C)], W.at[l, s, :, :, COLS[OUT]:COLS[FC1]],
                     gw_s.at[l, i], gw_r.at[l, i], peers[i])

    def gw_start(l):
        for i in range(3):
            gw_copy(l, i).start()
        W[l, s, :, :, COLS[OUT]:COLS[FC1]] = WO[l, :, :, pl.ds(pl.multiple_of(C * s, C), C)]

    def gw_end(l):
        for i in range(3):
            gw_copy(l, i).wait()

    def wtile(l, j, a, b):
        n = M // S
        if n == 1:
            return W[l, j, :, :, a:b].reshape(2 * RB, b - a)
        return W[l, pl.ds(j * n, n), :, :, a:b].reshape(2 * RB * n, b - a)

    def grad_of(l, j):
        return GF if (l, j) == (L - 1, FC2) else W.at[l]

    def GC(l, j):
        return slice(0, D) if (l, j) == (L - 1, FC2) else slice(COLS[j], COLS[j + 1])

    def rx_copy(l, j, k):
        a, b = COLS[j], COLS[j + 1]
        return rcopy(grad_of(l, j).at[zof[k], 1 - xx, :, GC(l, j)], XR.at[l, zof[k], :, a:b], rx_s.at[l, j, k], rx_r.at[l, j, k], xdev)

    def rz_copy(l, j, k):
        a, b = COLS[j], COLS[j + 1]
        return rcopy(XR.at[l, zof[k], :, a:b], ZR.at[l, k - 1, :, a:b], rz_s.at[l, j, k], rz_r.at[l, j, k], zdev[k])

    def rz_recv(l, j, k):
        a, b = COLS[j], COLS[j + 1]
        return rcopy(XR.at[l, zof[k], :, a:b], ZR.at[l, k - 1, :, a:b], rz_s.at[l, j, k], rz_r.at[l, j, k], zdev[k])

    def whole_of(l, j):
        return FIN.at[l, :, COLS[j]:COLS[j + 1]]

    def fo_start(l, j):
        for _, dst, c0, n in own_parts(l, j, s):
            src = FIN.at[l, :, c0:c0 + n]
            for i in range(2):
                rcopy(src, dst, fo_s.at[l, j, i], fo_r.at[l, j, i], peers[i]).start()
            pltpu.make_async_copy(src, dst, loc_sem.at[l, j]).start()

    def fo_pass(l, j):
        rcopy(whole_of(l, j), whole_of(l, j), fo_s.at[l, j, 1], fo_r.at[l, j, 1], peers[1]).wait_recv()
        for _, dst, c0, n in own_parts(l, j, ydev[1]):
            rcopy(dst, dst, fo_s.at[l, j, 2], fo_r.at[l, j, 2], core).start()

    def fo_wait(l, j):
        for i in range(3):
            c = rcopy(whole_of(l, j), whole_of(l, j), fo_s.at[l, j, i], fo_r.at[l, j, i], peers[i])
            c.wait_send()
            if i != 1:
                c.wait_recv()
        pltpu.make_async_copy(whole_of(l, j), whole_of(l, j), loc_sem.at[l, j]).wait()

    def red_first(l, j, k):
        a, b = COLS[j], COLS[j + 1]
        rx_copy(l, j, k).wait_recv()
        zz = zof[k]
        if k == 0:
            return
        for r0 in range(0, RB, 32):
            XR[l, zz, r0:r0 + 32, a:b] = (XR[l, zz, r0:r0 + 32, a:b].astype(F32) + grad_of(l, j)[zz, xx, r0:r0 + 32, GC(l, j)].astype(F32)).astype(BF16)
        rz_copy(l, j, k).start()

    def red_second(l, j):
        a, b = COLS[j], COLS[j + 1]
        red_first(l, j, 0)
        for k in range(1, M):
            rz_recv(l, j, k).wait_recv()
        for r0 in range(0, RB, 32):
            t = XR[l, z, r0:r0 + 32, a:b].astype(F32) + grad_of(l, j)[z, xx, r0:r0 + 32, GC(l, j)].astype(F32)
            for k in range(1, M):
                t = t + ZR[l, k - 1, r0:r0 + 32, a:b].astype(F32)
            FIN[l, r0:r0 + 32, a:b] = t.astype(BF16)
        fo_start(l, j)

    def red_end(l, j):
        for k in range(M):
            rx_copy(l, j, k).wait_send()
        for k in range(1, M):
            rz_copy(l, j, k).wait_send()
        fo_wait(l, j)

    events = []
    later = []
    done = {"n": 0}

    def red_later():
        if len(later) > 1:
            events.append((fo_pass,) + later.pop(0))
        if later:
            events.append((red_second,) + later[-1])

    def red_push(l, j):
        for k in list(range(1, M)) + [0]:
            rx_copy(l, j, k).start()
        events.extend((red_first, l, j, k) for k in range(1, M))
        red_later()
        later.append((l, j))

    def red_service(n):
        for _ in range(n):
            if done["n"] >= len(events):
                return
            f, *a = events[done["n"]]
            done["n"] += 1
            f(*a)

    def norm_back(l, src, e, gain, buf=None, g=None):
        def one(rows, acc):
            n, r = norm(src[l, rows, :])
            dm = re_rows(e, rows)
            dn = dm * gain
            pm = jnp.mean(dn, -1, keepdims=True)
            cm = jnp.mean(dn * n, -1, keepdims=True)
            dh = DH[rows, :] + r * (dn - pm - n * cm)
            DH[rows, :] = dh
            sums = acc[0] + fold(dm * n), acc[1] + fold(dm)
            if buf is None:
                return sums
            v = dh.astype(BF16)
            buf[s, rows, :] = v
            return sums + (acc[2] + fold(v.astype(F32)),)
        zero = jnp.zeros((8, D), F32)
        out = row_loop(one, (zero,) * (2 if buf is None else 3), lambda h: re_half(e, h),
                       None if buf is None else lambda h: ge_send(g, buf, h))
        re_sent(e)
        return [col_sum(v) for v in out]

    def low_of(buf, g):
        def one(rows, acc):
            v = DH[rows, :].astype(BF16)
            buf[s, rows, :] = v
            return acc + fold(v.astype(F32))
        return col_sum(row_loop(one, jnp.zeros((8, D), F32), after=lambda h: ge_send(g, buf, h)))

    def forward(l):
        e = 2 * l
        fsv = cfg["fsv"]

        def ln1(rows, _):
            n, _r = norm(H[l, rows, :])
            AF[l, s, rows, :] = (n * prow(l, 0) + prow(l, 2)).astype(BF16)
            return 0
        row_loop(ln1, 0, after=lambda h: ge_send(e, AF.at[l], h))
        ag_service(fsv[0])
        ge_end(e, AF.at[l])
        ag_finish(last_of[l, QK])
        for n in range(3):
            r = ddot(AF[l].reshape(R, D), W[l, :, :, :, C * n:C * n + C].reshape(D, C), 1, 0)
            if n == 0:
                r = r + prow_cols(l, 3)
            if n == 2:
                r = r + prow_cols(l, 4)
            QKV[l, :, C * n:C * n + C] = r.astype(BF16)
        ag_finish(last_of[l, OUT])
        wo_start(l)
        if l == 0:
            SGF[12 * (L - 1) + 7:12 * (L - 1) + 8, :] = low_of(BF.at[0], 2 * L)
        attend(l, 0)
        ag_service(fsv[1])
        attend(l, 1)
        ag_service(fsv[2])
        if l == 0:
            ge_end(2 * L, BF.at[0])
        wo_end(l)
        re_run(e + 0, partial_of(
            lambda chip: OB[l, pl.ds(pl.multiple_of(chip * 2 * TP, 16), 2 * TP), :],
            lambda j: WO[l, :, :, pl.ds(pl.multiple_of(j * C, C), C)].reshape(C, C), 0))
        ag_service(fsv[3])

        def post(rows, acc):
            hv = H[l, rows, :]
            br = re_rows(e + 0, rows) + prow(l, 5)
            mid = hv + br
            H2[l, rows, :] = mid
            n, _r = norm(mid)
            MF[l, s, rows, :] = (n * prow(l, 1) + prow(l, 6)).astype(BF16)
            t = TV[rows, 0:1]
            return acc[0] + fold(t * hv * hv), acc[1] + fold(t * br * br)
        zero = jnp.zeros((8, D), F32)
        s0, s1 = row_loop(post, (zero, zero), lambda h: re_half(e, h), lambda h: ge_send(e + 1, MF.at[l], h))
        re_sent(e)
        ag_service(fsv[4])
        ge_end(e + 1, MF.at[l])
        ag_finish(last_of[l, FC1])
        bias = PR[pl.ds(12 * l + 8 + s, 1), :]
        for j in range(FS // C):
            u = ddot(MF[l].reshape(R, D), W[l, :, :, :, COLS[FC1] + C * j:COLS[FC1] + C * j + C].reshape(D, C), 1, 0)
            u = u + bias[:, C * j:C * j + C]
            U[l, :, C * j:C * j + C] = u
            GW[:, C * j:C * j + C] = (u / (1.0 + jnp.exp(-1.702 * u))).astype(BF16)
        stat(3 * l, s0)
        stat(3 * l + 1, s1)
        if l == L - 1:
            for j in range(FS // C):
                GF[j, :, :, :] = ddot(GW[:, C * j:C * j + C], BF[0].reshape(R, D), 0, 0).astype(BF16).reshape(2, RB, D)
        ag_finish(last_of[l, FC2])
        if l == L - 1:
            red_push(l, FC2)
        re_run(e + 1, partial_of(
            lambda chip: GW[pl.ds(pl.multiple_of(chip * 2 * TP, 16), 2 * TP), :],
            lambda j: W[l, :, :, :, pl.ds(pl.multiple_of(COLS[FC2] + j * C, C), C)].reshape(FS, C), 0))

    def forward_end(l):
        e = 2 * l

        def last(rows, acc):
            out = re_rows(e + 1, rows) + prow(l, 7)
            res = H2[l, rows, :] + out
            H[l + 1, rows, :] = res
            t = TV[rows, 0:1]
            return acc + fold(t * out * out)
        ag_service(cfg["fsv"][5])
        stat(3 * l + 2, row_loop(last, jnp.zeros((8, D), F32), lambda h: re_half(e + 1, h)))
        re_sent(e + 1)

    def stat(i, v):
        STAT[...] = jnp.where(lane_idx == i, jnp.sum(col_sum(v), axis=1, keepdims=True), STAT[...])

    def backward(l):
        ge_a = re_a = 2 * L + 2 * (L - 1 - l)
        ge_b = re_b = ge_a + 1
        B0, B1 = BF.at[0], BF.at[1]
        svc = cfg["svc"][L - 1 - l]
        if l < L - 1:
            red_service(svc[0])
            ge_end(ge_a, B0)
        for j in range(FS // C):
            dg = ddot(BF[0].reshape(R, D), wtile(l, j, COLS[FC2], COLS[FC2] + D), 1, 1)
            u = U[l, :, C * j:C * j + C]
            sg = 1.0 / (1.0 + jnp.exp(-1.702 * u))
            if l < L - 1:
                GW[:, C * j:C * j + C] = (u * sg).astype(BF16)
            du = (dg * (sg + 1.702 * u * sg * (1.0 - sg))).astype(BF16)
            DU[:, C * j:C * j + C] = du
            SGF[pl.ds(12 * l + 8 + s, 1), C * j:C * j + C] = jnp.sum(du.astype(F32), axis=0, keepdims=True)
        red_service(svc[1])
        if l < L - 1:
            for j in range(FS // C):
                W[l, j, :, :, COLS[FC2]:COLS[FC2] + D] = ddot(GW[:, C * j:C * j + C], BF[0].reshape(R, D), 0, 0).astype(BF16).reshape(2, RB, D)
            red_push(l, FC2)
        re_run(re_a, partial_of(
            lambda chip: DU[pl.ds(pl.multiple_of(chip * 2 * TP, 16), 2 * TP), :],
            lambda j: wtile(l, j, COLS[FC1], COLS[FC1] + FS), 1))
        for j in range(S):
            W[l, j, :, :, COLS[FC1]:COLS[FC1] + FS] = ddot(MF[l, :, :, C * j:C * j + C].reshape(R, C), DU[...], 0, 0).astype(BF16).reshape(2, RB, FS)
        red_push(l, FC1)
        if l == L - 1:
            forward_end(l)
        red_service(svc[2])
        gg, bb, cc = norm_back(l, H2, re_a, prow(l, 1), B1, ge_b)
        SGF[12 * l + 1:12 * l + 2, :] = gg
        SGF[12 * l + 6:12 * l + 7, :] = bb
        SGF[12 * l + 5:12 * l + 6, :] = cc
        red_service(svc[3])
        ge_end(ge_b, B1)
        DO[...] = ddot(BF[1].reshape(R, D), WO[l].reshape(C, D), 1, 1).astype(BF16)
        for j in range(S):
            WO[l, :, :, C * j:C * j + C] = ddot(OB[l], BF[1, :, :, C * j:C * j + C].reshape(R, C), 0, 0).astype(BF16).reshape(2, RB, C)
        gw_start(l)
        attend_back(l, 0)
        red_service(svc[4])
        attend_back(l, 1)
        gw_end(l)
        red_push(l, OUT)
        red_service(svc[5])
        for i, (row, c0) in enumerate(((3, 0), (4, 2 * C))):
            SGF[12 * l + row:12 * l + row + 1, pl.ds(pl.multiple_of(C * s, C), C)] = jnp.sum(
                DQKV[:, c0:c0 + C].astype(F32), axis=0, keepdims=True)
        re_run(re_b, partial_of(
            lambda chip: DQKV[pl.ds(pl.multiple_of(chip * 2 * TP, 16), 2 * TP), :],
            lambda j: wtile(l, j, 0, 3 * C), 1))
        for j in range(S):
            W[l, j, :, :, 0:3 * C] = ddot(AF[l, :, :, C * j:C * j + C].reshape(R, C), DQKV[...], 0, 0).astype(BF16).reshape(2, RB, 3 * C)
        red_push(l, QK)
        red_service(svc[6])
        if l > 0:
            gg, bb, cc = norm_back(l, H, re_b, prow(l, 0), B0, ge_b + 1)
            SGF[12 * (l - 1) + 7:12 * (l - 1) + 8, :] = cc
        else:
            gg, bb = norm_back(l, H, re_b, prow(l, 0))
        SGF[12 * l + 0:12 * l + 1, :] = gg
        SGF[12 * l + 2:12 * l + 3, :] = bb
        red_service(svc[7])

    for l in range(L):
        forward(l)
        if l < L - 1:
            forward_end(l)
    ag_drain(0, last_of[L - 1, FC1] + 1)
    for l in reversed(range(L)):
        backward(l)
    gx_ref[...] = DH[0:T, :]
    y_ref[...] = H[L, 0:T, :].astype(BF16)
    STAT[...] = jnp.where(lane_idx == 3 * L, col_sum(TV[:, 0:1]), STAT[...])

    for i in range(M):
        for j in range(2):
            SG[i, j, 0:24, :] = SGF[0:24, 128 * (2 * i + j):128 * (2 * i + j) + 128]
            SG[i, j, 24:25, :] = STAT[...]
    sgx = rcopy(SG.at[:, 1 - xx], SX, st_s.at[0], st_r.at[0], xdev)
    sgx.start()

    def sz(k, frm):
        return rcopy(SX.at[zof[k]], SZ.at[zfrom[k] if frm else z], st_s.at[k], st_r.at[k], zdev[k])

    def stc(i, frm):
        slot = peers[i][1] if frm else s
        return rcopy(ST.at[s], ST.at[slot], st_s.at[M + i], st_r.at[M + i], peers[i])

    red_service(len(events))
    sgx.wait()
    SX[...] = SX[...] + SG[:, xx]
    SZ[z] = SX[z]
    for k in range(1, M):
        sz(k, False).start()
    red_later()
    red_service(len(events))
    for k in range(1, M):
        sz(k, True).wait_recv()
    tot = SZ[0]
    for k in range(1, M):
        tot = tot + SZ[k]
    ST[s] = tot
    for i in range(3):
        stc(i, False).start()
    for p in later:
        fo_pass(*p)
    for i in range(3):
        stc(i, True).wait_recv()
    tot = (ST[0] + ST[1]) + (ST[2] + ST[3])
    for l in range(L):
        ogain_ref[l] = tot[12 * l:12 * l + 2]
        obias_ref[l, 0:1, :] = tot[12 * l + 2:12 * l + 3]
        obias_ref[l, 1:5, :] = tot[12 * l + 4:12 * l + 8]
        oquery_ref[l:l + 1, :] = tot[12 * l + 3:12 * l + 4]
        for i in range(S):
            obfc_ref[l:l + 1, RB * i:RB * i + RB] = tot[12 * l + 8 + i:12 * l + 9 + i]
    sums = tot[12 * L:12 * L + 1]
    root = jnp.sqrt(sums / (jnp.maximum(sums[:, 3 * L:3 * L + 1], 1.0) * D))
    for l in range(L):
        rms_ref[l:l + 1, :] = root[:, 3 * l:3 * l + 3]
    for k in range(1, M):
        sz(k, False).wait_send()
    for i in range(3):
        stc(i, False).wait_send()
    ag_drain(last_of[L - 1, FC1] + 1, NP)
    for l in reversed(range(L)):
        for j in (FC2, FC1, OUT, QK):
            red_end(l, j)


def fused_local(cfg, block_input, key_mask, valid, gains, biases, w_qkv, w_out, w_fc1, b_fc1, w_fc2, cotangent):
    L, M, RB, T, TP, D, NC, FS = (cfg[n] for n in ("L", "M", "RB", "T", "TP", "D", "NC", "FS"))
    S, dp = 4, 2 * M
    C = D // S
    R = S * TP
    vm = pl.BlockSpec(memory_space=pltpu.VMEM)
    hbm = pl.BlockSpec(memory_space=pl.ANY)
    dma = pltpu.SemaphoreType.DMA
    v = pltpu.VMEM
    NP, NE = 1 + sum(cfg["cuts"]) * L, 4 * L
    out = pl.pallas_call(
        partial(fused_kernel, cfg),
        out_shape=(
            jax.ShapeDtypeStruct((T, D), BF16),
            jax.ShapeDtypeStruct((T, D), F32),
            jax.ShapeDtypeStruct((L, 3), F32),
            jax.ShapeDtypeStruct((L, 2, RB), F32),
            jax.ShapeDtypeStruct((L, 5, RB), F32),
            jax.ShapeDtypeStruct((L, RB), F32),
            jax.ShapeDtypeStruct((L, S * RB), F32),
            jax.ShapeDtypeStruct(w_qkv.shape, BF16),
            jax.ShapeDtypeStruct(w_out.shape, BF16),
            jax.ShapeDtypeStruct(w_fc1.shape, BF16),
            jax.ShapeDtypeStruct(w_fc2.shape, BF16),
        ),
        in_specs=[vm, vm, pl.BlockSpec(memory_space=pltpu.SMEM), vm, vm, vm, vm, hbm, hbm, hbm, hbm],
        out_specs=(vm,) * 7 + (hbm,) * 4,
        scratch_shapes=[
            v((L, M, 2, RB, NC), BF16),
            v((L, 2, RB, D), BF16),
            v((L, M, RB, NC), BF16),
            v((L, M - 1, RB, NC), BF16),
            v((L, S, TP, D), BF16),
            v((L, R, 3 * C), BF16),
            v((L, R, C), BF16),
            v((L, S, TP, D), BF16),
            v((L, R, FS), F32),
            v((L + 1, TP, D), F32),
            v((L, TP, D), F32),
            v((L, R, 128), F32),
            v((M, 2, RB, D), BF16),
            v((2, S, TP, D), BF16),
            v((2, 2, 2, TP, D), BF16),
            v((2, TP, D), BF16),
            v((2, TP, D), BF16),
            v((2, TP, D), BF16),
            v((R, FS), BF16),
            v((R, FS), BF16),
            v((R, 3 * C), BF16),
            v((R, C), BF16),
            v((2, R, 128), F32),
            v((TP, D), F32),
            v((S, 8, -(-TP // 128) * 128), F32),
            v((8, R), F32),
            v((TP, 128), F32),
            v((M, 2, 12 * L, RB), F32),
            v((12 * L, D), F32),
            v((12 * L, D), F32),
            v((M, 2, 32, RB), F32),
            v((M, 32, RB), F32),
            v((M, 32, RB), F32),
            v((S, 32, RB), F32),
            v((L, RB, NC), BF16),
            v((1, RB), F32),
            dma((L, 4)),
            dma((NP, M)), dma((NP, M)), dma((NP, M)), dma((NP, M)), dma((NP, M)), dma((NP, M)),
            dma((NE, 3, 2)), dma((NE, 3, 2)), dma((NE, 3, 2)), dma((NE, 3, 2)),
            dma((L, 3)), dma((L, 3)), dma((L, 3)), dma((L, 3)),
            dma((L, 4, M)), dma((L, 4, M)), dma((L, 4, M)), dma((L, 4, M)),
            dma((L, 4, 3)), dma((L, 4, 3)), dma((3,)), dma((3,)), dma((M + 3,)), dma((M + 3,)),
        ],
        compiler_params=pltpu.CompilerParams(
            collective_id=0, has_side_effects=True, vmem_limit_bytes=cfg["vmem"]),
        cost_estimate=pl.CostEstimate(flops=24_000_000_000, bytes_accessed=20_000_000, transcendentals=0),
    )(block_input[0], key_mask, valid, gains, biases, b_fc1, cotangent[0], w_qkv, w_out, w_fc1, w_fc2)
    y, gx, rms, o_gain, o_bias, o_query, o_bfc, o_qkv, o_out, o_fc1, o_fc2 = out
    return (y[None], gx[None], rms, o_gain, o_bias, o_query,
            o_qkv.astype(F32), o_out.astype(F32), o_fc1.astype(F32), o_bfc, o_fc2.astype(F32))


def local(*args):
    block_input, w_qkv, w_fc2 = args[0], args[5], args[9]
    L, RB = w_qkv.shape[:2]
    T, D = block_input.shape[1:]
    S, dp = lax.axis_size("seq"), lax.axis_size("dp")
    FS = w_fc2.shape[1] * dp // S
    fits = (S == 4 and dp == 2 * S and RB % 128 == 0 and D // S == 2 * RB and L * 12 + 1 <= 32
            and FS // dp == RB and HEAD_DIM * 2 == 128 and D // S == 4 * HEAD_DIM and block_input.shape[0] == 1)
    if not fits:
        return plain_local(*args)
    cfg = dict(L=L, M=dp // 2, RB=RB, T=T, TP=-(-T // 16) * 16, D=D, NC=D + 2 * FS, FS=FS, ahead=3, unroll=5, cuts=(2, 1, 2, 2), turned=((), (), (), (0,)), relay=True, fsv=(6, 2, 2, 3, 5, 4), vmem=62 * 2**20,
               svc=((0, 0, 3, 2, 2, 0, 4, 1),) + ((5, 0, 2, 3, 1, 2, 4, 0),) * (L - 1))
    return fused_local(cfg, *args)


def solution(mesh):
    return jax.shard_map(
        local,
        mesh=mesh,
        in_specs=(
            P("dp", "seq", None),
            P("dp", "seq"),
            P("dp"),
            P(None, None, "dp"),
            P(None, None, "dp"),
            P(None, "dp", None),
            P(None, "dp", None),
            P(None, "dp", None),
            P(None, "dp"),
            P(None, "dp", None),
            P("dp", "seq", None),
        ),
        out_specs=(
            P("dp", "seq", None),
            P("dp", "seq", None),
            P(),
            P(None, None, "dp"),
            P(None, None, "dp"),
            P(None, "dp"),
            P(None, "dp", None),
            P(None, "dp", None),
            P(None, "dp", None),
            P(None, "dp"),
            P(None, "dp", None),
        ),
        check_vma=False,
    )
```

```python
from functools import partial
import math

import jax
import jax.numpy as jnp
from jax import lax
from jax.experimental import pallas as pl
from jax.experimental.pallas import tpu as pltpu
from jax.sharding import PartitionSpec as P

HEADS = 16
HEAD_DIM = 64
F32 = jnp.float32
BF16 = jnp.bfloat16

epsilon = 1e-05


def norm_parts(values_in, gain, shift):
    center = values_in - jnp.mean(values_in, -1, keepdims=True)
    inverse = lax.rsqrt(jnp.mean(center * center, -1, keepdims=True) + epsilon)
    normal = center * inverse
    return (normal * gain + shift, normal, inverse)


def norm_back(grad_output, normal, inverse, gain):
    grad_gain = jnp.sum(grad_output * normal, 0)
    grad_shift = jnp.sum(grad_output, 0)
    grad_norm = grad_output * gain
    plain_mean = jnp.mean(grad_norm, -1, keepdims=True)
    cross_mean = jnp.mean(grad_norm * normal, -1, keepdims=True)
    return (grad_gain, grad_shift, inverse * (grad_norm - plain_mean - normal * cross_mean))


def dot(a, b, ca=1, cb=0):
    return lax.dot_general(a, b, (((ca,), (cb,)), ((), ())), preferred_element_type=F32)


def split_heads(x, width):
    return x.reshape(x.shape[0], width // HEAD_DIM, HEAD_DIM)


def scores_of(query, keys, mask_row, scale):
    scores = jnp.einsum("qhd,khd->hqk", query, keys, preferred_element_type=F32) * scale
    return jnp.where(mask_row[None, None, :] > 0, scores, -1000000000.0)


def gather_rows(x):
    return lax.all_gather(x, "seq", axis=0, tiled=True)


def scatter_rows(x):
    return lax.psum_scatter(x.astype(BF16), "seq", scatter_dimension=0, tiled=True).astype(F32)


def forward_layer(hidden, weights, params, mask_row, tok_valid):
    w_qkv, w_out, w_fc1, w_fc2 = weights
    gains, biases, bias_q, bias_v, b_fc1 = params
    scale = 1.0 / math.sqrt(HEAD_DIM)
    width = w_out.shape[0]
    normed, normal_one, inverse_one = norm_parts(hidden, gains[0], biases[0])
    normed_all = gather_rows(normed.astype(BF16))
    packed = dot(normed_all, w_qkv)
    packed = (packed + jnp.concatenate([bias_q, jnp.zeros_like(bias_q), bias_v])).astype(BF16)
    query, keys, values = (split_heads(packed[:, i * width : (i + 1) * width], width) for i in range(3))
    scores = scores_of(query, keys, mask_row, scale)
    row_max = jnp.max(scores, -1, keepdims=True)
    log_total = row_max + jnp.log(jnp.sum(jnp.exp(scores - row_max), -1, keepdims=True))
    probs = jnp.exp(scores - log_total).astype(BF16)
    mixed = jnp.einsum("hqk,khd->qhd", probs, values, preferred_element_type=F32).astype(BF16)
    mixed = mixed.reshape(mixed.shape[0], width)
    branch = scatter_rows(dot(mixed, w_out)) + biases[3]
    middle = hidden + branch
    normed_two, normal_two, inverse_two = norm_parts(middle, gains[1], biases[4])
    normed_two_all = gather_rows(normed_two.astype(BF16))
    inner = dot(normed_two_all, w_fc1) + b_fc1
    gate_sig = jax.nn.sigmoid(1.702 * inner)
    gated = (inner * gate_sig).astype(BF16)
    output = scatter_rows(dot(gated, w_fc2)) + biases[5]
    stat = jnp.stack([jnp.sum(tok_valid * jnp.sum(v * v, -1)) for v in (hidden, branch, output)])
    stored = (normal_one, inverse_one, normed_all, query, keys, values, log_total, mixed,
              normal_two, inverse_two, normed_two_all, inner, gate_sig, gated)
    return (middle + output, stored, stat)


def backward_layer(grad_result, weights, params, stored, mask_row):
    w_qkv, w_out, w_fc1, w_fc2 = weights
    gains = params[0]
    scale = 1.0 / math.sqrt(HEAD_DIM)
    (normal_one, inverse_one, normed_all, query, keys, values, log_total, mixed,
     normal_two, inverse_two, normed_two_all, inner, gate_sig, gated) = stored
    out_low = grad_result.astype(BF16)
    grad_bias_five = jnp.sum(out_low.astype(F32), 0)
    out_all = gather_rows(out_low)
    grad_fc2 = dot(gated, out_all, 0, 0)
    grad_gated = dot(out_all, w_fc2, 1, 1)
    grad_inner = (grad_gated * (gate_sig + 1.702 * inner * gate_sig * (1.0 - gate_sig))).astype(BF16)
    grad_bias_fc1 = jnp.sum(grad_inner.astype(F32), 0)
    grad_fc1 = dot(normed_two_all, grad_inner, 0, 0)
    grad_normed_two = scatter_rows(dot(grad_inner, w_fc1, 1, 1))
    grad_gain_two, grad_shift_two, grad_middle = norm_back(grad_normed_two, normal_two, inverse_two, gains[1])
    grad_middle = grad_middle + grad_result
    branch_low = grad_middle.astype(BF16)
    grad_bias_three = jnp.sum(branch_low.astype(F32), 0)
    branch_all = gather_rows(branch_low)
    grad_out = dot(mixed, branch_all, 0, 0)
    width = w_out.shape[0]
    grad_mixed = split_heads(dot(branch_all, w_out, 1, 1).astype(BF16), width)
    scores = scores_of(query, keys, mask_row, scale)
    probs = jnp.exp(scores - log_total)
    grad_probs = jnp.einsum("qhd,khd->hqk", grad_mixed, values, preferred_element_type=F32)
    inner_sum = jnp.sum(probs * grad_probs, -1, keepdims=True)
    grad_scores = (probs * (grad_probs - inner_sum)).astype(BF16)
    grad_q = (jnp.einsum("hqk,khd->qhd", grad_scores, keys, preferred_element_type=F32) * scale).astype(BF16)
    grad_k = (jnp.einsum("hqk,qhd->khd", grad_scores, query, preferred_element_type=F32) * scale).astype(BF16)
    grad_v = jnp.einsum("hqk,qhd->khd", probs.astype(BF16), grad_mixed, preferred_element_type=F32).astype(BF16)
    rows = grad_q.shape[0]
    grad_proj = jnp.concatenate([g.reshape(rows, width) for g in (grad_q, grad_k, grad_v)], 1)
    grad_bias_proj = jnp.sum(grad_proj.astype(F32), 0)
    grad_qkv = dot(normed_all, grad_proj, 0, 0)
    grad_normed = scatter_rows(dot(grad_proj, w_qkv, 1, 1))
    grad_gain_one, grad_shift_one, grad_hidden = norm_back(grad_normed, normal_one, inverse_one, gains[0])
    grad_hidden = grad_hidden + grad_middle
    rows_sum = jnp.stack([grad_gain_one, grad_gain_two, grad_shift_one, grad_bias_three, grad_shift_two, grad_bias_five])
    return (grad_hidden, (grad_qkv, grad_out, grad_fc1, grad_fc2), rows_sum, grad_bias_proj, grad_bias_fc1)


def plain_local(block_input, key_mask, valid, gains, biases, w_qkv, w_out, w_fc1, b_fc1, w_fc2, cotangent):
    layers = w_qkv.shape[0]
    groups = lax.axis_size("seq")
    shards = lax.axis_size("dp")
    me = lax.axis_index("seq")
    width = block_input.shape[2]
    hidden_width = w_fc2.shape[1] * shards
    part = width // groups
    images = block_input.shape[0]
    assert images == 1
    mask_row = lax.all_gather(key_mask, "seq", axis=1, tiled=True)[0]
    tok_valid = (key_mask * valid[:, None]).astype(F32)[0]
    hidden = block_input[0].astype(F32)
    small = jnp.concatenate([gains.reshape(layers, -1), biases.reshape(layers, -1), b_fc1], 1)
    small = lax.all_gather(small, "dp", axis=0).astype(F32)
    n_g, n_b = gains.shape[1] * gains.shape[2], biases.shape[1] * biases.shape[2]
    gains_all = small[:, :, :n_g].reshape(shards, layers, 2, -1).transpose(1, 2, 0, 3).reshape(layers, 2, width)
    biases_all = small[:, :, n_g : n_g + n_b].reshape(shards, layers, 6, -1).transpose(1, 2, 0, 3).reshape(layers, 6, width)
    fc_all = small[:, :, n_g + n_b :].transpose(1, 0, 2).reshape(layers, shards, groups, -1)
    fc_mine = lax.dynamic_index_in_dim(fc_all, me, 2, False).reshape(layers, -1)
    proj_mine = lax.dynamic_index_in_dim(biases_all.reshape(layers, 6, groups, part), me, 2, False)

    def columns(w, outer):
        view = w.reshape(w.shape[0], outer, groups, -1)
        return lax.dynamic_index_in_dim(view, me, 2, False).reshape(w.shape[0], -1)

    def rows_of(w):
        view = w.reshape(groups, -1, w.shape[1])
        return lax.dynamic_index_in_dim(view, me, 0, False)

    def gather(w):
        return lax.all_gather(w, "dp", axis=0, tiled=True)

    weights, params, stored_all, stats = [], [], [], []
    for layer in range(layers):
        weights.append((
            gather(columns(w_qkv[layer], 3)),
            rows_of(gather(w_out[layer])),
            gather(columns(w_fc1[layer], shards)),
            gather(rows_of(w_fc2[layer])),
        ))
        params.append((gains_all[layer], biases_all[layer], proj_mine[layer, 1], proj_mine[layer, 2], fc_mine[layer]))
    for layer in range(layers):
        hidden, stored, stat = forward_layer(hidden, weights[layer], params[layer], mask_row, tok_valid)
        stored_all.append(stored)
        stats.append(stat)
    totals = lax.psum(jnp.concatenate([jnp.stack(stats).reshape(-1), jnp.sum(tok_valid)[None]]), ("dp", "seq"))
    rms = jnp.sqrt(totals[:-1].reshape(layers, 3) / (jnp.maximum(totals[-1], 1.0) * width))

    grad_hidden = cotangent[0].astype(F32) * tok_valid[:, None]
    big = [None] * layers
    sums = [None] * layers
    for layer in reversed(range(layers)):
        grad_hidden, grads, rows_sum, grad_proj, grad_fc = backward_layer(
            grad_hidden, weights[layer], params[layer], stored_all[layer], mask_row
        )
        g_qkv, g_out, g_fc1, g_fc2 = (g.astype(BF16) for g in grads)
        g_out = lax.all_to_all(g_out, "seq", split_axis=1, concat_axis=0, tiled=True)

        def reduce_(g):
            g = lax.psum_scatter(g, "dp", scatter_dimension=0, tiled=True)
            return lax.all_gather(g, "seq", axis=0)

        def join(g, outer):
            view = g.reshape(groups, g.shape[1], outer, -1)
            return view.transpose(1, 2, 0, 3).reshape(g.shape[1], -1)

        big[layer] = (
            join(reduce_(g_qkv), 3).astype(F32),
            join(reduce_(g_out), 1).astype(F32),
            join(reduce_(g_fc1), shards).astype(F32),
            reduce_(g_fc2).reshape(w_fc2.shape[1], -1).astype(F32),
        )
        proj = lax.dynamic_update_slice(jnp.zeros((3, groups, part), F32), grad_proj.reshape(3, 1, part), (0, me, 0))
        fc = lax.dynamic_update_slice(jnp.zeros((shards, groups, hidden_width // (shards * groups)), F32),
                                      grad_fc.reshape(shards, 1, -1), (0, me, 0))
        sums[layer] = jnp.concatenate([
            rows_sum.reshape(6, shards, -1).transpose(1, 0, 2).reshape(shards, -1),
            proj.reshape(3, shards, -1).transpose(1, 0, 2).reshape(shards, -1),
            fc.reshape(shards, -1),
        ], 1)
    flat = jnp.stack(sums, 1).astype(F32)
    flat = lax.psum(lax.psum_scatter(flat, "dp", scatter_dimension=0, tiled=True)[0], "seq")
    per = width // shards
    rows9 = flat[:, : 9 * per].reshape(layers, 9, per)
    grad_bfc1 = flat[:, 9 * per :]
    stack = lambda i: jnp.stack([b[i] for b in big])
    bias_rest = jnp.concatenate([rows9[:, 2:3], rows9[:, 8:9], rows9[:, 3:6]], 1)
    return (
        hidden.astype(BF16)[None],
        grad_hidden[None],
        rms,
        rows9[:, :2],
        bias_rest,
        rows9[:, 6],
        stack(0),
        stack(1),
        stack(2),
        grad_bfc1,
        stack(3),
    )


MESH = pl.DeviceIdType.MESH
NEG = -1000000000.0


def ddot(a, b, ca, cb):
    return lax.dot_general(a, b, (((ca,), (cb,)), ((), ())), preferred_element_type=F32)


def fused_kernel(cfg, x_ref, mask_ref, valid_ref, gains_ref, biases_ref, bfc_ref, cot_ref, w_qkv, w_out, w_fc1, w_fc2,
                 y_ref, gx_ref, rms_ref, ogain_ref, obias_ref, oquery_ref, obfc_ref, o_qkv, o_out, o_fc1, o_fc2,
                 W, WO, XR, ZR, AF, QKV, OB, MF, U, H, H2, LSE,
                 GF, BF, PB, R0, R1, R2, DU, GW, DQKV, DO, DKV, DH, MK, MR, TV, PS, PR, SGF, SG, SX, SZ, ST, STAT,
                 loc_sem, agz_s, agz_r, agx_s, agx_r, agw_s, agw_r, ge_s, ge_r, re_s, re_r, wo_s, wo_r, gw_s, gw_r,
                 rx_s, rx_r, rz_s, rz_r, fo_s, fo_r, mk_s, mk_r, st_s, st_r):
    L, M, RB, T, TP, D, NC = cfg["L"], cfg["M"], cfg["RB"], cfg["T"], cfg["TP"], cfg["D"], cfg["NC"]
    S = 4
    R = S * TP
    C = D // S
    FS = cfg["FS"]
    SCALE = 1.0 / math.sqrt(HEAD_DIM)
    COLS = (0, 3 * C, 3 * C + C, 3 * C + C + FS, NC)
    QK, OUT, FC1, FC2 = range(4)
    d = lax.axis_index("dp")
    s = lax.axis_index("seq")
    z = d // 2
    xx = d % 2
    ypos = s // 2
    cpos = s % 2
    core = (d, s + 1 - 2 * cpos)
    ydev = (d, s + 2 - 4 * ypos)
    diag = (d, (s + 1 - 2 * cpos) + 2 - 4 * ypos)
    xdev = (d + 1 - 2 * xx, s)
    zof = [lax.rem(z + k, M) for k in range(M)]
    zdev = [(2 * zof[k] + xx, s) for k in range(M)]
    zfrom = [lax.rem(z + M - k, M) for k in range(M)]

    def rcopy(src, dst, ss, rs, dev):
        return pltpu.make_async_remote_copy(src_ref=src, dst_ref=dst, send_sem=ss, recv_sem=rs,
                                            device_id=dev, device_id_type=MESH)

    bar = pltpu.get_barrier_semaphore()
    for dev in [core, ydev, diag, xdev] + zdev[1:]:
        pl.semaphore_signal(bar, inc=1, device_id=dev, device_id_type=MESH)
    pl.semaphore_wait(bar, 3 + M)

    def wslot(l, zz, xp, j):
        return W.at[l, zz, xp, :, COLS[j]:COLS[j + 1]]

    def own_parts(l, j, s):
        a = COLS[j]

        def at_s(start, width):
            return pl.ds(pl.multiple_of(start + width * s, width), width)
        if j == QK:
            return [(w_qkv.at[l, :, at_s(D * i, C)], o_qkv.at[l, :, at_s(D * i, C)], a + C * i, C) for i in range(3)]
        if j == OUT:
            return [(w_out.at[l, :, at_s(0, C)], o_out.at[l, :, at_s(0, C)], a, C)]
        if j == FC1:
            return [(w_fc1.at[l, :, at_s(S * RB * i, RB)], o_fc1.at[l, :, at_s(S * RB * i, RB)], a + RB * i, RB) for i in range(2 * M)]
        return [(w_fc2.at[l, at_s(0, RB), :], o_fc2.at[l, at_s(0, RB), :], a, D)]

    def own_load(l, j):
        for src, _, c0, n in own_parts(l, j, s):
            pltpu.make_async_copy(src, W.at[l, z, xx, :, c0:c0 + n], loc_sem.at[l, j]).start()

    def own_wait(l, j):
        pltpu.make_async_copy(wslot(l, z, xx, j), wslot(l, z, xx, j), loc_sem.at[l, j]).wait()

    pieces = [(0, 0, 0, 0, False)]
    for l in range(L):
        for j in range(4):
            n, turned = cfg["cuts"][j], cfg["turned"][j]
            w = (COLS[j + 1] - COLS[j]) // n
            pieces += [(l, j, COLS[j] + w * i, COLS[j] + w * i + w, i in turned) for i in range(n)]
    NP = len(pieces)
    last_of = {(l, j): max(p for p in range(1, NP) if pieces[p][:2] == (l, j)) for l in range(L) for j in range(4)}
    far = M - 1
    lower = z < M // 2
    edge = jnp.where(lower, z, far - z)
    near_of = []
    for i in range(M - 1):
        t = i + jnp.where(i >= edge, 1, 0)
        near_of.append(jnp.where(lower, t, far - t))
    relay_to = jnp.where(lower, 0, far)
    relays = jnp.logical_and(z > 0, z < far)
    direct = {k: (z < far if k == 1 else z > 0 if k == M - 1 else None) for k in range(1, M)}
    if not cfg["relay"]:
        direct, relays = {k: None for k in range(1, M)}, z < 0

    def when(cond, f):
        if cond is None:
            f()
        else:
            pl.when(cond)(f)

    def ag_slot(p, zz, xp):
        l, j, c0, c1, _ = pieces[p]
        return PS.at[zz, xp] if p == 0 else W.at[l, zz, xp, :, c0:c1]

    def ag_z(p, zz, xp, to, i, ss, rs):
        return rcopy(ag_slot(p, zz, xp), ag_slot(p, zz, xp), ss.at[p, i], rs.at[p, zz], (2 * to + xx, s))

    def ag_x(p, zz, xp):
        return rcopy(ag_slot(p, zz, xp), ag_slot(p, zz, xp), agx_s.at[p, zz], agx_r.at[p, zz], xdev)

    def ag_issue(p):
        l, j, _, _, x_first = pieces[p]
        ag_load(p)
        for k in range(1, M):
            when(direct[k], ag_z(p, z, xx, zof[k], k, agz_s, agz_r).start)
        if not x_first:
            ag_x(p, z, xx).start()
            return
        ag_x(p, z, 1 - xx).wait_recv()
        for k in range(1, M):
            when(direct[k], ag_z(p, z, 1 - xx, zof[k], k, agw_s, agw_r).start)

    def ag_load(p):
        l, j = pieces[p][:2]
        if p > 0 and (l, j) not in loaded:
            own_wait(l, j)
            loaded.add((l, j))

    def ag_turned(l):
        for p in range(NP):
            if pieces[p][4] and pieces[p][0] == l:
                ag_load(p)
                ag_x(p, z, xx).start()

    loaded = set()
    queue = []
    for p in range(NP):
        queue += [(p, i) for i in range(M - 1)]
    state = {"next": 0, "issued": 0}

    def ag_issue_to(n):
        while state["issued"] < min(n, NP):
            ag_issue(state["issued"])
            state["issued"] += 1

    def ag_service(n):
        for _ in range(n):
            if state["next"] == len(queue):
                return
            p, i = queue[state["next"]]
            x_first = pieces[p][4]
            ag_issue_to(p + 1)
            zz = near_of[i]
            got = [(xx, agz_s, agz_r)] + ([(1 - xx, agw_s, agw_r)] if x_first else [])
            for xp, ss, rs in got:
                ag_z(p, zz, xp, zz, 0, ss, rs).wait_recv()
                if not x_first:
                    ag_x(p, zz, xp).start()
                if i == M - 2 and cfg["relay"]:
                    when(relays, ag_z(p, zz, xp, relay_to, 0, ss, rs).start)
            state["next"] += 1
            if i == M - 2:
                ag_issue_to(p + 1 + cfg["ahead"])

    def ag_finish(p):
        while state["next"] < len(queue) and queue[state["next"]][0] <= p:
            ag_service(1)
        for q in range(p + 1):
            if q not in finished:
                finished.add(q)
                if not pieces[q][4]:
                    for zz in range(M):
                        ag_x(q, zz, 1 - xx).wait_recv()

    finished = set()

    def ag_drain(first, last):
        for p in range(first, last):
            x_first = pieces[p][4]
            for ss, rs in [(agz_s, agz_r)] + ([(agw_s, agw_r)] if x_first else []):
                for k in range(1, M):
                    when(direct[k], ag_z(p, z, xx, zof[k], k, ss, rs).wait_send)
                if cfg["relay"]:
                    when(relays, ag_z(p, z, xx, relay_to, 0, ss, rs).wait_send)
            for zz in [z] if x_first else range(M):
                ag_x(p, zz, xx).wait_send()

    for l in range(L):
        for j in range(4):
            own_load(l, j)
    for l in range(L):
        PS[z, xx, 12 * l:12 * l + 2, :] = gains_ref[l].astype(F32)
        PS[z, xx, 12 * l + 2:12 * l + 8, :] = biases_ref[l].astype(F32)
        for i in range(S):
            PS[z, xx, 12 * l + 8 + i:12 * l + 9 + i, :] = bfc_ref[l:l + 1, RB * i:RB * i + RB].astype(F32)
    row = mask_ref[...].astype(F32)
    MK[s] = jnp.zeros_like(MK[s])
    MK[s, 0:1, 0:T] = row
    ag_issue_to(1)
    mks = [rcopy(MK.at[s], MK.at[s], mk_s.at[i], mk_r.at[i], dev) for i, dev in enumerate((core, ydev, diag))]
    for c in mks:
        c.start()
    ag_issue_to(1 + cfg["ahead"])
    ag_turned(0)
    diagonal = lax.broadcasted_iota(jnp.int32, (T, T), 0) == lax.broadcasted_iota(jnp.int32, (T, T), 1)
    TV[...] = jnp.zeros_like(TV)
    TV[0:T, :] = jnp.broadcast_to(
        jnp.sum(jnp.where(diagonal, row, 0.0), axis=1, keepdims=True) * valid_ref[0].astype(F32), (T, 128))
    H[0] = jnp.zeros((TP, D), F32)
    H[0, 0:T, :] = x_ref[...].astype(F32)
    SGF[...] = jnp.zeros_like(SGF)
    SG[...] = jnp.zeros_like(SG)
    STAT[...] = jnp.zeros_like(STAT)
    for i, c in enumerate(mks):
        c.wait_send()
        rcopy(MK.at[s], MK.at[(core, ydev, diag)[i][1]], mk_s.at[i], mk_r.at[i], (core, ydev, diag)[i]).wait_recv()
    MR[...] = jnp.concatenate([MK[i, :, 0:TP] for i in range(S)], axis=1)
    ag_finish(0)
    for i in range(M):
        for j in range(2):
            PR[:, 128 * (2 * i + j):128 * (2 * i + j) + 128] = PS[i, j]

    DH[...] = jnp.zeros_like(DH)
    DH[0:T, :] = cot_ref[...].astype(F32) * TV[0:T, 0:1]

    def prow(l, i):
        return PR[12 * l + i:12 * l + i + 1, :]

    def prow_cols(l, i):
        return PR[12 * l + i:12 * l + i + 1, pl.ds(pl.multiple_of(C * s, C), C)]

    HB = TP // 2

    def ge_part(e, buf, i, h):
        rows = pl.ds(h * HB, HB)
        if i == 0:
            return rcopy(buf.at[s, rows], buf.at[s, rows], ge_s.at[e, 0, h], ge_r.at[e, 0, h], core)
        if i == 1:
            return rcopy(buf.at[s, rows], buf.at[s, rows], ge_s.at[e, 1, h], ge_r.at[e, 1, h], ydev)
        return rcopy(buf.at[ydev[1], rows], buf.at[ydev[1], rows], ge_s.at[e, 2, h], ge_r.at[e, 2, h], core)

    def ge_send(e, buf, h):
        ge_part(e, buf, 1, h).start()
        ge_part(e, buf, 0, h).start()

    def ge_end(e, buf):
        for h in range(2):
            rcopy(buf.at[s, pl.ds(h * HB, HB)], buf.at[ydev[1], pl.ds(h * HB, HB)],
                  ge_s.at[e, 1, h], ge_r.at[e, 1, h], ydev).wait_recv()
            ge_part(e, buf, 2, h).start()
        for h in range(2):
            rcopy(buf.at[s, pl.ds(h * HB, HB)], buf.at[core[1], pl.ds(h * HB, HB)],
                  ge_s.at[e, 0, h], ge_r.at[e, 0, h], core).wait_recv()
        for h in range(2):
            rcopy(buf.at[ydev[1], pl.ds(h * HB, HB)], buf.at[diag[1], pl.ds(h * HB, HB)],
                  ge_s.at[e, 2, h], ge_r.at[e, 2, h], core).wait_recv()
        for i in range(3):
            for h in range(2):
                ge_part(e, buf, i, h).wait_send()

    def re_copy(e, i, h):
        b = e % 2
        rows = pl.ds(h * HB, HB)
        if i == 0:
            return rcopy(PB.at[b, 1 - ypos, 1 - cpos, rows], R0.at[b, rows], re_s.at[e, 0, h], re_r.at[e, 0, h], core)
        if i == 1:
            return rcopy(PB.at[b, 1 - ypos, cpos, rows], R1.at[b, rows], re_s.at[e, 1, h], re_r.at[e, 1, h], ydev)
        return rcopy(PB.at[b, ypos, 1 - cpos, rows], R2.at[b, rows], re_s.at[e, 2, h], re_r.at[e, 2, h], core)

    def re_run(e, partial):
        b = e % 2
        partial(1 - ypos, b)
        for h in range(2):
            re_copy(e, 0, h).start()
        for h in range(2):
            re_copy(e, 0, h).wait_recv()
            for r0 in range(h * HB, h * HB + HB, 16):
                PB[b, 1 - ypos, cpos, r0:r0 + 16, :] = (
                    PB[b, 1 - ypos, cpos, r0:r0 + 16, :].astype(F32) + R0[b, r0:r0 + 16, :].astype(F32)).astype(BF16)
            re_copy(e, 1, h).start()
        partial(ypos, b)
        for h in range(2):
            re_copy(e, 2, h).start()

    def re_half(e, h):
        for i in (2, 1):
            re_copy(e, i, h).wait_recv()

    def re_sent(e):
        for i in range(3):
            for h in range(2):
                re_copy(e, i, h).wait_send()

    def re_rows(e, rows):
        b = e % 2
        return (PB[b, ypos, cpos, rows, :].astype(F32) + R2[b, rows, :].astype(F32)) + R1[b, rows, :].astype(F32)

    def partial_of(lhs, rhs, cb):
        def run(chip, b):
            def tile(j, _):
                cols = pl.ds(pl.multiple_of(j * C, C), C)
                r = ddot(lhs(chip), rhs(j), 1, cb).astype(BF16)
                PB[b, chip, :, :, cols] = r.reshape(2, TP, C)
                return 0
            lax.fori_loop(0, S, tile, 0)
        return run

    def row_loop(body, init, before=None, after=None):
        for h in range(2):
            if before is not None:
                before(h)

            def one(i, carry):
                return body(pl.ds(pl.multiple_of(h * HB + i * 16, 16), 16), carry)
            init = lax.fori_loop(0, HB // 16, one, init, unroll=cfg["unroll"])
            if after is not None:
                after(h)
        return init

    def norm(v):
        center = v - jnp.mean(v, -1, keepdims=True)
        inverse = lax.rsqrt(jnp.mean(center * center, -1, keepdims=True) + epsilon)
        return center * inverse, inverse

    def fold(v):
        return v[0:8] + v[8:16]

    def col_sum(v):
        return jnp.sum(v, axis=0, keepdims=True)

    lane_low = lax.broadcasted_iota(jnp.int32, (1, 2 * HEAD_DIM), 1) < HEAD_DIM
    lane_idx = lax.broadcasted_iota(jnp.int32, (1, 128), 1)

    def attend(l, pair):
        def block(i, _):
            rows = pl.ds(pl.multiple_of(i * TP, 16), TP)
            q = QKV[l, rows, 128 * pair:128 * pair + 128]
            k = QKV[l, :, C + 128 * pair:C + 128 * pair + 128]
            v = QKV[l, :, 2 * C + 128 * pair:2 * C + 128 * pair + 128]
            outs, lses = [], []
            for h in range(2):
                keep = lane_low if h == 0 else jnp.logical_not(lane_low)
                qh = jnp.where(keep, q, jnp.zeros_like(q))
                sc = ddot(qh, k, 1, 1) * SCALE
                sc = jnp.where(MR[0:1, :] > 0, sc, NEG)
                mx = jnp.max(sc, -1, keepdims=True)
                ex = jnp.exp(sc - mx)
                tot = jnp.sum(ex, -1, keepdims=True)
                outs.append(ddot(ex.astype(BF16), v, 1, 0) / tot)
                lses.append(mx + jnp.log(tot))
            OB[l, rows, 128 * pair:128 * pair + 128] = jnp.where(lane_low, outs[0], outs[1]).astype(BF16)
            held = jnp.where(lane_idx == 2 * pair, lses[0], lses[1])
            LSE[l, rows, :] = held if pair == 0 else jnp.where(lane_idx < 2 * pair, LSE[l, rows, :], held)
            return 0
        lax.fori_loop(0, S, block, 0)

    def attend_back(l, pair):
        DKV[...] = jnp.zeros_like(DKV)

        def block(i, _):
            rows = pl.ds(pl.multiple_of(i * TP, 16), TP)
            q = QKV[l, rows, 128 * pair:128 * pair + 128]
            k = QKV[l, :, C + 128 * pair:C + 128 * pair + 128]
            v = QKV[l, :, 2 * C + 128 * pair:2 * C + 128 * pair + 128]
            do = DO[rows, 128 * pair:128 * pair + 128]
            lse = LSE[l, rows, :]
            dqs = []
            dk = dv = None
            for h in range(2):
                keep = lane_low if h == 0 else jnp.logical_not(lane_low)
                qh = jnp.where(keep, q, jnp.zeros_like(q))
                doh = jnp.where(keep, do, jnp.zeros_like(do))
                sc = ddot(qh, k, 1, 1) * SCALE
                sc = jnp.where(MR[0:1, :] > 0, sc, NEG)
                p = jnp.exp(sc - lse[:, 2 * pair + h:2 * pair + h + 1])
                dp = ddot(doh, v, 1, 1)
                inner = jnp.sum(p * dp, -1, keepdims=True)
                ds = (p * (dp - inner)).astype(BF16)
                dqs.append(ddot(ds, k, 1, 0))
                dkh = ddot(ds, qh, 0, 0)
                dvh = ddot(p.astype(BF16), doh, 0, 0)
                dk = dkh if dk is None else dk + dkh
                dv = dvh if dv is None else dv + dvh
            DQKV[rows, 128 * pair:128 * pair + 128] = (jnp.where(lane_low, dqs[0], dqs[1]) * SCALE).astype(BF16)
            DKV[0] += dk
            DKV[1] += dv
            return 0
        lax.fori_loop(0, S, block, 0)
        DQKV[:, C + 128 * pair:C + 128 * pair + 128] = (DKV[0] * SCALE).astype(BF16)
        DQKV[:, 2 * C + 128 * pair:2 * C + 128 * pair + 128] = DKV[1].astype(BF16)

    peers = (core, ydev, diag)

    def wo_copy(l, i):
        to = peers[i][1]
        return rcopy(W.at[l, to, :, :, COLS[OUT]:COLS[FC1]], WO.at[l, :, :, pl.ds(pl.multiple_of(C * s, C), C)],
                     wo_s.at[l, i], wo_r.at[l, i], peers[i])

    def wo_start(l):
        for i in range(3):
            wo_copy(l, i).start()
        WO[l, :, :, pl.ds(pl.multiple_of(C * s, C), C)] = W[l, s, :, :, COLS[OUT]:COLS[FC1]]

    def wo_end(l):
        for i in range(3):
            wo_copy(l, i).wait()

    def gw_copy(l, i):
        to = peers[i][1]
        return rcopy(WO.at[l, :, :, pl.ds(pl.multiple_of(C * to, C), C)], W.at[l, s, :, :, COLS[OUT]:COLS[FC1]],
                     gw_s.at[l, i], gw_r.at[l, i], peers[i])

    def gw_start(l):
        for i in range(3):
            gw_copy(l, i).start()
        W[l, s, :, :, COLS[OUT]:COLS[FC1]] = WO[l, :, :, pl.ds(pl.multiple_of(C * s, C), C)]

    def gw_end(l):
        for i in range(3):
            gw_copy(l, i).wait()

    def wtile(l, j, a, b):
        n = M // S
        if n == 1:
            return W[l, j, :, :, a:b].reshape(2 * RB, b - a)
        return W[l, pl.ds(j * n, n), :, :, a:b].reshape(2 * RB * n, b - a)

    def grad_of(l, j):
        return GF if (l, j) == (L - 1, FC2) else W.at[l]

    def GC(l, j):
        return slice(0, D) if (l, j) == (L - 1, FC2) else slice(COLS[j], COLS[j + 1])

    at_end = edge == 0
    block_of = [jnp.where(at_end, near_of[M - 2 - i], near_of[i]) for i in range(M - 1)] + [z]
    first_to = jnp.where(at_end, near_of[0], block_of[0])
    first_slot = jnp.where(at_end, near_of[0], z)

    def rx_copy(l, j, k):
        a, b = COLS[j], COLS[j + 1]
        zz = block_of[k]
        return rcopy(grad_of(l, j).at[zz, 1 - xx, :, GC(l, j)], XR.at[l, zz, :, a:b], rx_s.at[l, j, k], rx_r.at[l, j, k], xdev)

    def rz_copy(l, j, k):
        a, b = COLS[j], COLS[j + 1]
        to, slot = (first_to, first_slot) if k == 0 else (block_of[k], z)
        return rcopy(XR.at[l, block_of[k], :, a:b], ZR.at[l, slot, :, a:b], rz_s.at[l, j, k], rz_r.at[l, j, slot], (2 * to + xx, s))

    def rz_recv(l, j, slot):
        a, b = COLS[j], COLS[j + 1]
        return rcopy(XR.at[l, z, :, a:b], ZR.at[l, slot, :, a:b], rz_s.at[l, j, 0], rz_r.at[l, j, slot], xdev)

    def whole_of(l, j):
        return XR.at[l, z, :, COLS[j]:COLS[j + 1]]

    def fo_start(l, j):
        for _, dst, c0, n in own_parts(l, j, s):
            src = XR.at[l, z, :, c0:c0 + n]
            for i in range(2):
                rcopy(src, dst, fo_s.at[l, j, i], fo_r.at[l, j, i], peers[i]).start()
            pltpu.make_async_copy(src, dst, loc_sem.at[l, j]).start()

    def fo_pass(l, j):
        rcopy(whole_of(l, j), whole_of(l, j), fo_s.at[l, j, 1], fo_r.at[l, j, 1], peers[1]).wait_recv()
        for _, dst, c0, n in own_parts(l, j, ydev[1]):
            rcopy(dst, dst, fo_s.at[l, j, 2], fo_r.at[l, j, 2], core).start()

    def fo_wait(l, j):
        for i in range(3):
            c = rcopy(whole_of(l, j), whole_of(l, j), fo_s.at[l, j, i], fo_r.at[l, j, i], peers[i])
            c.wait_send()
            if i != 1:
                c.wait_recv()
        pltpu.make_async_copy(whole_of(l, j), whole_of(l, j), loc_sem.at[l, j]).wait()

    def red_first(l, j, k):
        a, b = COLS[j], COLS[j + 1]
        rx_copy(l, j, k).wait_recv()
        zz = block_of[k]
        if k == M - 1:
            return
        for r0 in range(0, RB, 32):
            XR[l, zz, r0:r0 + 32, a:b] = (XR[l, zz, r0:r0 + 32, a:b].astype(F32) + grad_of(l, j)[zz, xx, r0:r0 + 32, GC(l, j)].astype(F32)).astype(BF16)
        if k == M - 2:
            @pl.when(jnp.logical_not(at_end))
            def _():
                rz_recv(l, j, z).wait_recv()
                for r0 in range(0, RB, 32):
                    XR[l, zz, r0:r0 + 32, a:b] = (XR[l, zz, r0:r0 + 32, a:b].astype(F32) + ZR[l, z, r0:r0 + 32, a:b].astype(F32)).astype(BF16)
        rz_copy(l, j, k).start()

    def red_second(l, j):
        a, b = COLS[j], COLS[j + 1]
        red_first(l, j, M - 1)

        def total(n):
            for i in range(n):
                rz_recv(l, j, near_of[i]).wait_recv()
            for r0 in range(0, RB, 32):
                t = XR[l, z, r0:r0 + 32, a:b].astype(F32) + grad_of(l, j)[z, xx, r0:r0 + 32, GC(l, j)].astype(F32)
                for i in range(n):
                    t = t + ZR[l, near_of[i], r0:r0 + 32, a:b].astype(F32)
                XR[l, z, r0:r0 + 32, a:b] = t.astype(BF16)
        pl.when(at_end)(lambda: total(M - 2))
        pl.when(jnp.logical_not(at_end))(lambda: total(M - 1))
        fo_start(l, j)

    def red_end(l, j):
        for k in range(M):
            rx_copy(l, j, k).wait_send()
        for k in range(M - 1):
            rz_copy(l, j, k).wait_send()
        fo_wait(l, j)

    events = []
    later, late = [], []
    done = {"n": 0}

    def red_later():
        if len(later) > 1:
            late.append(later.pop(0))
        if later:
            events.append((red_second,) + later[-1])

    def red_push(l, j):
        for k in range(M):
            rx_copy(l, j, k).start()
        events.extend((red_first, l, j, k) for k in range(M - 1))
        red_later()
        later.append((l, j))

    def red_service(n):
        for _ in range(n):
            if done["n"] >= len(events):
                return
            f, *a = events[done["n"]]
            done["n"] += 1
            f(*a)

    def norm_back(l, src, e, gain, buf=None, g=None):
        def one(rows, acc):
            n, r = norm(src[l, rows, :])
            dm = re_rows(e, rows)
            dn = dm * gain
            pm = jnp.mean(dn, -1, keepdims=True)
            cm = jnp.mean(dn * n, -1, keepdims=True)
            dh = DH[rows, :] + r * (dn - pm - n * cm)
            DH[rows, :] = dh
            sums = acc[0] + fold(dm * n), acc[1] + fold(dm)
            if buf is None:
                return sums
            v = dh.astype(BF16)
            buf[s, rows, :] = v
            return sums + (acc[2] + fold(v.astype(F32)),)
        zero = jnp.zeros((8, D), F32)
        out = row_loop(one, (zero,) * (2 if buf is None else 3), lambda h: re_half(e, h),
                       None if buf is None else lambda h: ge_send(g, buf, h))
        re_sent(e)
        return [col_sum(v) for v in out]

    def low_of(buf, g):
        def one(rows, acc):
            v = DH[rows, :].astype(BF16)
            buf[s, rows, :] = v
            return acc + fold(v.astype(F32))
        return col_sum(row_loop(one, jnp.zeros((8, D), F32), after=lambda h: ge_send(g, buf, h)))

    def forward(l):
        e = 2 * l
        fsv = cfg["fsv"]

        def ln1(rows, _):
            n, _r = norm(H[l, rows, :])
            AF[l, s, rows, :] = (n * prow(l, 0) + prow(l, 2)).astype(BF16)
            return 0
        row_loop(ln1, 0, after=lambda h: ge_send(e, AF.at[l], h))
        ag_service(fsv[0])
        ge_end(e, AF.at[l])
        ag_finish(last_of[l, QK])
        for n in range(3):
            r = ddot(AF[l].reshape(R, D), W[l, :, :, :, C * n:C * n + C].reshape(D, C), 1, 0)
            if n == 0:
                r = r + prow_cols(l, 3)
            if n == 2:
                r = r + prow_cols(l, 4)
            QKV[l, :, C * n:C * n + C] = r.astype(BF16)
        ag_finish(last_of[l, OUT])
        wo_start(l)
        if l == 0:
            SGF[12 * (L - 1) + 7:12 * (L - 1) + 8, :] = low_of(BF.at[0], 2 * L)
        attend(l, 0)
        ag_service(fsv[1])
        attend(l, 1)
        if l < L - 1:
            ag_turned(l + 1)
        ag_service(fsv[2])
        if l == 0:
            ge_end(2 * L, BF.at[0])
        wo_end(l)
        re_run(e + 0, partial_of(
            lambda chip: OB[l, pl.ds(pl.multiple_of(chip * 2 * TP, 16), 2 * TP), :],
            lambda j: WO[l, :, :, pl.ds(pl.multiple_of(j * C, C), C)].reshape(C, C), 0))
        ag_service(fsv[3])

        def post(rows, acc):
            hv = H[l, rows, :]
            br = re_rows(e + 0, rows) + prow(l, 5)
            mid = hv + br
            H2[l, rows, :] = mid
            n, _r = norm(mid)
            MF[l, s, rows, :] = (n * prow(l, 1) + prow(l, 6)).astype(BF16)
            t = TV[rows, 0:1]
            return acc[0] + fold(t * hv * hv), acc[1] + fold(t * br * br)
        zero = jnp.zeros((8, D), F32)
        s0, s1 = row_loop(post, (zero, zero), lambda h: re_half(e, h), lambda h: ge_send(e + 1, MF.at[l], h))
        re_sent(e)
        ag_service(fsv[4])
        ge_end(e + 1, MF.at[l])
        ag_finish(last_of[l, FC1])
        bias = PR[pl.ds(12 * l + 8 + s, 1), :]
        for j in range(FS // C):
            u = ddot(MF[l].reshape(R, D), W[l, :, :, :, COLS[FC1] + C * j:COLS[FC1] + C * j + C].reshape(D, C), 1, 0)
            u = u + bias[:, C * j:C * j + C]
            U[l, :, C * j:C * j + C] = u
            GW[:, C * j:C * j + C] = (u / (1.0 + jnp.exp(-1.702 * u))).astype(BF16)
        stat(3 * l, s0)
        stat(3 * l + 1, s1)
        if l == L - 1:
            for j in range(FS // C):
                GF[j, :, :, :] = ddot(GW[:, C * j:C * j + C], BF[0].reshape(R, D), 0, 0).astype(BF16).reshape(2, RB, D)
        ag_finish(last_of[l, FC2])
        if l == L - 1:
            red_push(l, FC2)
        re_run(e + 1, partial_of(
            lambda chip: GW[pl.ds(pl.multiple_of(chip * 2 * TP, 16), 2 * TP), :],
            lambda j: W[l, :, :, :, pl.ds(pl.multiple_of(COLS[FC2] + j * C, C), C)].reshape(FS, C), 0))

    def forward_end(l):
        e = 2 * l

        def last(rows, acc):
            out = re_rows(e + 1, rows) + prow(l, 7)
            res = H2[l, rows, :] + out
            H[l + 1, rows, :] = res
            t = TV[rows, 0:1]
            return acc + fold(t * out * out)
        ag_service(cfg["fsv"][5])
        stat(3 * l + 2, row_loop(last, jnp.zeros((8, D), F32), lambda h: re_half(e + 1, h)))
        re_sent(e + 1)

    def stat(i, v):
        STAT[...] = jnp.where(lane_idx == i, jnp.sum(col_sum(v), axis=1, keepdims=True), STAT[...])

    def backward(l):
        ge_a = re_a = 2 * L + 2 * (L - 1 - l)
        ge_b = re_b = ge_a + 1
        B0, B1 = BF.at[0], BF.at[1]
        svc = cfg["svc"][L - 1 - l]
        if l < L - 1:
            red_service(svc[0])
            ge_end(ge_a, B0)
        for j in range(FS // C):
            dg = ddot(BF[0].reshape(R, D), wtile(l, j, COLS[FC2], COLS[FC2] + D), 1, 1)
            u = U[l, :, C * j:C * j + C]
            sg = 1.0 / (1.0 + jnp.exp(-1.702 * u))
            if l < L - 1:
                GW[:, C * j:C * j + C] = (u * sg).astype(BF16)
            du = (dg * (sg + 1.702 * u * sg * (1.0 - sg))).astype(BF16)
            DU[:, C * j:C * j + C] = du
            SGF[pl.ds(12 * l + 8 + s, 1), C * j:C * j + C] = jnp.sum(du.astype(F32), axis=0, keepdims=True)
        red_service(svc[1])
        if l < L - 1:
            for j in range(FS // C):
                W[l, j, :, :, COLS[FC2]:COLS[FC2] + D] = ddot(GW[:, C * j:C * j + C], BF[0].reshape(R, D), 0, 0).astype(BF16).reshape(2, RB, D)
            red_push(l, FC2)
        re_run(re_a, partial_of(
            lambda chip: DU[pl.ds(pl.multiple_of(chip * 2 * TP, 16), 2 * TP), :],
            lambda j: wtile(l, j, COLS[FC1], COLS[FC1] + FS), 1))
        for j in range(S):
            W[l, j, :, :, COLS[FC1]:COLS[FC1] + FS] = ddot(MF[l, :, :, C * j:C * j + C].reshape(R, C), DU[...], 0, 0).astype(BF16).reshape(2, RB, FS)
        red_push(l, FC1)
        if l == L - 1:
            forward_end(l)
        red_service(svc[2])
        gg, bb, cc = norm_back(l, H2, re_a, prow(l, 1), B1, ge_b)
        SGF[12 * l + 1:12 * l + 2, :] = gg
        SGF[12 * l + 6:12 * l + 7, :] = bb
        SGF[12 * l + 5:12 * l + 6, :] = cc
        red_service(svc[3])
        ge_end(ge_b, B1)
        DO[...] = ddot(BF[1].reshape(R, D), WO[l].reshape(C, D), 1, 1).astype(BF16)
        for j in range(S):
            WO[l, :, :, C * j:C * j + C] = ddot(OB[l], BF[1, :, :, C * j:C * j + C].reshape(R, C), 0, 0).astype(BF16).reshape(2, RB, C)
        gw_start(l)
        attend_back(l, 0)
        red_service(svc[4])
        attend_back(l, 1)
        gw_end(l)
        red_push(l, OUT)
        red_service(svc[5])
        for i, (row, c0) in enumerate(((3, 0), (4, 2 * C))):
            SGF[12 * l + row:12 * l + row + 1, pl.ds(pl.multiple_of(C * s, C), C)] = jnp.sum(
                DQKV[:, c0:c0 + C].astype(F32), axis=0, keepdims=True)
        re_run(re_b, partial_of(
            lambda chip: DQKV[pl.ds(pl.multiple_of(chip * 2 * TP, 16), 2 * TP), :],
            lambda j: wtile(l, j, 0, 3 * C), 1))
        for j in range(S):
            W[l, j, :, :, 0:3 * C] = ddot(AF[l, :, :, C * j:C * j + C].reshape(R, C), DQKV[...], 0, 0).astype(BF16).reshape(2, RB, 3 * C)
        red_push(l, QK)
        red_service(svc[6])
        if l > 0:
            gg, bb, cc = norm_back(l, H, re_b, prow(l, 0), B0, ge_b + 1)
            SGF[12 * (l - 1) + 7:12 * (l - 1) + 8, :] = cc
        else:
            gg, bb = norm_back(l, H, re_b, prow(l, 0))
        SGF[12 * l + 0:12 * l + 1, :] = gg
        SGF[12 * l + 2:12 * l + 3, :] = bb
        red_service(svc[7])

    for l in range(L):
        forward(l)
        if l < L - 1:
            forward_end(l)
    ag_drain(0, last_of[L - 1, FC1] + 1)
    for l in reversed(range(L)):
        backward(l)
    gx_ref[...] = DH[0:T, :]
    y_ref[...] = H[L, 0:T, :].astype(BF16)
    STAT[...] = jnp.where(lane_idx == 3 * L, col_sum(TV[:, 0:1]), STAT[...])

    for i in range(M):
        for j in range(2):
            SG[i, j, 0:24, :] = SGF[0:24, 128 * (2 * i + j):128 * (2 * i + j) + 128]
            SG[i, j, 24:25, :] = STAT[...]
    sgx = rcopy(SG.at[:, 1 - xx], SX, st_s.at[0], st_r.at[0], xdev)
    sgx.start()

    def sz(k, frm):
        return rcopy(SX.at[zof[k]], SZ.at[zfrom[k] if frm else z], st_s.at[k], st_r.at[k], zdev[k])

    def stc(i, frm):
        slot = peers[i][1] if frm else s
        return rcopy(ST.at[s], ST.at[slot], st_s.at[M + i], st_r.at[M + i], peers[i])

    red_service(len(events))
    sgx.wait()
    SX[...] = SX[...] + SG[:, xx]
    SZ[z] = SX[z]
    for k in range(1, M):
        sz(k, False).start()
    red_later()
    red_service(len(events))
    for k in range(1, M):
        sz(k, True).wait_recv()
    tot = SZ[0]
    for k in range(1, M):
        tot = tot + SZ[k]
    ST[s] = tot
    for i in range(3):
        stc(i, False).start()
    for p in late + later:
        fo_pass(*p)
    for i in range(3):
        stc(i, True).wait_recv()
    tot = (ST[0] + ST[1]) + (ST[2] + ST[3])
    for l in range(L):
        ogain_ref[l] = tot[12 * l:12 * l + 2]
        obias_ref[l, 0:1, :] = tot[12 * l + 2:12 * l + 3]
        obias_ref[l, 1:5, :] = tot[12 * l + 4:12 * l + 8]
        oquery_ref[l:l + 1, :] = tot[12 * l + 3:12 * l + 4]
        for i in range(S):
            obfc_ref[l:l + 1, RB * i:RB * i + RB] = tot[12 * l + 8 + i:12 * l + 9 + i]
    sums = tot[12 * L:12 * L + 1]
    root = jnp.sqrt(sums / (jnp.maximum(sums[:, 3 * L:3 * L + 1], 1.0) * D))
    for l in range(L):
        rms_ref[l:l + 1, :] = root[:, 3 * l:3 * l + 3]
    for k in range(1, M):
        sz(k, False).wait_send()
    for i in range(3):
        stc(i, False).wait_send()
    ag_drain(last_of[L - 1, FC1] + 1, NP)
    for l in reversed(range(L)):
        for j in (FC2, FC1, OUT, QK):
            red_end(l, j)


def fused_local(cfg, block_input, key_mask, valid, gains, biases, w_qkv, w_out, w_fc1, b_fc1, w_fc2, cotangent):
    L, M, RB, T, TP, D, NC, FS = (cfg[n] for n in ("L", "M", "RB", "T", "TP", "D", "NC", "FS"))
    S, dp = 4, 2 * M
    C = D // S
    R = S * TP
    vm = pl.BlockSpec(memory_space=pltpu.VMEM)
    hbm = pl.BlockSpec(memory_space=pl.ANY)
    dma = pltpu.SemaphoreType.DMA
    v = pltpu.VMEM
    NP, NE = 1 + sum(cfg["cuts"]) * L, 4 * L
    out = pl.pallas_call(
        partial(fused_kernel, cfg),
        out_shape=(
            jax.ShapeDtypeStruct((T, D), BF16),
            jax.ShapeDtypeStruct((T, D), F32),
            jax.ShapeDtypeStruct((L, 3), F32),
            jax.ShapeDtypeStruct((L, 2, RB), F32),
            jax.ShapeDtypeStruct((L, 5, RB), F32),
            jax.ShapeDtypeStruct((L, RB), F32),
            jax.ShapeDtypeStruct((L, S * RB), F32),
            jax.ShapeDtypeStruct(w_qkv.shape, BF16),
            jax.ShapeDtypeStruct(w_out.shape, BF16),
            jax.ShapeDtypeStruct(w_fc1.shape, BF16),
            jax.ShapeDtypeStruct(w_fc2.shape, BF16),
        ),
        in_specs=[vm, vm, pl.BlockSpec(memory_space=pltpu.SMEM), vm, vm, vm, vm, hbm, hbm, hbm, hbm],
        out_specs=(vm,) * 7 + (hbm,) * 4,
        scratch_shapes=[
            v((L, M, 2, RB, NC), BF16),
            v((L, 2, RB, D), BF16),
            v((L, M, RB, NC), BF16),
            v((L, M, RB, NC), BF16),
            v((L, S, TP, D), BF16),
            v((L, R, 3 * C), BF16),
            v((L, R, C), BF16),
            v((L, S, TP, D), BF16),
            v((L, R, FS), F32),
            v((L + 1, TP, D), F32),
            v((L, TP, D), F32),
            v((L, R, 128), F32),
            v((M, 2, RB, D), BF16),
            v((2, S, TP, D), BF16),
            v((2, 2, 2, TP, D), BF16),
            v((2, TP, D), BF16),
            v((2, TP, D), BF16),
            v((2, TP, D), BF16),
            v((R, FS), BF16),
            v((R, FS), BF16),
            v((R, 3 * C), BF16),
            v((R, C), BF16),
            v((2, R, 128), F32),
            v((TP, D), F32),
            v((S, 8, -(-TP // 128) * 128), F32),
            v((8, R), F32),
            v((TP, 128), F32),
            v((M, 2, 12 * L, RB), F32),
            v((12 * L, D), F32),
            v((12 * L, D), F32),
            v((M, 2, 32, RB), F32),
            v((M, 32, RB), F32),
            v((M, 32, RB), F32),
            v((S, 32, RB), F32),
            v((1, RB), F32),
            dma((L, 4)),
            dma((NP, M)), dma((NP, M)), dma((NP, M)), dma((NP, M)), dma((NP, M)), dma((NP, M)),
            dma((NE, 3, 2)), dma((NE, 3, 2)), dma((NE, 3, 2)), dma((NE, 3, 2)),
            dma((L, 3)), dma((L, 3)), dma((L, 3)), dma((L, 3)),
            dma((L, 4, M)), dma((L, 4, M)), dma((L, 4, M)), dma((L, 4, M)),
            dma((L, 4, 3)), dma((L, 4, 3)), dma((3,)), dma((3,)), dma((M + 3,)), dma((M + 3,)),
        ],
        compiler_params=pltpu.CompilerParams(
            collective_id=0, has_side_effects=True, vmem_limit_bytes=cfg["vmem"]),
        cost_estimate=pl.CostEstimate(flops=24_000_000_000, bytes_accessed=20_000_000, transcendentals=0),
    )(block_input[0], key_mask, valid, gains, biases, b_fc1, cotangent[0], w_qkv, w_out, w_fc1, w_fc2)
    y, gx, rms, o_gain, o_bias, o_query, o_bfc, o_qkv, o_out, o_fc1, o_fc2 = out
    return (y[None], gx[None], rms, o_gain, o_bias, o_query,
            o_qkv.astype(F32), o_out.astype(F32), o_fc1.astype(F32), o_bfc, o_fc2.astype(F32))


def local(*args):
    block_input, w_qkv, w_fc2 = args[0], args[5], args[9]
    L, RB = w_qkv.shape[:2]
    T, D = block_input.shape[1:]
    S, dp = lax.axis_size("seq"), lax.axis_size("dp")
    FS = w_fc2.shape[1] * dp // S
    fits = (S == 4 and dp == 2 * S and RB % 128 == 0 and D // S == 2 * RB and L * 12 + 1 <= 32
            and FS // dp == RB and HEAD_DIM * 2 == 128 and D // S == 4 * HEAD_DIM and block_input.shape[0] == 1)
    if not fits:
        return plain_local(*args)
    cfg = dict(L=L, M=dp // 2, RB=RB, T=T, TP=-(-T // 16) * 16, D=D, NC=D + 2 * FS, FS=FS, ahead=3, unroll=5, cuts=(2, 1, 2, 2), turned=((), (), (), (0,)), relay=True, fsv=(6, 2, 2, 3, 5, 4), vmem=62 * 2**20,
               svc=((0, 0, 3, 2, 2, 0, 3, 1),) + ((4, 0, 2, 2, 1, 2, 3, 0),) * (L - 1))
    return fused_local(cfg, *args)


def solution(mesh):
    return jax.shard_map(
        local,
        mesh=mesh,
        in_specs=(
            P("dp", "seq", None),
            P("dp", "seq"),
            P("dp"),
            P(None, None, "dp"),
            P(None, None, "dp"),
            P(None, "dp", None),
            P(None, "dp", None),
            P(None, "dp", None),
            P(None, "dp"),
            P(None, "dp", None),
            P("dp", "seq", None),
        ),
        out_specs=(
            P("dp", "seq", None),
            P("dp", "seq", None),
            P(),
            P(None, None, "dp"),
            P(None, None, "dp"),
            P(None, "dp"),
            P(None, "dp", None),
            P(None, "dp", None),
            P(None, "dp", None),
            P(None, "dp"),
            P(None, "dp", None),
        ),
        check_vma=False,
    )
```

```python
from functools import partial
import math

import jax
import jax.numpy as jnp
from jax import lax
from jax.experimental import pallas as pl
from jax.experimental.pallas import tpu as pltpu
from jax.sharding import PartitionSpec as P

HEADS = 16
HEAD_DIM = 64
F32 = jnp.float32
BF16 = jnp.bfloat16

epsilon = 1e-05


def norm_parts(values_in, gain, shift):
    center = values_in - jnp.mean(values_in, -1, keepdims=True)
    inverse = lax.rsqrt(jnp.mean(center * center, -1, keepdims=True) + epsilon)
    normal = center * inverse
    return (normal * gain + shift, normal, inverse)


def norm_back(grad_output, normal, inverse, gain):
    grad_gain = jnp.sum(grad_output * normal, 0)
    grad_shift = jnp.sum(grad_output, 0)
    grad_norm = grad_output * gain
    plain_mean = jnp.mean(grad_norm, -1, keepdims=True)
    cross_mean = jnp.mean(grad_norm * normal, -1, keepdims=True)
    return (grad_gain, grad_shift, inverse * (grad_norm - plain_mean - normal * cross_mean))


def dot(a, b, ca=1, cb=0):
    return lax.dot_general(a, b, (((ca,), (cb,)), ((), ())), preferred_element_type=F32)


def split_heads(x, width):
    return x.reshape(x.shape[0], width // HEAD_DIM, HEAD_DIM)


def scores_of(query, keys, mask_row, scale):
    scores = jnp.einsum("qhd,khd->hqk", query, keys, preferred_element_type=F32) * scale
    return jnp.where(mask_row[None, None, :] > 0, scores, -1000000000.0)


def gather_rows(x):
    return lax.all_gather(x, "seq", axis=0, tiled=True)


def scatter_rows(x):
    return lax.psum_scatter(x.astype(BF16), "seq", scatter_dimension=0, tiled=True).astype(F32)


def forward_layer(hidden, weights, params, mask_row, tok_valid):
    w_qkv, w_out, w_fc1, w_fc2 = weights
    gains, biases, bias_q, bias_v, b_fc1 = params
    scale = 1.0 / math.sqrt(HEAD_DIM)
    width = w_out.shape[0]
    normed, normal_one, inverse_one = norm_parts(hidden, gains[0], biases[0])
    normed_all = gather_rows(normed.astype(BF16))
    packed = dot(normed_all, w_qkv)
    packed = (packed + jnp.concatenate([bias_q, jnp.zeros_like(bias_q), bias_v])).astype(BF16)
    query, keys, values = (split_heads(packed[:, i * width : (i + 1) * width], width) for i in range(3))
    scores = scores_of(query, keys, mask_row, scale)
    row_max = jnp.max(scores, -1, keepdims=True)
    log_total = row_max + jnp.log(jnp.sum(jnp.exp(scores - row_max), -1, keepdims=True))
    probs = jnp.exp(scores - log_total).astype(BF16)
    mixed = jnp.einsum("hqk,khd->qhd", probs, values, preferred_element_type=F32).astype(BF16)
    mixed = mixed.reshape(mixed.shape[0], width)
    branch = scatter_rows(dot(mixed, w_out)) + biases[3]
    middle = hidden + branch
    normed_two, normal_two, inverse_two = norm_parts(middle, gains[1], biases[4])
    normed_two_all = gather_rows(normed_two.astype(BF16))
    inner = dot(normed_two_all, w_fc1) + b_fc1
    gate_sig = jax.nn.sigmoid(1.702 * inner)
    gated = (inner * gate_sig).astype(BF16)
    output = scatter_rows(dot(gated, w_fc2)) + biases[5]
    stat = jnp.stack([jnp.sum(tok_valid * jnp.sum(v * v, -1)) for v in (hidden, branch, output)])
    stored = (normal_one, inverse_one, normed_all, query, keys, values, log_total, mixed,
              normal_two, inverse_two, normed_two_all, inner, gate_sig, gated)
    return (middle + output, stored, stat)


def backward_layer(grad_result, weights, params, stored, mask_row):
    w_qkv, w_out, w_fc1, w_fc2 = weights
    gains = params[0]
    scale = 1.0 / math.sqrt(HEAD_DIM)
    (normal_one, inverse_one, normed_all, query, keys, values, log_total, mixed,
     normal_two, inverse_two, normed_two_all, inner, gate_sig, gated) = stored
    out_low = grad_result.astype(BF16)
    grad_bias_five = jnp.sum(out_low.astype(F32), 0)
    out_all = gather_rows(out_low)
    grad_fc2 = dot(gated, out_all, 0, 0)
    grad_gated = dot(out_all, w_fc2, 1, 1)
    grad_inner = (grad_gated * (gate_sig + 1.702 * inner * gate_sig * (1.0 - gate_sig))).astype(BF16)
    grad_bias_fc1 = jnp.sum(grad_inner.astype(F32), 0)
    grad_fc1 = dot(normed_two_all, grad_inner, 0, 0)
    grad_normed_two = scatter_rows(dot(grad_inner, w_fc1, 1, 1))
    grad_gain_two, grad_shift_two, grad_middle = norm_back(grad_normed_two, normal_two, inverse_two, gains[1])
    grad_middle = grad_middle + grad_result
    branch_low = grad_middle.astype(BF16)
    grad_bias_three = jnp.sum(branch_low.astype(F32), 0)
    branch_all = gather_rows(branch_low)
    grad_out = dot(mixed, branch_all, 0, 0)
    width = w_out.shape[0]
    grad_mixed = split_heads(dot(branch_all, w_out, 1, 1).astype(BF16), width)
    scores = scores_of(query, keys, mask_row, scale)
    probs = jnp.exp(scores - log_total)
    grad_probs = jnp.einsum("qhd,khd->hqk", grad_mixed, values, preferred_element_type=F32)
    inner_sum = jnp.sum(probs * grad_probs, -1, keepdims=True)
    grad_scores = (probs * (grad_probs - inner_sum)).astype(BF16)
    grad_q = (jnp.einsum("hqk,khd->qhd", grad_scores, keys, preferred_element_type=F32) * scale).astype(BF16)
    grad_k = (jnp.einsum("hqk,qhd->khd", grad_scores, query, preferred_element_type=F32) * scale).astype(BF16)
    grad_v = jnp.einsum("hqk,qhd->khd", probs.astype(BF16), grad_mixed, preferred_element_type=F32).astype(BF16)
    rows = grad_q.shape[0]
    grad_proj = jnp.concatenate([g.reshape(rows, width) for g in (grad_q, grad_k, grad_v)], 1)
    grad_bias_proj = jnp.sum(grad_proj.astype(F32), 0)
    grad_qkv = dot(normed_all, grad_proj, 0, 0)
    grad_normed = scatter_rows(dot(grad_proj, w_qkv, 1, 1))
    grad_gain_one, grad_shift_one, grad_hidden = norm_back(grad_normed, normal_one, inverse_one, gains[0])
    grad_hidden = grad_hidden + grad_middle
    rows_sum = jnp.stack([grad_gain_one, grad_gain_two, grad_shift_one, grad_bias_three, grad_shift_two, grad_bias_five])
    return (grad_hidden, (grad_qkv, grad_out, grad_fc1, grad_fc2), rows_sum, grad_bias_proj, grad_bias_fc1)


def plain_local(block_input, key_mask, valid, gains, biases, w_qkv, w_out, w_fc1, b_fc1, w_fc2, cotangent):
    layers = w_qkv.shape[0]
    groups = lax.axis_size("seq")
    shards = lax.axis_size("dp")
    me = lax.axis_index("seq")
    width = block_input.shape[2]
    hidden_width = w_fc2.shape[1] * shards
    part = width // groups
    images = block_input.shape[0]
    assert images == 1
    mask_row = lax.all_gather(key_mask, "seq", axis=1, tiled=True)[0]
    tok_valid = (key_mask * valid[:, None]).astype(F32)[0]
    hidden = block_input[0].astype(F32)
    small = jnp.concatenate([gains.reshape(layers, -1), biases.reshape(layers, -1), b_fc1], 1)
    small = lax.all_gather(small, "dp", axis=0).astype(F32)
    n_g, n_b = gains.shape[1] * gains.shape[2], biases.shape[1] * biases.shape[2]
    gains_all = small[:, :, :n_g].reshape(shards, layers, 2, -1).transpose(1, 2, 0, 3).reshape(layers, 2, width)
    biases_all = small[:, :, n_g : n_g + n_b].reshape(shards, layers, 6, -1).transpose(1, 2, 0, 3).reshape(layers, 6, width)
    fc_all = small[:, :, n_g + n_b :].transpose(1, 0, 2).reshape(layers, shards, groups, -1)
    fc_mine = lax.dynamic_index_in_dim(fc_all, me, 2, False).reshape(layers, -1)
    proj_mine = lax.dynamic_index_in_dim(biases_all.reshape(layers, 6, groups, part), me, 2, False)

    def columns(w, outer):
        view = w.reshape(w.shape[0], outer, groups, -1)
        return lax.dynamic_index_in_dim(view, me, 2, False).reshape(w.shape[0], -1)

    def rows_of(w):
        view = w.reshape(groups, -1, w.shape[1])
        return lax.dynamic_index_in_dim(view, me, 0, False)

    def gather(w):
        return lax.all_gather(w, "dp", axis=0, tiled=True)

    weights, params, stored_all, stats = [], [], [], []
    for layer in range(layers):
        weights.append((
            gather(columns(w_qkv[layer], 3)),
            rows_of(gather(w_out[layer])),
            gather(columns(w_fc1[layer], shards)),
            gather(rows_of(w_fc2[layer])),
        ))
        params.append((gains_all[layer], biases_all[layer], proj_mine[layer, 1], proj_mine[layer, 2], fc_mine[layer]))
    for layer in range(layers):
        hidden, stored, stat = forward_layer(hidden, weights[layer], params[layer], mask_row, tok_valid)
        stored_all.append(stored)
        stats.append(stat)
    totals = lax.psum(jnp.concatenate([jnp.stack(stats).reshape(-1), jnp.sum(tok_valid)[None]]), ("dp", "seq"))
    rms = jnp.sqrt(totals[:-1].reshape(layers, 3) / (jnp.maximum(totals[-1], 1.0) * width))

    grad_hidden = cotangent[0].astype(F32) * tok_valid[:, None]
    big = [None] * layers
    sums = [None] * layers
    for layer in reversed(range(layers)):
        grad_hidden, grads, rows_sum, grad_proj, grad_fc = backward_layer(
            grad_hidden, weights[layer], params[layer], stored_all[layer], mask_row
        )
        g_qkv, g_out, g_fc1, g_fc2 = (g.astype(BF16) for g in grads)
        g_out = lax.all_to_all(g_out, "seq", split_axis=1, concat_axis=0, tiled=True)

        def reduce_(g):
            g = lax.psum_scatter(g, "dp", scatter_dimension=0, tiled=True)
            return lax.all_gather(g, "seq", axis=0)

        def join(g, outer):
            view = g.reshape(groups, g.shape[1], outer, -1)
            return view.transpose(1, 2, 0, 3).reshape(g.shape[1], -1)

        big[layer] = (
            join(reduce_(g_qkv), 3).astype(F32),
            join(reduce_(g_out), 1).astype(F32),
            join(reduce_(g_fc1), shards).astype(F32),
            reduce_(g_fc2).reshape(w_fc2.shape[1], -1).astype(F32),
        )
        proj = lax.dynamic_update_slice(jnp.zeros((3, groups, part), F32), grad_proj.reshape(3, 1, part), (0, me, 0))
        fc = lax.dynamic_update_slice(jnp.zeros((shards, groups, hidden_width // (shards * groups)), F32),
                                      grad_fc.reshape(shards, 1, -1), (0, me, 0))
        sums[layer] = jnp.concatenate([
            rows_sum.reshape(6, shards, -1).transpose(1, 0, 2).reshape(shards, -1),
            proj.reshape(3, shards, -1).transpose(1, 0, 2).reshape(shards, -1),
            fc.reshape(shards, -1),
        ], 1)
    flat = jnp.stack(sums, 1).astype(F32)
    flat = lax.psum(lax.psum_scatter(flat, "dp", scatter_dimension=0, tiled=True)[0], "seq")
    per = width // shards
    rows9 = flat[:, : 9 * per].reshape(layers, 9, per)
    grad_bfc1 = flat[:, 9 * per :]
    stack = lambda i: jnp.stack([b[i] for b in big])
    bias_rest = jnp.concatenate([rows9[:, 2:3], rows9[:, 8:9], rows9[:, 3:6]], 1)
    return (
        hidden.astype(BF16)[None],
        grad_hidden[None],
        rms,
        rows9[:, :2],
        bias_rest,
        rows9[:, 6],
        stack(0),
        stack(1),
        stack(2),
        grad_bfc1,
        stack(3),
    )


MESH = pl.DeviceIdType.MESH
NEG = -1000000000.0


def ddot(a, b, ca, cb):
    return lax.dot_general(a, b, (((ca,), (cb,)), ((), ())), preferred_element_type=F32)


def fused_kernel(cfg, x_ref, mask_ref, valid_ref, gains_ref, biases_ref, bfc_ref, cot_ref, w_qkv, w_out, w_fc1, w_fc2,
                 y_ref, gx_ref, rms_ref, ogain_ref, obias_ref, oquery_ref, obfc_ref, o_qkv, o_out, o_fc1, o_fc2,
                 W, WO, XR, ZR, AF, QKV, OB, MF, U, H, H2, LSE,
                 GF, BF, PB, R0, R1, R2, DU, GW, DQKV, DO, DKV, DH, MK, MR, TV, PS, PR, SGF, SG, SX, SZ, ST, STAT,
                 loc_sem, agz_s, agz_r, agx_s, agx_r, agw_s, agw_r, ge_s, ge_r, re_s, re_r, wo_s, wo_r, gw_s, gw_r,
                 rx_s, rx_r, rz_s, rz_r, fo_s, fo_r, mk_s, mk_r, st_s, st_r):
    L, M, RB, T, TP, D, NC = cfg["L"], cfg["M"], cfg["RB"], cfg["T"], cfg["TP"], cfg["D"], cfg["NC"]
    S = 4
    R = S * TP
    C = D // S
    FS = cfg["FS"]
    SCALE = 1.0 / math.sqrt(HEAD_DIM)
    COLS = (0, 3 * C, 3 * C + C, 3 * C + C + FS, NC)
    QK, OUT, FC1, FC2 = range(4)
    d = lax.axis_index("dp")
    s = lax.axis_index("seq")
    z = d // 2
    xx = d % 2
    ypos = s // 2
    cpos = s % 2
    core = (d, s + 1 - 2 * cpos)
    ydev = (d, s + 2 - 4 * ypos)
    diag = (d, (s + 1 - 2 * cpos) + 2 - 4 * ypos)
    xdev = (d + 1 - 2 * xx, s)
    zof = [lax.rem(z + k, M) for k in range(M)]
    zdev = [(2 * zof[k] + xx, s) for k in range(M)]
    zfrom = [lax.rem(z + M - k, M) for k in range(M)]

    def rcopy(src, dst, ss, rs, dev):
        return pltpu.make_async_remote_copy(src_ref=src, dst_ref=dst, send_sem=ss, recv_sem=rs,
                                            device_id=dev, device_id_type=MESH)

    bar = pltpu.get_barrier_semaphore()
    for dev in [core, ydev, diag, xdev] + zdev[1:]:
        pl.semaphore_signal(bar, inc=1, device_id=dev, device_id_type=MESH)
    pl.semaphore_wait(bar, 3 + M)

    def wslot(l, zz, xp, j):
        return W.at[l, zz, xp, :, COLS[j]:COLS[j + 1]]

    def own_parts(l, j, s):
        a = COLS[j]

        def at_s(start, width):
            return pl.ds(pl.multiple_of(start + width * s, width), width)
        if j == QK:
            return [(w_qkv.at[l, :, at_s(D * i, C)], o_qkv.at[l, :, at_s(D * i, C)], a + C * i, C) for i in range(3)]
        if j == OUT:
            return [(w_out.at[l, :, at_s(0, C)], o_out.at[l, :, at_s(0, C)], a, C)]
        if j == FC1:
            return [(w_fc1.at[l, :, at_s(S * RB * i, RB)], o_fc1.at[l, :, at_s(S * RB * i, RB)], a + RB * i, RB) for i in range(2 * M)]
        return [(w_fc2.at[l, at_s(0, RB), :], o_fc2.at[l, at_s(0, RB), :], a, D)]

    def own_load(l, j):
        for src, _, c0, n in own_parts(l, j, s):
            pltpu.make_async_copy(src, W.at[l, z, xx, :, c0:c0 + n], loc_sem.at[l, j]).start()

    def own_wait(l, j):
        pltpu.make_async_copy(wslot(l, z, xx, j), wslot(l, z, xx, j), loc_sem.at[l, j]).wait()

    pieces = [(0, 0, 0, 0, False)]
    for l in range(L):
        for j in range(4):
            n, turned = cfg["cuts"][j], cfg["turned"][j]
            w = (COLS[j + 1] - COLS[j]) // n
            pieces += [(l, j, COLS[j] + w * i, COLS[j] + w * i + w, i in turned) for i in range(n)]
    NP = len(pieces)
    last_of = {(l, j): max(p for p in range(1, NP) if pieces[p][:2] == (l, j)) for l in range(L) for j in range(4)}
    far = M - 1
    lower = z < M // 2
    edge = jnp.where(lower, z, far - z)
    near_of = []
    for i in range(M - 1):
        t = i + jnp.where(i >= edge, 1, 0)
        near_of.append(jnp.where(lower, t, far - t))
    relay_to = jnp.where(lower, 0, far)
    relays = jnp.logical_and(z > 0, z < far)
    direct = {k: (z < far if k == 1 else z > 0 if k == M - 1 else None) for k in range(1, M)}
    if not cfg["relay"]:
        direct, relays = {k: None for k in range(1, M)}, z < 0

    def when(cond, f):
        if cond is None:
            f()
        else:
            pl.when(cond)(f)

    def ag_slot(p, zz, xp):
        l, j, c0, c1, _ = pieces[p]
        return PS.at[zz, xp] if p == 0 else W.at[l, zz, xp, :, c0:c1]

    def ag_z(p, zz, xp, to, i, ss, rs):
        return rcopy(ag_slot(p, zz, xp), ag_slot(p, zz, xp), ss.at[p, i], rs.at[p, zz], (2 * to + xx, s))

    def ag_x(p, zz, xp):
        return rcopy(ag_slot(p, zz, xp), ag_slot(p, zz, xp), agx_s.at[p, zz], agx_r.at[p, zz], xdev)

    def ag_issue(p):
        l, j, _, _, x_first = pieces[p]
        ag_load(p)
        for k in range(1, M):
            when(direct[k], ag_z(p, z, xx, zof[k], k, agz_s, agz_r).start)
        if not x_first:
            ag_x(p, z, xx).start()
            return
        ag_x(p, z, 1 - xx).wait_recv()
        for k in range(1, M):
            when(direct[k], ag_z(p, z, 1 - xx, zof[k], k, agw_s, agw_r).start)

    def ag_load(p):
        l, j = pieces[p][:2]
        if p > 0 and (l, j) not in loaded:
            own_wait(l, j)
            loaded.add((l, j))

    def ag_turned(l):
        for p in range(NP):
            if pieces[p][4] and pieces[p][0] == l:
                ag_load(p)
                ag_x(p, z, xx).start()

    loaded = set()
    queue = []
    for p in range(NP):
        queue += [(p, i) for i in range(M - 1)]
    state = {"next": 0, "issued": 0}

    def ag_issue_to(n):
        while state["issued"] < min(n, NP):
            ag_issue(state["issued"])
            state["issued"] += 1

    def ag_service(n):
        for _ in range(n):
            if state["next"] == len(queue):
                return
            p, i = queue[state["next"]]
            x_first = pieces[p][4]
            ag_issue_to(p + 1)
            zz = near_of[i]
            got = [(xx, agz_s, agz_r)] + ([(1 - xx, agw_s, agw_r)] if x_first else [])
            for xp, ss, rs in got:
                ag_z(p, zz, xp, zz, 0, ss, rs).wait_recv()
                if not x_first:
                    ag_x(p, zz, xp).start()
                if i == M - 2 and cfg["relay"]:
                    when(relays, ag_z(p, zz, xp, relay_to, 0, ss, rs).start)
            state["next"] += 1
            if i == M - 2:
                ag_issue_to(p + 1 + cfg["ahead"])

    def ag_finish(p):
        while state["next"] < len(queue) and queue[state["next"]][0] <= p:
            ag_service(1)
        for q in range(p + 1):
            if q not in finished:
                finished.add(q)
                if not pieces[q][4]:
                    for zz in range(M):
                        ag_x(q, zz, 1 - xx).wait_recv()

    finished = set()

    def ag_drain(first, last):
        for p in range(first, last):
            x_first = pieces[p][4]
            for ss, rs in [(agz_s, agz_r)] + ([(agw_s, agw_r)] if x_first else []):
                for k in range(1, M):
                    when(direct[k], ag_z(p, z, xx, zof[k], k, ss, rs).wait_send)
                if cfg["relay"]:
                    when(relays, ag_z(p, z, xx, relay_to, 0, ss, rs).wait_send)
            for zz in [z] if x_first else range(M):
                ag_x(p, zz, xx).wait_send()

    for l in range(L):
        for j in range(4):
            own_load(l, j)
    for l in range(L):
        PS[z, xx, 12 * l:12 * l + 2, :] = gains_ref[l].astype(F32)
        PS[z, xx, 12 * l + 2:12 * l + 8, :] = biases_ref[l].astype(F32)
        for i in range(S):
            PS[z, xx, 12 * l + 8 + i:12 * l + 9 + i, :] = bfc_ref[l:l + 1, RB * i:RB * i + RB].astype(F32)
    row = mask_ref[...].astype(F32)
    MK[s] = jnp.zeros_like(MK[s])
    MK[s, 0:1, 0:T] = row
    ag_issue_to(1)
    mks = [rcopy(MK.at[s], MK.at[s], mk_s.at[i], mk_r.at[i], dev) for i, dev in enumerate((core, ydev, diag))]
    for c in mks:
        c.start()
    ag_issue_to(1 + cfg["ahead"])
    ag_turned(0)
    diagonal = lax.broadcasted_iota(jnp.int32, (T, T), 0) == lax.broadcasted_iota(jnp.int32, (T, T), 1)
    TV[...] = jnp.zeros_like(TV)
    TV[0:T, :] = jnp.broadcast_to(
        jnp.sum(jnp.where(diagonal, row, 0.0), axis=1, keepdims=True) * valid_ref[0].astype(F32), (T, 128))
    H[0] = jnp.zeros((TP, D), F32)
    H[0, 0:T, :] = x_ref[...].astype(F32)
    SGF[...] = jnp.zeros_like(SGF)
    SG[...] = jnp.zeros_like(SG)
    STAT[...] = jnp.zeros_like(STAT)
    for i, c in enumerate(mks):
        c.wait_send()
        rcopy(MK.at[s], MK.at[(core, ydev, diag)[i][1]], mk_s.at[i], mk_r.at[i], (core, ydev, diag)[i]).wait_recv()
    MR[...] = jnp.concatenate([MK[i, :, 0:TP] for i in range(S)], axis=1)
    ag_finish(0)
    for i in range(M):
        for j in range(2):
            PR[:, 128 * (2 * i + j):128 * (2 * i + j) + 128] = PS[i, j]

    DH[...] = jnp.zeros_like(DH)
    DH[0:T, :] = cot_ref[...].astype(F32) * TV[0:T, 0:1]

    def prow(l, i):
        return PR[12 * l + i:12 * l + i + 1, :]

    def prow_cols(l, i):
        return PR[12 * l + i:12 * l + i + 1, pl.ds(pl.multiple_of(C * s, C), C)]

    HB = TP // 2

    def ge_part(e, buf, i, h):
        rows = pl.ds(h * HB, HB)
        if i == 0:
            return rcopy(buf.at[s, rows], buf.at[s, rows], ge_s.at[e, 0, h], ge_r.at[e, 0, h], core)
        if i == 1:
            return rcopy(buf.at[s, rows], buf.at[s, rows], ge_s.at[e, 1, h], ge_r.at[e, 1, h], ydev)
        return rcopy(buf.at[ydev[1], rows], buf.at[ydev[1], rows], ge_s.at[e, 2, h], ge_r.at[e, 2, h], core)

    def ge_send(e, buf, h):
        ge_part(e, buf, 1, h).start()
        ge_part(e, buf, 0, h).start()

    def ge_end(e, buf):
        for h in range(2):
            rcopy(buf.at[s, pl.ds(h * HB, HB)], buf.at[ydev[1], pl.ds(h * HB, HB)],
                  ge_s.at[e, 1, h], ge_r.at[e, 1, h], ydev).wait_recv()
            ge_part(e, buf, 2, h).start()
        for h in range(2):
            rcopy(buf.at[s, pl.ds(h * HB, HB)], buf.at[core[1], pl.ds(h * HB, HB)],
                  ge_s.at[e, 0, h], ge_r.at[e, 0, h], core).wait_recv()
        for h in range(2):
            rcopy(buf.at[ydev[1], pl.ds(h * HB, HB)], buf.at[diag[1], pl.ds(h * HB, HB)],
                  ge_s.at[e, 2, h], ge_r.at[e, 2, h], core).wait_recv()
        for i in range(3):
            for h in range(2):
                ge_part(e, buf, i, h).wait_send()

    def re_copy(e, i, h):
        b = e % 2
        rows = pl.ds(h * HB, HB)
        if i == 0:
            return rcopy(PB.at[b, 1 - ypos, 1 - cpos, rows], R0.at[b, rows], re_s.at[e, 0, h], re_r.at[e, 0, h], core)
        if i == 1:
            return rcopy(PB.at[b, 1 - ypos, cpos, rows], R1.at[b, rows], re_s.at[e, 1, h], re_r.at[e, 1, h], ydev)
        return rcopy(PB.at[b, ypos, 1 - cpos, rows], R2.at[b, rows], re_s.at[e, 2, h], re_r.at[e, 2, h], core)

    def re_run(e, partial):
        b = e % 2
        partial(1 - ypos, b)
        for h in range(2):
            re_copy(e, 0, h).start()
        for h in range(2):
            re_copy(e, 0, h).wait_recv()
            for r0 in range(h * HB, h * HB + HB, 16):
                PB[b, 1 - ypos, cpos, r0:r0 + 16, :] = (
                    PB[b, 1 - ypos, cpos, r0:r0 + 16, :].astype(F32) + R0[b, r0:r0 + 16, :].astype(F32)).astype(BF16)
            re_copy(e, 1, h).start()
        partial(ypos, b)
        for h in range(2):
            re_copy(e, 2, h).start()

    def re_half(e, h):
        for i in (2, 1):
            re_copy(e, i, h).wait_recv()

    def re_sent(e):
        for i in range(3):
            for h in range(2):
                re_copy(e, i, h).wait_send()

    def re_rows(e, rows):
        b = e % 2
        return (PB[b, ypos, cpos, rows, :].astype(F32) + R2[b, rows, :].astype(F32)) + R1[b, rows, :].astype(F32)

    def partial_of(lhs, rhs, cb):
        def run(chip, b):
            def tile(j, _):
                cols = pl.ds(pl.multiple_of(j * C, C), C)
                r = ddot(lhs(chip), rhs(j), 1, cb).astype(BF16)
                PB[b, chip, :, :, cols] = r.reshape(2, TP, C)
                return 0
            lax.fori_loop(0, S, tile, 0)
        return run

    def row_loop(body, init, before=None, after=None):
        for h in range(2):
            if before is not None:
                before(h)

            def one(i, carry):
                return body(pl.ds(pl.multiple_of(h * HB + i * 16, 16), 16), carry)
            init = lax.fori_loop(0, HB // 16, one, init, unroll=cfg["unroll"])
            if after is not None:
                after(h)
        return init

    def norm(v):
        center = v - jnp.mean(v, -1, keepdims=True)
        inverse = lax.rsqrt(jnp.mean(center * center, -1, keepdims=True) + epsilon)
        return center * inverse, inverse

    def fold(v):
        return v[0:8] + v[8:16]

    def col_sum(v):
        return jnp.sum(v, axis=0, keepdims=True)

    lane_low = lax.broadcasted_iota(jnp.int32, (1, 2 * HEAD_DIM), 1) < HEAD_DIM
    lane_idx = lax.broadcasted_iota(jnp.int32, (1, 128), 1)

    def attend(l, pair):
        def block(i, _):
            rows = pl.ds(pl.multiple_of(i * TP, 16), TP)
            q = QKV[l, rows, 128 * pair:128 * pair + 128]
            k = QKV[l, :, C + 128 * pair:C + 128 * pair + 128]
            v = QKV[l, :, 2 * C + 128 * pair:2 * C + 128 * pair + 128]
            outs, lses = [], []
            for h in range(2):
                keep = lane_low if h == 0 else jnp.logical_not(lane_low)
                qh = jnp.where(keep, q, jnp.zeros_like(q))
                sc = ddot(qh, k, 1, 1) * SCALE
                sc = jnp.where(MR[0:1, :] > 0, sc, NEG)
                mx = jnp.max(sc, -1, keepdims=True)
                ex = jnp.exp(sc - mx)
                tot = jnp.sum(ex, -1, keepdims=True)
                outs.append(ddot(ex.astype(BF16), v, 1, 0) / tot)
                lses.append(mx + jnp.log(tot))
            OB[l, rows, 128 * pair:128 * pair + 128] = jnp.where(lane_low, outs[0], outs[1]).astype(BF16)
            held = jnp.where(lane_idx == 2 * pair, lses[0], lses[1])
            LSE[l, rows, :] = held if pair == 0 else jnp.where(lane_idx < 2 * pair, LSE[l, rows, :], held)
            return 0
        lax.fori_loop(0, S, block, 0)

    def attend_back(l, pair):
        DKV[...] = jnp.zeros_like(DKV)

        def block(i, _):
            rows = pl.ds(pl.multiple_of(i * TP, 16), TP)
            q = QKV[l, rows, 128 * pair:128 * pair + 128]
            k = QKV[l, :, C + 128 * pair:C + 128 * pair + 128]
            v = QKV[l, :, 2 * C + 128 * pair:2 * C + 128 * pair + 128]
            do = DO[rows, 128 * pair:128 * pair + 128]
            lse = LSE[l, rows, :]
            dqs = []
            dk = dv = None
            for h in range(2):
                keep = lane_low if h == 0 else jnp.logical_not(lane_low)
                qh = jnp.where(keep, q, jnp.zeros_like(q))
                doh = jnp.where(keep, do, jnp.zeros_like(do))
                sc = ddot(qh, k, 1, 1) * SCALE
                sc = jnp.where(MR[0:1, :] > 0, sc, NEG)
                p = jnp.exp(sc - lse[:, 2 * pair + h:2 * pair + h + 1])
                dp = ddot(doh, v, 1, 1)
                inner = jnp.sum(p * dp, -1, keepdims=True)
                ds = (p * (dp - inner)).astype(BF16)
                dqs.append(ddot(ds, k, 1, 0))
                dkh = ddot(ds, qh, 0, 0)
                dvh = ddot(p.astype(BF16), doh, 0, 0)
                dk = dkh if dk is None else dk + dkh
                dv = dvh if dv is None else dv + dvh
            DQKV[rows, 128 * pair:128 * pair + 128] = (jnp.where(lane_low, dqs[0], dqs[1]) * SCALE).astype(BF16)
            DKV[0] += dk
            DKV[1] += dv
            return 0
        lax.fori_loop(0, S, block, 0)
        DQKV[:, C + 128 * pair:C + 128 * pair + 128] = (DKV[0] * SCALE).astype(BF16)
        DQKV[:, 2 * C + 128 * pair:2 * C + 128 * pair + 128] = DKV[1].astype(BF16)

    peers = (core, ydev, diag)

    def wo_copy(l, i):
        to = peers[i][1]
        return rcopy(W.at[l, to, :, :, COLS[OUT]:COLS[FC1]], WO.at[l, :, :, pl.ds(pl.multiple_of(C * s, C), C)],
                     wo_s.at[l, i], wo_r.at[l, i], peers[i])

    def wo_start(l):
        for i in range(3):
            wo_copy(l, i).start()
        WO[l, :, :, pl.ds(pl.multiple_of(C * s, C), C)] = W[l, s, :, :, COLS[OUT]:COLS[FC1]]

    def wo_end(l):
        for i in range(3):
            wo_copy(l, i).wait()

    def gw_copy(l, i):
        to = peers[i][1]
        return rcopy(WO.at[l, :, :, pl.ds(pl.multiple_of(C * to, C), C)], W.at[l, s, :, :, COLS[OUT]:COLS[FC1]],
                     gw_s.at[l, i], gw_r.at[l, i], peers[i])

    def gw_start(l):
        for i in range(3):
            gw_copy(l, i).start()
        W[l, s, :, :, COLS[OUT]:COLS[FC1]] = WO[l, :, :, pl.ds(pl.multiple_of(C * s, C), C)]

    def gw_end(l):
        for i in range(3):
            gw_copy(l, i).wait()

    def wtile(l, j, a, b):
        n = M // S
        if n == 1:
            return W[l, j, :, :, a:b].reshape(2 * RB, b - a)
        return W[l, pl.ds(j * n, n), :, :, a:b].reshape(2 * RB * n, b - a)

    def grad_of(l, j):
        return GF if (l, j) == (L - 1, FC2) else W.at[l]

    def GC(l, j):
        return slice(0, D) if (l, j) == (L - 1, FC2) else slice(COLS[j], COLS[j + 1])

    at_end = edge == 0
    block_of = [jnp.where(at_end, near_of[M - 2 - i], near_of[i]) for i in range(M - 1)] + [z]
    first_to = jnp.where(at_end, near_of[0], block_of[0])
    first_slot = jnp.where(at_end, near_of[0], z)

    def rx_copy(l, j, k):
        a, b = COLS[j], COLS[j + 1]
        zz = block_of[k]
        return rcopy(grad_of(l, j).at[zz, 1 - xx, :, GC(l, j)], XR.at[l, zz, :, a:b], rx_s.at[l, j, k], rx_r.at[l, j, k], xdev)

    def rz_copy(l, j, k):
        a, b = COLS[j], COLS[j + 1]
        to, slot = (first_to, first_slot) if k == 0 else (block_of[k], z)
        return rcopy(XR.at[l, block_of[k], :, a:b], ZR.at[l, slot, :, a:b], rz_s.at[l, j, k], rz_r.at[l, j, slot], (2 * to + xx, s))

    def rz_recv(l, j, slot):
        a, b = COLS[j], COLS[j + 1]
        return rcopy(XR.at[l, z, :, a:b], ZR.at[l, slot, :, a:b], rz_s.at[l, j, 0], rz_r.at[l, j, slot], xdev)

    def whole_of(l, j):
        return XR.at[l, z, :, COLS[j]:COLS[j + 1]]

    def fo_start(l, j):
        for _, dst, c0, n in own_parts(l, j, s):
            src = XR.at[l, z, :, c0:c0 + n]
            for i in range(2):
                rcopy(src, dst, fo_s.at[l, j, i], fo_r.at[l, j, i], peers[i]).start()
            pltpu.make_async_copy(src, dst, loc_sem.at[l, j]).start()

    def fo_pass(l, j):
        rcopy(whole_of(l, j), whole_of(l, j), fo_s.at[l, j, 1], fo_r.at[l, j, 1], peers[1]).wait_recv()
        for _, dst, c0, n in own_parts(l, j, ydev[1]):
            rcopy(dst, dst, fo_s.at[l, j, 2], fo_r.at[l, j, 2], core).start()

    def fo_wait(l, j):
        for i in range(3):
            c = rcopy(whole_of(l, j), whole_of(l, j), fo_s.at[l, j, i], fo_r.at[l, j, i], peers[i])
            c.wait_send()
            if i != 1:
                c.wait_recv()
        pltpu.make_async_copy(whole_of(l, j), whole_of(l, j), loc_sem.at[l, j]).wait()

    def red_first(l, j, k):
        a, b = COLS[j], COLS[j + 1]
        rx_copy(l, j, k).wait_recv()
        zz = block_of[k]
        if k == M - 1:
            return
        for r0 in range(0, RB, 32):
            XR[l, zz, r0:r0 + 32, a:b] = (XR[l, zz, r0:r0 + 32, a:b].astype(F32) + grad_of(l, j)[zz, xx, r0:r0 + 32, GC(l, j)].astype(F32)).astype(BF16)
        if k == M - 2:
            @pl.when(jnp.logical_not(at_end))
            def _():
                rz_recv(l, j, z).wait_recv()
                for r0 in range(0, RB, 32):
                    XR[l, zz, r0:r0 + 32, a:b] = (XR[l, zz, r0:r0 + 32, a:b].astype(F32) + ZR[l, z, r0:r0 + 32, a:b].astype(F32)).astype(BF16)
        rz_copy(l, j, k).start()

    def red_second(l, j):
        a, b = COLS[j], COLS[j + 1]
        red_first(l, j, M - 1)

        def total(n):
            for i in range(n):
                rz_recv(l, j, near_of[i]).wait_recv()
            for r0 in range(0, RB, 32):
                t = XR[l, z, r0:r0 + 32, a:b].astype(F32) + grad_of(l, j)[z, xx, r0:r0 + 32, GC(l, j)].astype(F32)
                for i in range(n):
                    t = t + ZR[l, near_of[i], r0:r0 + 32, a:b].astype(F32)
                XR[l, z, r0:r0 + 32, a:b] = t.astype(BF16)
        pl.when(at_end)(lambda: total(M - 2))
        pl.when(jnp.logical_not(at_end))(lambda: total(M - 1))
        fo_start(l, j)

    def red_end(l, j):
        for k in range(M):
            rx_copy(l, j, k).wait_send()
        for k in range(M - 1):
            rz_copy(l, j, k).wait_send()
        fo_wait(l, j)

    events = []
    later, late = [], []
    done = {"n": 0}

    def red_later():
        if len(later) > 1:
            late.append(later.pop(0))
        if later:
            events.append((red_second,) + later[-1])

    def red_push(l, j):
        for k in range(M):
            rx_copy(l, j, k).start()
        events.extend((red_first, l, j, k) for k in range(M - 1))
        red_later()
        later.append((l, j))

    def red_service(n):
        for _ in range(n):
            if done["n"] >= len(events):
                return
            f, *a = events[done["n"]]
            done["n"] += 1
            f(*a)

    def norm_back(l, src, e, gain, buf=None, g=None):
        def one(rows, acc):
            n, r = norm(src[l, rows, :])
            dm = re_rows(e, rows)
            dn = dm * gain
            pm = jnp.mean(dn, -1, keepdims=True)
            cm = jnp.mean(dn * n, -1, keepdims=True)
            dh = DH[rows, :] + r * (dn - pm - n * cm)
            DH[rows, :] = dh
            sums = acc[0] + fold(dm * n), acc[1] + fold(dm)
            if buf is None:
                return sums
            v = dh.astype(BF16)
            buf[s, rows, :] = v
            return sums + (acc[2] + fold(v.astype(F32)),)
        zero = jnp.zeros((8, D), F32)
        out = row_loop(one, (zero,) * (2 if buf is None else 3), lambda h: re_half(e, h),
                       None if buf is None else lambda h: ge_send(g, buf, h))
        re_sent(e)
        return [col_sum(v) for v in out]

    def low_of(buf, g):
        def one(rows, acc):
            v = DH[rows, :].astype(BF16)
            buf[s, rows, :] = v
            return acc + fold(v.astype(F32))
        return col_sum(row_loop(one, jnp.zeros((8, D), F32), after=lambda h: ge_send(g, buf, h)))

    def forward(l):
        e = 2 * l
        fsv = cfg["fsv"]

        def ln1(rows, _):
            n, _r = norm(H[l, rows, :])
            AF[l, s, rows, :] = (n * prow(l, 0) + prow(l, 2)).astype(BF16)
            return 0
        if l == 0:
            row_loop(ln1, 0, after=lambda h: ge_send(e, AF.at[l], h))
        ag_service(fsv[0])
        ge_end(e, AF.at[l])
        ag_finish(last_of[l, QK])
        for n in range(3):
            r = ddot(AF[l].reshape(R, D), W[l, :, :, :, C * n:C * n + C].reshape(D, C), 1, 0)
            if n == 0:
                r = r + prow_cols(l, 3)
            if n == 2:
                r = r + prow_cols(l, 4)
            QKV[l, :, C * n:C * n + C] = r.astype(BF16)
        ag_finish(last_of[l, OUT])
        wo_start(l)
        if l == 0:
            SGF[12 * (L - 1) + 7:12 * (L - 1) + 8, :] = low_of(BF.at[0], 2 * L)
        attend(l, 0)
        ag_service(fsv[1])
        attend(l, 1)
        if l < L - 1:
            ag_turned(l + 1)
        ag_service(fsv[2])
        if l == 0:
            ge_end(2 * L, BF.at[0])
        wo_end(l)
        re_run(e + 0, partial_of(
            lambda chip: OB[l, pl.ds(pl.multiple_of(chip * 2 * TP, 16), 2 * TP), :],
            lambda j: WO[l, :, :, pl.ds(pl.multiple_of(j * C, C), C)].reshape(C, C), 0))
        ag_service(fsv[3])

        def post(rows, acc):
            hv = H[l, rows, :]
            br = re_rows(e + 0, rows) + prow(l, 5)
            mid = hv + br
            H2[l, rows, :] = mid
            n, _r = norm(mid)
            MF[l, s, rows, :] = (n * prow(l, 1) + prow(l, 6)).astype(BF16)
            t = TV[rows, 0:1]
            return acc[0] + fold(t * hv * hv), acc[1] + fold(t * br * br)
        zero = jnp.zeros((8, D), F32)
        s0, s1 = row_loop(post, (zero, zero), lambda h: re_half(e, h), lambda h: ge_send(e + 1, MF.at[l], h))
        re_sent(e)
        ag_service(fsv[4])
        ge_end(e + 1, MF.at[l])
        ag_finish(last_of[l, FC1])
        bias = PR[pl.ds(12 * l + 8 + s, 1), :]
        for j in range(FS // C):
            u = ddot(MF[l].reshape(R, D), W[l, :, :, :, COLS[FC1] + C * j:COLS[FC1] + C * j + C].reshape(D, C), 1, 0)
            u = u + bias[:, C * j:C * j + C]
            U[l, :, C * j:C * j + C] = u
            GW[:, C * j:C * j + C] = (u / (1.0 + jnp.exp(-1.702 * u))).astype(BF16)
        stat(3 * l, s0)
        stat(3 * l + 1, s1)
        if l == L - 1:
            for j in range(FS // C):
                GF[j, :, :, :] = ddot(GW[:, C * j:C * j + C], BF[0].reshape(R, D), 0, 0).astype(BF16).reshape(2, RB, D)
        ag_finish(last_of[l, FC2])
        if l == L - 1:
            red_push(l, FC2)
        re_run(e + 1, partial_of(
            lambda chip: GW[pl.ds(pl.multiple_of(chip * 2 * TP, 16), 2 * TP), :],
            lambda j: W[l, :, :, :, pl.ds(pl.multiple_of(COLS[FC2] + j * C, C), C)].reshape(FS, C), 0))

    def forward_end(l):
        e = 2 * l

        def last(rows, acc):
            out = re_rows(e + 1, rows) + prow(l, 7)
            res = H2[l, rows, :] + out
            H[l + 1, rows, :] = res
            if l < L - 1:
                n, _r = norm(res)
                AF[l + 1, s, rows, :] = (n * prow(l + 1, 0) + prow(l + 1, 2)).astype(BF16)
            t = TV[rows, 0:1]
            return acc + fold(t * out * out)
        ag_service(cfg["fsv"][5])
        stat(3 * l + 2, row_loop(last, jnp.zeros((8, D), F32), lambda h: re_half(e + 1, h),
                                 None if l == L - 1 else lambda h: ge_send(e + 2, AF.at[l + 1], h)))
        re_sent(e + 1)

    def stat(i, v):
        STAT[...] = jnp.where(lane_idx == i, jnp.sum(col_sum(v), axis=1, keepdims=True), STAT[...])

    def backward(l):
        ge_a = re_a = 2 * L + 2 * (L - 1 - l)
        ge_b = re_b = ge_a + 1
        B0, B1 = BF.at[0], BF.at[1]
        svc = cfg["svc"][L - 1 - l]
        if l < L - 1:
            red_service(svc[0])
            ge_end(ge_a, B0)
        for j in range(FS // C):
            dg = ddot(BF[0].reshape(R, D), wtile(l, j, COLS[FC2], COLS[FC2] + D), 1, 1)
            u = U[l, :, C * j:C * j + C]
            sg = 1.0 / (1.0 + jnp.exp(-1.702 * u))
            if l < L - 1:
                GW[:, C * j:C * j + C] = (u * sg).astype(BF16)
            du = (dg * (sg + 1.702 * u * sg * (1.0 - sg))).astype(BF16)
            DU[:, C * j:C * j + C] = du
            SGF[pl.ds(12 * l + 8 + s, 1), C * j:C * j + C] = jnp.sum(du.astype(F32), axis=0, keepdims=True)
        red_service(svc[1])
        if l < L - 1:
            for j in range(FS // C):
                W[l, j, :, :, COLS[FC2]:COLS[FC2] + D] = ddot(GW[:, C * j:C * j + C], BF[0].reshape(R, D), 0, 0).astype(BF16).reshape(2, RB, D)
            red_push(l, FC2)
        re_run(re_a, partial_of(
            lambda chip: DU[pl.ds(pl.multiple_of(chip * 2 * TP, 16), 2 * TP), :],
            lambda j: wtile(l, j, COLS[FC1], COLS[FC1] + FS), 1))
        for j in range(S):
            W[l, j, :, :, COLS[FC1]:COLS[FC1] + FS] = ddot(MF[l, :, :, C * j:C * j + C].reshape(R, C), DU[...], 0, 0).astype(BF16).reshape(2, RB, FS)
        red_push(l, FC1)
        if l == L - 1:
            forward_end(l)
        red_service(svc[2])
        gg, bb, cc = norm_back(l, H2, re_a, prow(l, 1), B1, ge_b)
        SGF[12 * l + 1:12 * l + 2, :] = gg
        SGF[12 * l + 6:12 * l + 7, :] = bb
        SGF[12 * l + 5:12 * l + 6, :] = cc
        red_service(svc[3])
        ge_end(ge_b, B1)
        DO[...] = ddot(BF[1].reshape(R, D), WO[l].reshape(C, D), 1, 1).astype(BF16)
        for j in range(S):
            WO[l, :, :, C * j:C * j + C] = ddot(OB[l], BF[1, :, :, C * j:C * j + C].reshape(R, C), 0, 0).astype(BF16).reshape(2, RB, C)
        gw_start(l)
        attend_back(l, 0)
        red_service(svc[4])
        attend_back(l, 1)
        gw_end(l)
        red_push(l, OUT)
        red_service(svc[5])
        for i, (row, c0) in enumerate(((3, 0), (4, 2 * C))):
            SGF[12 * l + row:12 * l + row + 1, pl.ds(pl.multiple_of(C * s, C), C)] = jnp.sum(
                DQKV[:, c0:c0 + C].astype(F32), axis=0, keepdims=True)
        re_run(re_b, partial_of(
            lambda chip: DQKV[pl.ds(pl.multiple_of(chip * 2 * TP, 16), 2 * TP), :],
            lambda j: wtile(l, j, 0, 3 * C), 1))
        for j in range(S):
            W[l, j, :, :, 0:3 * C] = ddot(AF[l, :, :, C * j:C * j + C].reshape(R, C), DQKV[...], 0, 0).astype(BF16).reshape(2, RB, 3 * C)
        red_push(l, QK)
        red_service(svc[6])
        if l > 0:
            gg, bb, cc = norm_back(l, H, re_b, prow(l, 0), B0, ge_b + 1)
            SGF[12 * (l - 1) + 7:12 * (l - 1) + 8, :] = cc
        else:
            gg, bb = norm_back(l, H, re_b, prow(l, 0))
        SGF[12 * l + 0:12 * l + 1, :] = gg
        SGF[12 * l + 2:12 * l + 3, :] = bb
        red_service(svc[7])

    for l in range(L):
        forward(l)
        if l < L - 1:
            forward_end(l)
    ag_drain(0, last_of[L - 1, FC1] + 1)
    for l in reversed(range(L)):
        backward(l)
    gx_ref[...] = DH[0:T, :]
    y_ref[...] = H[L, 0:T, :].astype(BF16)
    STAT[...] = jnp.where(lane_idx == 3 * L, col_sum(TV[:, 0:1]), STAT[...])

    for i in range(M):
        for j in range(2):
            SG[i, j, 0:24, :] = SGF[0:24, 128 * (2 * i + j):128 * (2 * i + j) + 128]
            SG[i, j, 24:25, :] = STAT[...]
    sgx = rcopy(SG.at[:, 1 - xx], SX, st_s.at[0], st_r.at[0], xdev)
    sgx.start()

    def sz(k, frm):
        return rcopy(SX.at[zof[k]], SZ.at[zfrom[k] if frm else z], st_s.at[k], st_r.at[k], zdev[k])

    def stc(i, frm):
        slot = peers[i][1] if frm else s
        return rcopy(ST.at[s], ST.at[slot], st_s.at[M + i], st_r.at[M + i], peers[i])

    passed = set()

    def pass_on(keep):
        ready = [tuple(a) for f, *a in events[:done["n"]] if f is red_second]
        for p in ready[:len(ready) - keep]:
            if p not in passed:
                passed.add(p)
                fo_pass(*p)

    pass_on(1)
    red_service(len(events))
    sgx.wait()
    SX[...] = SX[...] + SG[:, xx]
    SZ[z] = SX[z]
    for k in range(1, M):
        sz(k, False).start()
    pass_on(0)
    red_later()
    red_service(len(events))
    for k in range(1, M):
        sz(k, True).wait_recv()
    tot = SZ[0]
    for k in range(1, M):
        tot = tot + SZ[k]
    ST[s] = tot
    for i in range(3):
        stc(i, False).start()
    pass_on(0)
    for i in range(3):
        stc(i, True).wait_recv()
    tot = (ST[0] + ST[1]) + (ST[2] + ST[3])
    for l in range(L):
        ogain_ref[l] = tot[12 * l:12 * l + 2]
        obias_ref[l, 0:1, :] = tot[12 * l + 2:12 * l + 3]
        obias_ref[l, 1:5, :] = tot[12 * l + 4:12 * l + 8]
        oquery_ref[l:l + 1, :] = tot[12 * l + 3:12 * l + 4]
        for i in range(S):
            obfc_ref[l:l + 1, RB * i:RB * i + RB] = tot[12 * l + 8 + i:12 * l + 9 + i]
    sums = tot[12 * L:12 * L + 1]
    root = jnp.sqrt(sums / (jnp.maximum(sums[:, 3 * L:3 * L + 1], 1.0) * D))
    for l in range(L):
        rms_ref[l:l + 1, :] = root[:, 3 * l:3 * l + 3]
    for k in range(1, M):
        sz(k, False).wait_send()
    for i in range(3):
        stc(i, False).wait_send()
    ag_drain(last_of[L - 1, FC1] + 1, NP)
    for l in reversed(range(L)):
        for j in (FC2, FC1, OUT, QK):
            red_end(l, j)


def fused_local(cfg, block_input, key_mask, valid, gains, biases, w_qkv, w_out, w_fc1, b_fc1, w_fc2, cotangent):
    L, M, RB, T, TP, D, NC, FS = (cfg[n] for n in ("L", "M", "RB", "T", "TP", "D", "NC", "FS"))
    S, dp = 4, 2 * M
    C = D // S
    R = S * TP
    vm = pl.BlockSpec(memory_space=pltpu.VMEM)
    hbm = pl.BlockSpec(memory_space=pl.ANY)
    dma = pltpu.SemaphoreType.DMA
    v = pltpu.VMEM
    NP, NE = 1 + sum(cfg["cuts"]) * L, 4 * L
    out = pl.pallas_call(
        partial(fused_kernel, cfg),
        out_shape=(
            jax.ShapeDtypeStruct((T, D), BF16),
            jax.ShapeDtypeStruct((T, D), F32),
            jax.ShapeDtypeStruct((L, 3), F32),
            jax.ShapeDtypeStruct((L, 2, RB), F32),
            jax.ShapeDtypeStruct((L, 5, RB), F32),
            jax.ShapeDtypeStruct((L, RB), F32),
            jax.ShapeDtypeStruct((L, S * RB), F32),
            jax.ShapeDtypeStruct(w_qkv.shape, BF16),
            jax.ShapeDtypeStruct(w_out.shape, BF16),
            jax.ShapeDtypeStruct(w_fc1.shape, BF16),
            jax.ShapeDtypeStruct(w_fc2.shape, BF16),
        ),
        in_specs=[vm, vm, pl.BlockSpec(memory_space=pltpu.SMEM), vm, vm, vm, vm, hbm, hbm, hbm, hbm],
        out_specs=(vm,) * 7 + (hbm,) * 4,
        scratch_shapes=[
            v((L, M, 2, RB, NC), BF16),
            v((L, 2, RB, D), BF16),
            v((L, M, RB, NC), BF16),
            v((L, M, RB, NC), BF16),
            v((L, S, TP, D), BF16),
            v((L, R, 3 * C), BF16),
            v((L, R, C), BF16),
            v((L, S, TP, D), BF16),
            v((L, R, FS), F32),
            v((L + 1, TP, D), F32),
            v((L, TP, D), F32),
            v((L, R, 128), F32),
            v((M, 2, RB, D), BF16),
            v((2, S, TP, D), BF16),
            v((2, 2, 2, TP, D), BF16),
            v((2, TP, D), BF16),
            v((2, TP, D), BF16),
            v((2, TP, D), BF16),
            v((R, FS), BF16),
            v((R, FS), BF16),
            v((R, 3 * C), BF16),
            v((R, C), BF16),
            v((2, R, 128), F32),
            v((TP, D), F32),
            v((S, 8, -(-TP // 128) * 128), F32),
            v((8, R), F32),
            v((TP, 128), F32),
            v((M, 2, 12 * L, RB), F32),
            v((12 * L, D), F32),
            v((12 * L, D), F32),
            v((M, 2, 32, RB), F32),
            v((M, 32, RB), F32),
            v((M, 32, RB), F32),
            v((S, 32, RB), F32),
            v((1, RB), F32),
            dma((L, 4)),
            dma((NP, M)), dma((NP, M)), dma((NP, M)), dma((NP, M)), dma((NP, M)), dma((NP, M)),
            dma((NE, 3, 2)), dma((NE, 3, 2)), dma((NE, 3, 2)), dma((NE, 3, 2)),
            dma((L, 3)), dma((L, 3)), dma((L, 3)), dma((L, 3)),
            dma((L, 4, M)), dma((L, 4, M)), dma((L, 4, M)), dma((L, 4, M)),
            dma((L, 4, 3)), dma((L, 4, 3)), dma((3,)), dma((3,)), dma((M + 3,)), dma((M + 3,)),
        ],
        compiler_params=pltpu.CompilerParams(
            collective_id=0, has_side_effects=True, vmem_limit_bytes=cfg["vmem"]),
        cost_estimate=pl.CostEstimate(flops=24_000_000_000, bytes_accessed=20_000_000, transcendentals=0),
    )(block_input[0], key_mask, valid, gains, biases, b_fc1, cotangent[0], w_qkv, w_out, w_fc1, w_fc2)
    y, gx, rms, o_gain, o_bias, o_query, o_bfc, o_qkv, o_out, o_fc1, o_fc2 = out
    return (y[None], gx[None], rms, o_gain, o_bias, o_query,
            o_qkv.astype(F32), o_out.astype(F32), o_fc1.astype(F32), o_bfc, o_fc2.astype(F32))


def local(*args):
    block_input, w_qkv, w_fc2 = args[0], args[5], args[9]
    L, RB = w_qkv.shape[:2]
    T, D = block_input.shape[1:]
    S, dp = lax.axis_size("seq"), lax.axis_size("dp")
    FS = w_fc2.shape[1] * dp // S
    fits = (S == 4 and dp == 2 * S and RB % 128 == 0 and D // S == 2 * RB and L * 12 + 1 <= 32
            and FS // dp == RB and HEAD_DIM * 2 == 128 and D // S == 4 * HEAD_DIM and block_input.shape[0] == 1)
    if not fits:
        return plain_local(*args)
    cfg = dict(L=L, M=dp // 2, RB=RB, T=T, TP=-(-T // 16) * 16, D=D, NC=D + 2 * FS, FS=FS, ahead=3, unroll=5, cuts=(2, 1, 2, 2), turned=((), (), (), (0,)), relay=True, fsv=(6, 2, 2, 3, 5, 4), vmem=62 * 2**20,
               svc=((0, 0, 3, 2, 2, 0, 3, 1),) + ((4, 0, 2, 2, 1, 2, 3, 0),) * (L - 1))
    return fused_local(cfg, *args)


def solution(mesh):
    return jax.shard_map(
        local,
        mesh=mesh,
        in_specs=(
            P("dp", "seq", None),
            P("dp", "seq"),
            P("dp"),
            P(None, None, "dp"),
            P(None, None, "dp"),
            P(None, "dp", None),
            P(None, "dp", None),
            P(None, "dp", None),
            P(None, "dp"),
            P(None, "dp", None),
            P("dp", "seq", None),
        ),
        out_specs=(
            P("dp", "seq", None),
            P("dp", "seq", None),
            P(),
            P(None, None, "dp"),
            P(None, None, "dp"),
            P(None, "dp"),
            P(None, "dp", None),
            P(None, "dp", None),
            P(None, "dp", None),
            P(None, "dp"),
            P(None, "dp", None),
        ),
        check_vma=False,
    )
```
